32 devices in a mesh: wide: 16 (over z, y, core), narrow: 2 (over x).
Axes of the slice: x: 2, y: 2, z: 4, core: 2. Of those that a mesh axis runs over, the one named last changes fastest.
Arguments:
- tokens_short: bfloat16 [128, 128, 768], P(('wide', 'narrow')), may hold values from -6 to 6
- lengths_short: int32 [128], P(('wide', 'narrow')), may hold values from 20 to 128
- tokens_long: bfloat16 [128, 320, 768], P(('wide', 'narrow')), may hold values from -6 to 6
- lengths_long: int32 [128], P(('wide', 'narrow')), may hold values from 129 to 320
- query_weight: bfloat16 [768, 768], P(('wide', 'narrow')), may hold values from -0.3125 to 0.3125
- key_weight: bfloat16 [768, 768], P(('wide', 'narrow')), may hold values from -0.3125 to 0.3125
- value_weight: bfloat16 [768, 768], P(('wide', 'narrow')), may hold values from -0.21875 to 0.21875
- out_weight: bfloat16 [768, 768], P(('wide', 'narrow')), may hold values from -0.625 to 0.625
- up_weight: bfloat16 [768, 3072], P(('wide', 'narrow')), may hold values from -0.21875 to 0.21875
- down_weight: bfloat16 [3072, 768], P(('wide', 'narrow')), may hold values from -0.109375 to 0.109375
- embed_weight: bfloat16 [768, 128], P(('wide', 'narrow')), may hold values from -0.21875 to 0.21875
- query_bias: bfloat16 [768], P(('wide', 'narrow')), may hold values from -3 to 3
- value_bias: bfloat16 [768], P(('wide', 'narrow')), may hold values from -3 to 3
- out_bias: bfloat16 [768], P(('wide', 'narrow')), may hold values from -3 to 3
- attention_gain: bfloat16 [768], P(('wide', 'narrow')), may hold values from 0.5 to 1.5
- attention_shift: bfloat16 [768], P(('wide', 'narrow')), may hold values from -2 to 2
- up_bias: bfloat16 [3072], P(('wide', 'narrow')), may hold values from -3 to 3
- down_bias: bfloat16 [768], P(('wide', 'narrow')), may hold values from -3 to 3
- final_gain: bfloat16 [768], P(('wide', 'narrow')), may hold values from 0.5 to 1.5
- final_shift: bfloat16 [768], P(('wide', 'narrow')), may hold values from -2 to 2
- cotangent_short: bfloat16 [128, 128, 128], P(('wide', 'narrow')), may hold values from -6 to 6
- cotangent_long: bfloat16 [128, 320, 128], P(('wide', 'narrow')), may hold values from -6 to 6
Outputs:
- embed_short: float32 [128, 128, 128], P(('wide', 'narrow'))
- embed_long: float32 [128, 320, 128], P(('wide', 'narrow'))
- grad_tokens_short: float32 [128, 128, 768], P(('wide', 'narrow'))
- grad_tokens_long: float32 [128, 320, 768], P(('wide', 'narrow'))
- grad_query_weight: float32 [768, 768], P(('wide', 'narrow'))
- grad_key_weight: float32 [768, 768], P(('wide', 'narrow'))
- grad_value_weight: float32 [768, 768], P(('wide', 'narrow'))
- grad_out_weight: float32 [768, 768], P(('wide', 'narrow'))
- grad_up_weight: float32 [768, 3072], P(('wide', 'narrow'))
- grad_down_weight: float32 [3072, 768], P(('wide', 'narrow'))
- grad_embed_weight: float32 [768, 128], P(('wide', 'narrow'))
- grad_query_bias: float32 [768], P(('wide', 'narrow'))
- grad_value_bias: float32 [768], P(('wide', 'narrow'))
- grad_out_bias: float32 [768], P(('wide', 'narrow'))
- grad_attention_gain: float32 [768], P(('wide', 'narrow'))
- grad_attention_shift: float32 [768], P(('wide', 'narrow'))
- grad_up_bias: float32 [3072], P(('wide', 'narrow'))
- grad_down_bias: float32 [768], P(('wide', 'narrow'))
- grad_final_gain: float32 [768], P(('wide', 'narrow'))
- grad_final_shift: float32 [768], P(('wide', 'narrow'))
The draws below stay inside these ranges and needn't reach their ends.
All inputs are finite; a program needn't handle non-finite values.
Results may differ from the reference program's by a relative error of at most 0.015.
The reference program's roundings to bfloat16 on the way count: a program that leaves them out, or rounds other values in their place, can miss the bound.
Values may be sent and summed in bfloat16 or wider, within the bound.
A program may use at most 256 MiB of HBM per device.

```python
import math
import jax
import jax.numpy as jnp
from jax import lax

D = 768
HD = 64
FF = 3072
P_SIZE = 128
LS = 128
LL = 320
SHORT_DEV = 4
LONG_DEV = 4
NS = 128
NL = 128


def set_ends(result, own_key, least, top_value):
    spot = [jax.random.randint(jax.random.fold_in(own_key, axis), (), 0, length) for axis, length in enumerate(result.shape)]
    widest = result.shape.index(max(result.shape))
    next_to = spot[:widest] + [(spot[widest] + 1) % result.shape[widest]] + spot[widest + 1:]
    return result.at[tuple(spot)].set(least).at[tuple(next_to)].set(top_value)


def level_of(rng, dims, shards, low, high):
    def one(position, blocks):
        draws = jax.random.uniform(jax.random.fold_in(jax.random.fold_in(rng, 6), position), (blocks,), jnp.float32, low / len(shards), high / len(shards))
        return jnp.repeat(jnp.exp(draws), dims[position] // blocks).reshape((-1,) + (1,) * (len(dims) - position - 1))

    loudness = one(*shards[0])
    for cut in shards[1:]:
        loudness = loudness * one(*cut)
    return loudness


def gaussian(rng, shape, deviation, most, cuts=(), held_as=jnp.bfloat16):
    gain = level_of(rng, shape, cuts, -0.22, 0.18) if cuts else 1.0
    entries = jax.random.normal(rng, shape, jnp.float32) * deviation * gain
    return jnp.minimum(jnp.maximum(entries, -most), most).astype(held_as)


def setup_inputs(seed: int = 0) -> dict:
    streams_of = jax.random.split(jax.random.key(seed), 23)
    return {
        "tokens_short": gaussian(streams_of[0], (NS, LS, D), 1.0, 6.0, ((0, 32),)),
        "lengths_short": set_ends(jax.random.randint(streams_of[1], (NS,), min(20, LS // 2), LS + 1), jax.random.fold_in(streams_of[1], 1), min(20, LS // 2), LS).astype(jnp.int32),
        "tokens_long": gaussian(streams_of[2], (NL, LL, D), 1.0, 6.0, ((0, 32),)),
        "lengths_long": set_ends(jax.random.randint(streams_of[3], (NL,), LS + 1, LL + 1), jax.random.fold_in(streams_of[3], 1), LS + 1, LL).astype(jnp.int32),
        "query_weight": gaussian(streams_of[4], (D, D), (D // 2) ** -0.5, 0.3125, ((0, 32),)),
        "key_weight": gaussian(streams_of[5], (D, D), (D // 2) ** -0.5, 0.3125, ((0, 32),)),
        "value_weight": gaussian(streams_of[6], (D, D), D ** -0.5, 0.21875, ((0, 32),)),
        "out_weight": gaussian(streams_of[7], (D, D), (D // 8) ** -0.5, 0.625, ((0, 32),)),
        "up_weight": gaussian(streams_of[8], (D, FF), D ** -0.5, 0.21875, ((0, 32),)),
        "down_weight": gaussian(streams_of[9], (FF, D), FF ** -0.5, 0.109375, ((0, 32),)),
        "embed_weight": gaussian(streams_of[10], (D, P_SIZE), D ** -0.5, 0.21875, ((0, 32),)),
        "query_bias": gaussian(streams_of[11], (D,), 0.5, 3.0, ((0, 32),)),
        "value_bias": gaussian(streams_of[12], (D,), 0.5, 3.0, ((0, 32),)),
        "out_bias": gaussian(streams_of[13], (D,), 0.5, 3.0, ((0, 32),)),
        "attention_gain": jnp.clip(1.0 + 0.1 * jax.random.normal(streams_of[14], (D,), jnp.float32), 0.5, 1.5).astype(jnp.bfloat16),
        "attention_shift": gaussian(streams_of[15], (D,), 0.3, 2.0, ((0, 32),)),
        "up_bias": gaussian(streams_of[16], (FF,), 0.5, 3.0, ((0, 32),)),
        "down_bias": gaussian(streams_of[17], (D,), 0.5, 3.0, ((0, 32),)),
        "final_gain": jnp.clip(1.0 + 0.1 * jax.random.normal(streams_of[18], (D,), jnp.float32), 0.5, 1.5).astype(jnp.bfloat16),
        "final_shift": gaussian(streams_of[19], (D,), 0.3, 2.0, ((0, 32),)),
        "cotangent_short": gaussian(streams_of[20], (NS, LS, P_SIZE), 1.0, 6.0, ((0, 32),)),
        "cotangent_long": gaussian(streams_of[21], (NL, LL, P_SIZE), 1.0, 6.0, ((0, 32),)),
    }


@jax.custom_vjp
def low(v):
    return lax.optimization_barrier(v.astype(jnp.bfloat16)).astype(jnp.float32)

@jax.custom_vjp
def low_back(v):
    return v

def low_keep(v):
    return (low(v), None)

def low_pass(kept, grad):
    return (grad,)

def back_keep(v):
    return (v, None)

def back_low(kept, grad):
    return (low(grad),)
low.defvjp(low_keep, low_pass)
low_back.defvjp(back_keep, back_low)
highest = lax.Precision.HIGHEST
norm_epsilon = 1e-12
unit_epsilon = 1e-06
masked_fill = -1000000000.0

def layer_norm(residual, norm_gain, norm_shift):
    center = residual - lax.optimization_barrier(jnp.mean(residual, axis=-1, keepdims=True))
    variance = lax.optimization_barrier(jnp.mean(center * center, axis=-1, keepdims=True))
    return center * lax.rsqrt(variance + norm_epsilon) * norm_gain + norm_shift

def gelu_exact(pre_act):
    return 0.5 * pre_act * (1.0 + lax.erf(pre_act * (1.0 / math.sqrt(2.0))))

def normalize(embedding, token_mask):
    squares = lax.optimization_barrier(jnp.sum(embedding * embedding, axis=-1, keepdims=True))
    return math.sqrt(P_SIZE) * embedding * lax.rsqrt(squares + unit_epsilon) * token_mask[..., None]

def soft_weights(scaled, key_mask):
    masked = jnp.where(key_mask, scaled, masked_fill)
    row_peak = lax.optimization_barrier(jnp.max(masked, axis=-1, keepdims=True))
    exponent = jnp.exp(masked - row_peak)
    return exponent / lax.optimization_barrier(jnp.sum(exponent, axis=-1, keepdims=True))

def layer_block(params, inputs):
    tokens, token_mask = inputs
    query_weight, key_weight, value_weight, out_weight, up_weight, down_weight, embed_weight, query_bias, value_bias, out_bias, attention_gain, attention_shift, up_bias, down_bias, final_gain, final_shift = params
    seq_count, length, model_width = tokens.shape
    head_count = model_width // HD
    score_scale = 1.0 / math.sqrt(HD)

    def project(left_side, weight):
        return jnp.einsum('bld,de->ble', left_side, weight, precision=highest)
    query = low_back(low(project(tokens, query_weight) + query_bias)).reshape(seq_count, length, head_count, HD)
    key_proj = low_back(low(project(tokens, key_weight))).reshape(seq_count, length, head_count, HD)
    value = low_back(low(project(tokens, value_weight) + value_bias)).reshape(seq_count, length, head_count, HD)
    scores = low_back(jnp.einsum('bqhe,bkhe->bhqk', query, key_proj, precision=highest) * score_scale)
    key_mask = token_mask[:, None, None, :] > 0.5
    attn_probs = soft_weights(scores, key_mask)
    context = jnp.einsum('bhqk,bkhe->bqhe', low(attn_probs), value, precision=highest)
    context = low_back(low(context.reshape(seq_count, length, model_width)))
    attn_out = low_back(project(context, out_weight) + out_bias)
    normed_one = layer_norm(tokens + attn_out, attention_gain, attention_shift)
    pre_act = low_back(jnp.einsum('bld,df->blf', low(normed_one), up_weight, precision=highest) + up_bias)
    act_low = low(gelu_exact(pre_act))
    ffn_out = low_back(jnp.einsum('blf,fd->bld', act_low, down_weight, precision=highest) + down_bias)
    normed_two = layer_norm(normed_one + ffn_out, final_gain, final_shift)
    embedding = low_back(jnp.einsum('bld,dp->blp', low(normed_two), embed_weight, precision=highest))
    return normalize(embedding, token_mask)

def bucket(params, tokens, lengths, length, group_size):
    seq_total = tokens.shape[0]
    positions = jnp.arange(length, dtype=jnp.int32)
    token_mask = (positions[None, :] < lengths[:, None].astype(jnp.int32)).astype(jnp.float32)
    grouped = tokens.reshape(seq_total // group_size, group_size, length, D)
    grouped_mask = token_mask.reshape(seq_total // group_size, group_size, length)
    checked = jax.checkpoint(layer_block)

    def scan_step(scan_carry, inputs):
        return (scan_carry, checked(params, inputs))
    _, outputs = lax.scan(scan_step, jnp.zeros((), jnp.float32), (grouped, grouped_mask))
    return outputs.reshape(seq_total, length, P_SIZE)

def reference(tokens_short, lengths_short, tokens_long, lengths_long, query_weight, key_weight, value_weight, out_weight, up_weight, down_weight, embed_weight, query_bias, value_bias, out_bias, attention_gain, attention_shift, up_bias, down_bias, final_gain, final_shift, cotangent_short, cotangent_long):
    params = tuple((weight.astype(jnp.float32) for weight in (query_weight, key_weight, value_weight, out_weight, up_weight, down_weight, embed_weight, query_bias, value_bias, out_bias, attention_gain, attention_shift, up_bias, down_bias, final_gain, final_shift)))

    def forward(short_in, long_in, weights):
        return (bucket(weights, short_in, lengths_short, LS, SHORT_DEV * 8), bucket(weights, long_in, lengths_long, LL, LONG_DEV * 2))
    (embed_short, embed_long), pull_back = jax.vjp(forward, tokens_short.astype(jnp.float32), tokens_long.astype(jnp.float32), params)
    grad_short, grad_long, param_grads = pull_back((cotangent_short.astype(jnp.float32), cotangent_long.astype(jnp.float32)))
    return (embed_short, embed_long, grad_short, grad_long, param_grads[0], param_grads[1], param_grads[2], param_grads[3], param_grads[4], param_grads[5], param_grads[6], param_grads[7], param_grads[8], param_grads[9], param_grads[10], param_grads[11], param_grads[12], param_grads[13], param_grads[14], param_grads[15])
```

```python
import functools
import math

import jax
import jax.numpy as jnp
from jax import lax
from jax.experimental import pallas as pl
from jax.experimental.pallas import tpu as pltpu
from jax.sharding import PartitionSpec as P

MESH = pl.DeviceIdType.MESH

HD = 64
P_SIZE = 128


norm_epsilon = 1e-12
unit_epsilon = 1e-06
masked_fill = -1000000000.0


def layer_norm(residual, norm_gain, norm_shift):
    center = residual - jnp.mean(residual, axis=-1, keepdims=True)
    variance = jnp.mean(center * center, axis=-1, keepdims=True)
    return center * lax.rsqrt(variance + norm_epsilon) * norm_gain + norm_shift


def gelu_exact(pre_act):
    return 0.5 * pre_act * (1.0 + lax.erf(pre_act * (1.0 / math.sqrt(2.0))))


def normalize(embedding, token_mask):
    squares = jnp.sum(embedding * embedding, axis=-1, keepdims=True)
    return math.sqrt(P_SIZE) * embedding * lax.rsqrt(squares + unit_epsilon) * token_mask[..., None]


def soft_weights(scaled, key_mask):
    masked = jnp.where(key_mask, scaled, masked_fill)
    row_peak = jnp.max(masked, axis=-1, keepdims=True)
    exponent = jnp.exp(masked - row_peak)
    return exponent / jnp.sum(exponent, axis=-1, keepdims=True)


def matmul(left_side, right_side, form):
    return jnp.einsum(form, left_side, right_side, preferred_element_type=jnp.float32)


def forward(tokens, lengths, full_weights):
    (
        query_weight,
        key_weight,
        value_weight,
        out_weight,
        up_weight,
        down_weight,
        embed_weight,
        query_bias,
        value_bias,
        out_bias,
        attention_gain,
        attention_shift,
        up_bias,
        down_bias,
        final_gain,
        final_shift,
    ) = full_weights
    seq_count, length, model_width = tokens.shape
    head_count = model_width // HD
    score_scale = 1.0 / math.sqrt(HD)
    positions = jnp.arange(length, dtype=jnp.int32)
    token_mask = (positions[None, :] < lengths[:, None]).astype(jnp.float32)
    key_mask = token_mask[:, None, None, :] > 0.5
    query_low = (matmul(tokens, query_weight, "bld,de->ble") + query_bias).astype(jnp.bfloat16)
    query_low = query_low.reshape(seq_count, length, head_count, HD)
    key_low = matmul(tokens, key_weight, "bld,de->ble").astype(jnp.bfloat16)
    key_low = key_low.reshape(seq_count, length, head_count, HD)
    value_low = (matmul(tokens, value_weight, "bld,de->ble") + value_bias).astype(jnp.bfloat16)
    value_low = value_low.reshape(seq_count, length, head_count, HD)
    raw_scores = matmul(query_low, key_low, "bqhe,bkhe->bhqk") * score_scale
    attn_probs = soft_weights(raw_scores, key_mask)
    probs_low = attn_probs.astype(jnp.bfloat16)
    context_low = matmul(probs_low, value_low, "bhqk,bkhe->bqhe")
    context_low = context_low.reshape(seq_count, length, model_width).astype(jnp.bfloat16)
    attn_out = matmul(context_low, out_weight, "bld,de->ble") + out_bias
    resid_one = tokens.astype(jnp.float32) + attn_out
    normed_one = layer_norm(resid_one, attention_gain, attention_shift)
    hidden_low = normed_one.astype(jnp.bfloat16)
    pre_act = matmul(hidden_low, up_weight, "bld,df->blf") + up_bias
    act_low = gelu_exact(pre_act).astype(jnp.bfloat16)
    ffn_out = matmul(act_low, down_weight, "blf,fd->bld") + down_bias
    resid_two = normed_one + ffn_out
    final_low = layer_norm(resid_two, final_gain, final_shift).astype(jnp.bfloat16)
    embedding = matmul(final_low, embed_weight, "bld,dp->blp")
    result = normalize(embedding, token_mask)
    saved = (
        tokens,
        token_mask,
        query_low,
        key_low,
        value_low,
        attn_probs,
        probs_low,
        context_low,
        resid_one,
        hidden_low,
        pre_act,
        act_low,
        resid_two,
        final_low,
        embedding,
    )
    return (result, saved)


def backward(saved, full_weights, cotangent):
    (
        tokens,
        token_mask,
        query_low,
        key_low,
        value_low,
        attn_probs,
        probs_low,
        context_low,
        resid_one,
        hidden_low,
        pre_act,
        act_low,
        resid_two,
        final_low,
        embedding,
    ) = saved
    (
        query_weight,
        key_weight,
        value_weight,
        out_weight,
        up_weight,
        down_weight,
        embed_weight,
        query_bias,
        value_bias,
        out_bias,
        attention_gain,
        attention_shift,
        up_bias,
        down_bias,
        final_gain,
        final_shift,
    ) = full_weights
    seq_count, length, model_width = tokens.shape
    score_scale = 1.0 / math.sqrt(HD)
    _, pull_norm = jax.vjp(lambda vector: normalize(vector, token_mask), embedding)
    (embed_grad,) = pull_norm(cotangent.astype(jnp.float32))
    embed_low = embed_grad.astype(jnp.bfloat16)
    grad_embed = matmul(final_low, embed_low, "bld,blp->dp")
    final_grad = matmul(embed_low, embed_weight, "blp,dp->bld")
    _, pull_two = jax.vjp(
        layer_norm, resid_two, final_gain.astype(jnp.float32), final_shift.astype(jnp.float32)
    )
    resid_two_grad, grad_final_gain, grad_final_shift = pull_two(final_grad)
    ffn_low = resid_two_grad.astype(jnp.bfloat16)
    grad_down_bias = jnp.sum(ffn_low, axis=(0, 1), dtype=jnp.float32)
    grad_down = matmul(act_low, ffn_low, "blf,bld->fd")
    act_grad = matmul(ffn_low, down_weight, "bld,fd->blf")
    _, pull_gelu = jax.vjp(gelu_exact, pre_act)
    (pre_grad,) = pull_gelu(act_grad)
    pre_low = pre_grad.astype(jnp.bfloat16)
    grad_up_bias = jnp.sum(pre_low, axis=(0, 1), dtype=jnp.float32)
    grad_up = matmul(hidden_low, pre_low, "bld,blf->df")
    normed_grad = resid_two_grad + matmul(pre_low, up_weight, "blf,df->bld")
    _, pull_one = jax.vjp(
        layer_norm,
        resid_one,
        attention_gain.astype(jnp.float32),
        attention_shift.astype(jnp.float32),
    )
    resid_one_grad, grad_attention_gain, grad_attention_shift = pull_one(normed_grad)
    attn_low = resid_one_grad.astype(jnp.bfloat16)
    grad_out_bias = jnp.sum(attn_low, axis=(0, 1), dtype=jnp.float32)
    grad_out = matmul(context_low, attn_low, "bld,ble->de")
    context_grad = matmul(attn_low, out_weight, "ble,de->bld").astype(jnp.bfloat16)
    context_grad = context_grad.reshape(seq_count, length, -1, HD)
    value_grad = matmul(probs_low, context_grad, "bhqk,bqhe->bkhe")
    probs_grad = matmul(context_grad, value_low, "bqhe,bkhe->bhqk")
    score_low = attn_probs * (probs_grad - jnp.sum(probs_grad * attn_probs, axis=-1, keepdims=True))
    score_low = score_low.astype(jnp.bfloat16)
    query_grad = (matmul(score_low, key_low, "bhqk,bkhe->bqhe") * score_scale).astype(jnp.bfloat16)
    query_grad = query_grad.reshape(seq_count, length, model_width)
    key_grad = (matmul(score_low, query_low, "bhqk,bqhe->bkhe") * score_scale).astype(jnp.bfloat16)
    key_grad = key_grad.reshape(seq_count, length, model_width)
    value_grad_low = value_grad.astype(jnp.bfloat16).reshape(seq_count, length, model_width)
    grad_query_bias = jnp.sum(query_grad, axis=(0, 1), dtype=jnp.float32)
    grad_value_bias = jnp.sum(value_grad_low, axis=(0, 1), dtype=jnp.float32)
    grad_query = matmul(tokens, query_grad, "bld,ble->de")
    grad_key = matmul(tokens, key_grad, "bld,ble->de")
    grad_value = matmul(tokens, value_grad_low, "bld,ble->de")
    input_grad = (
        resid_one_grad
        + matmul(query_grad, query_weight, "ble,de->bld")
        + matmul(key_grad, key_weight, "ble,de->bld")
        + matmul(value_grad_low, value_weight, "ble,de->bld")
    )
    gradients = (
        grad_query,
        grad_key,
        grad_value,
        grad_out,
        grad_up,
        grad_down,
        grad_embed,
        grad_query_bias,
        grad_value_bias,
        grad_out_bias,
        grad_attention_gain,
        grad_attention_shift,
        grad_up_bias,
        grad_down_bias,
        grad_final_gain,
        grad_final_shift,
    )
    return (input_grad, gradients)


BOTH = ("wide", "narrow")
WIRE = (1280, 384, 1664, 1536)
CUT = (640, 128, 896, 768)
COPIES = 39


def place():
    wide = lax.axis_index("wide")
    return wide // 4, (wide // 2) % 2, wide % 2, lax.axis_index("narrow")


def greet(z, y, c, x):
    partners = [device((z + d) % 4, y, c, x) for d in (1, 2, 3)]
    partners += [device(z, 1 - y, c, x), device(z, y, 1 - c, x), device(z, y, c, 1 - x)]
    barrier = pltpu.get_barrier_semaphore()
    for partner in partners:
        pl.semaphore_signal(barrier, inc=1, device_id=partner, device_id_type=MESH)
    pl.semaphore_wait(barrier, len(partners))


def device(z, y, c, x):
    return (z * 4 + y * 2 + c, x)


class Lazy:
    def __init__(self, make):
        self.make = make

    def __getitem__(self, way):
        return self.make(way)


class Gather:
    def __init__(self, held, cut, send, recv, first):
        self.held, self.cut, self.send, self.recv, self.first = held, cut, send, recv, first
        self.z, self.y, self.c, self.x = place()

    def view(self, block, half):
        if half is None:
            return self.held.at[block]
        lanes = self.held.shape[-1]
        low, size = ((0, self.cut), (self.cut, lanes - self.cut))[half]
        return self.held.at[(*block, slice(None), pl.ds(low, size))]

    def plan(self, slot, out, into, half, target):
        def copy(block):
            return pltpu.make_async_remote_copy(
                src_ref=self.view(block, half),
                dst_ref=self.view(block, half),
                send_sem=self.send.at[self.first + slot],
                recv_sem=self.recv.at[self.first + slot],
                device_id=target,
                device_id_type=MESH,
            )

        return Lazy(lambda way: copy((out, into)[way]))

    def along_z(self, d):
        z, y, c, x = self.z, self.y, self.c, self.x
        return self.plan(d - 1, (z, y, c, x), ((z + 4 - d) % 4, y, c, x), None, device((z + d) % 4, y, c, x))

    def to_x(self, d):
        z, y, c, x = (self.z + 4 - d) % 4, self.y, self.c, self.x
        return self.plan(3 + d, (z, y, c, x), (z, y, c, 1 - x), None, device(self.z, y, c, 1 - x))

    def to_y(self, d):
        z, y, c, x = (self.z + 4 - d) % 4, self.y, self.c, self.x
        return self.plan(7 + d, (z, y, c, x), (z, 1 - y, c, x), None, device(self.z, 1 - y, c, x))

    def corner(self, d, half):
        z, y, c, x = (self.z + 4 - d) % 4, self.y, self.c, self.x
        if half == 0:
            return self.plan(11 + d, (z, y, c, 1 - x), (z, 1 - y, c, 1 - x), 0, device(self.z, 1 - y, c, x))
        return self.plan(15 + d, (z, 1 - y, c, x), (z, 1 - y, c, 1 - x), 1, device(self.z, y, c, 1 - x))

    def to_core(self, d, kind):
        z, c = (self.z + 4 - d) % 4, self.c
        y = 1 - self.y if kind >= 2 else self.y
        x = 1 - self.x if kind in (1, 3, 4) else self.x
        half = kind - 3 if kind >= 3 else None
        return self.plan(19 + 4 * kind + d, (z, y, c, x), (z, y, 1 - c, x), half, device(self.z, self.y, 1 - c, self.x))

    def start_z(self):
        for d in (1, 2, 3):
            self.along_z(d)[0].start()

    def spread(self, d):
        self.to_x(d)[0].start()
        self.to_y(d)[0].start()
        self.to_core(d, 0)[0].start()

    def column(self):
        for d in (1, 2, 3):
            self.along_z(d)[1].wait_recv()
            self.spread(d)

    def turn(self):
        for d in range(4):
            self.to_x(d)[1].wait_recv()
            self.corner(d, 0)[0].start()
            self.to_core(d, 1)[0].start()
            self.to_y(d)[1].wait_recv()
            self.corner(d, 1)[0].start()
            self.to_core(d, 2)[0].start()

    def finish(self):
        for d in range(4):
            for half in (0, 1):
                self.corner(d, half)[1].wait_recv()
                self.to_core(d, 3 + half)[0].start()

    def arrive(self):
        for d in range(4):
            for kind in range(5):
                self.to_core(d, kind)[1].wait_recv()

    def drain(self):
        for d in range(4):
            if d:
                self.along_z(d)[0].wait_send()
            self.to_x(d)[0].wait_send()
            self.to_y(d)[0].wait_send()
            for half in (0, 1):
                self.corner(d, half)[0].wait_send()
            for kind in range(5):
                self.to_core(d, kind)[0].wait_send()


def run_gathers(gathers):
    for one in gathers:
        one.start_z()
    for step in range(len(gathers) + 2):
        if step < len(gathers):
            gathers[step].spread(0)
            gathers[step].column()
        if 0 <= step - 1 < len(gathers):
            gathers[step - 1].turn()
        if 0 <= step - 2 < len(gathers):
            gathers[step - 2].finish()


def stack_halves(whole):
    half = whole.shape[1] // 2
    return jnp.concatenate([whole[:, :half], whole[:, half:]], axis=0).astype(jnp.bfloat16)


def unpack_rows(held, targets):
    def pair(p, carry):
        z, y, c = p // 4, (p // 2) % 2, p % 2
        one, two = held[z, y, c, 0].astype(jnp.float32), held[z, y, c, 1].astype(jnp.float32)
        for side, low, ref, column, lanes in targets:
            rows = slice(24 * side, 24 * side + 24)
            both = jnp.concatenate([one[rows, low : low + lanes], two[rows, low : low + lanes]], axis=0)
            ref[pl.ds(pl.multiple_of(p * 48, 48), 48), column : column + lanes] = both.astype(jnp.bfloat16)
        return carry

    lax.fori_loop(0, 16, pair, 0)


def gather_kernel(q_ref, k_ref, v_ref, o_ref, u_ref, e_ref, d_ref, vec_ref, qkv_out, out_out, up_out, embed_out, down_out, vec_out, h0, h1, h2, h3, send, recv):
    z, y, c, x = place()
    wide = lambda ref: ref[...].astype(jnp.float32)
    h0[z, y, c, x, :, :1152] = stack_halves(jnp.concatenate([wide(q_ref), wide(k_ref), wide(v_ref)], axis=1))
    h0[z, y, c, x, :, 1152:] = vec_ref[...]
    h1[z, y, c, x] = stack_halves(wide(o_ref))
    h2[z, y, c, x] = stack_halves(jnp.concatenate([wide(u_ref), wide(e_ref), wide(e_ref)], axis=1))
    h3[z, y, c, x, :, :768] = d_ref[:48]
    h3[z, y, c, x, :, 768:] = d_ref[48:]
    greet(z, y, c, x)
    gathers = [Gather(h, CUT[i], send, recv, COPIES * i) for i, h in enumerate((h0, h1, h2, h3))]
    run_gathers(gathers)
    gathers[0].arrive()
    unpack_rows(h0, [(0, 0, qkv_out, 0, 1152), (1, 0, qkv_out, 1152, 1152)])

    def vectors(p, carry):
        vec_out[p] = h0[p // 8, (p // 4) % 2, (p // 2) % 2, p % 2, :16, 1152:]
        return carry

    lax.fori_loop(0, 32, vectors, 0)
    gathers[1].arrive()
    unpack_rows(h1, [(0, 0, out_out, 0, 384), (1, 0, out_out, 384, 384)])
    gathers[2].arrive()
    unpack_rows(h2, [(0, 0, up_out, 0, 1664), (1, 0, up_out, 1664, 1408), (1, 1408, embed_out, 0, 128)])
    gathers[3].arrive()

    def down(p, carry):
        block = h3[p // 8, (p // 4) % 2, (p // 2) % 2, p % 2]
        down_out[pl.ds(pl.multiple_of(p * 96, 96), 48)] = block[:, :768]
        down_out[pl.ds(pl.multiple_of(p * 96 + 48, 48), 48)] = block[:, 768:]
        return carry

    lax.fori_loop(0, 32, down, 0)
    for one in gathers:
        one.drain()


def gather_all(query, key, value, out, up, embed, down, vectors):
    vmem = pl.BlockSpec(memory_space=pltpu.VMEM)
    shape = lambda *dims: jax.ShapeDtypeStruct(dims, jnp.bfloat16)
    return pl.pallas_call(
        gather_kernel,
        out_shape=(shape(768, 2304), shape(768, 768), shape(768, 3072), shape(768, 128), shape(3072, 768), shape(32, 16, 128)),
        in_specs=[vmem] * 8,
        out_specs=(vmem,) * 6,
        scratch_shapes=[pltpu.VMEM((4, 2, 2, 2, 48, lanes), jnp.bfloat16) for lanes in WIRE]
        + [pltpu.SemaphoreType.DMA((COPIES * 4,)), pltpu.SemaphoreType.DMA((COPIES * 4,))],
        compiler_params=pltpu.CompilerParams(collective_id=0, has_side_effects=True, vmem_limit_bytes=60 * 2**20),
    )(query, key, value, out, up, embed, down, vectors)


class Scatter:
    def __init__(self, mine, cut, work, send, recv, first):
        self.mine, self.cut, self.send, self.recv, self.first = mine, cut, send, recv, first
        self.core_in, self.total, self.corner_y, self.corner_x, self.from_x, self.from_y, self.from_z = work
        self.z, self.y, self.c, self.x = place()

    def copy(self, slot, source, target, partner):
        return pltpu.make_async_remote_copy(
            src_ref=source,
            dst_ref=target,
            send_sem=self.send.at[self.first + slot],
            recv_sem=self.recv.at[self.first + slot],
            device_id=partner,
            device_id_type=MESH,
        )

    def spot(self, kind):
        return (1 - self.y if kind in (0, 2) else self.y), (1 - self.x if kind in (0, 1) else self.x)

    def core(self, kind):
        y, x = self.spot(kind)
        return self.copy(
            kind,
            self.mine.at[:, y, 1 - self.c, x],
            self.core_in.at[:, y, x],
            device(self.z, self.y, 1 - self.c, self.x),
        )

    def turn(self, d, half):
        z = (self.z + d) % 4
        y, x = self.spot(0)
        low, size = ((0, self.cut), (self.cut, self.mine.shape[-1] - self.cut))[half]
        source = self.total.at[z, y, x, :, pl.ds(low, size)]
        if half == 0:
            return self.copy(4 + d, source, self.corner_y.at[z], device(self.z, 1 - self.y, self.c, self.x))
        return self.copy(8 + d, source, self.corner_x.at[z], device(self.z, self.y, self.c, 1 - self.x))

    def to_x(self, d):
        z = (self.z + d) % 4
        return self.copy(12 + d, self.total.at[z, self.y, 1 - self.x], self.from_x.at[z], device(self.z, self.y, self.c, 1 - self.x))

    def to_y(self, d):
        z = (self.z + d) % 4
        return self.copy(16 + d, self.total.at[z, 1 - self.y, self.x], self.from_y.at[z], device(self.z, 1 - self.y, self.c, self.x))

    def along_z(self, d):
        z = (self.z + d) % 4
        return self.copy(19 + d, self.total.at[z, self.y, self.x], self.from_z.at[d - 1], device(z, self.y, self.c, self.x))

    def start(self):
        for kind in range(4):
            self.core(kind).start()

    def merge(self):
        for kind in range(4):
            self.core(kind).wait_recv()
            y, x = self.spot(kind)

            def add(z, carry):
                here = self.mine[z, y, self.c, x].astype(jnp.float32)
                self.total[z, y, x] = (here + self.core_in[z, y, x].astype(jnp.float32)).astype(jnp.bfloat16)
                return carry

            lax.fori_loop(0, 4, add, 0)
            if kind == 0:
                for d in (1, 2, 3, 0):
                    self.turn(d, 0).start()
                    self.turn(d, 1).start()

    def bend(self):
        for d in (1, 2, 3, 0):
            z = (self.z + d) % 4
            self.turn(d, 0).wait_recv()
            here = self.total[z, self.y, 1 - self.x, :, : self.cut].astype(jnp.float32)
            self.total[z, self.y, 1 - self.x, :, : self.cut] = (here + self.corner_y[z].astype(jnp.float32)).astype(jnp.bfloat16)
            self.to_x(d).start()
            self.turn(d, 1).wait_recv()
            here = self.total[z, 1 - self.y, self.x, :, self.cut :].astype(jnp.float32)
            self.total[z, 1 - self.y, self.x, :, self.cut :] = (here + self.corner_x[z].astype(jnp.float32)).astype(jnp.bfloat16)
            self.to_y(d).start()

    def close(self):
        for d in (1, 2, 3, 0):
            z = (self.z + d) % 4
            self.to_x(d).wait_recv()
            self.to_y(d).wait_recv()
            here = self.total[z, self.y, self.x].astype(jnp.float32) + self.from_x[z].astype(jnp.float32)
            self.total[z, self.y, self.x] = (here + self.from_y[z].astype(jnp.float32)).astype(jnp.bfloat16)
            if d:
                self.along_z(d).start()

    def result(self):
        total = self.total[self.z, self.y, self.x].astype(jnp.float32)
        for d in (1, 2, 3):
            self.along_z(d).wait_recv()
            total = total + self.from_z[d - 1].astype(jnp.float32)
        return total

    def drain(self):
        for kind in range(4):
            self.core(kind).wait_send()
        for d in range(4):
            self.turn(d, 0).wait_send()
            self.turn(d, 1).wait_send()
            self.to_x(d).wait_send()
            self.to_y(d).wait_send()
            if d:
                self.along_z(d).wait_send()


SUMS = 23


def work_shapes(lanes, cut):
    held = lambda *dims: pltpu.VMEM((*dims, 48, lanes), jnp.bfloat16)
    part = lambda size: pltpu.VMEM((4, 48, size), jnp.bfloat16)
    return [held(4, 2, 2), held(4, 2, 2), part(cut), part(lanes - cut), held(4), held(4), held(3)]


def scatter_kernel(*refs):
    count = len(WIRE)
    mine, outs, refs = refs[:count], refs[count : 2 * count], refs[2 * count :]
    work, (send, recv) = refs[: 7 * count], refs[7 * count :]
    greet(*place())
    order = (3, 2, 1, 0)
    sums = [Scatter(mine[i], CUT[i], work[7 * i : 7 * i + 7], send, recv, SUMS * i) for i in order]
    for one in sums:
        one.start()
    for step in range(count + 3):
        if step < count:
            sums[step].merge()
        if 0 <= step - 1 < count:
            sums[step - 1].bend()
        if 0 <= step - 2 < count:
            sums[step - 2].close()
        if 0 <= step - 3 < count:
            outs[order[step - 3]][...] = sums[step - 3].result()
    for one in sums:
        one.drain()


def scatter_all(pieces):
    vmem = pl.BlockSpec(memory_space=pltpu.VMEM)
    scratch = []
    for lanes, cut in zip(WIRE, CUT):
        scratch += work_shapes(lanes, cut)
    return pl.pallas_call(
        scatter_kernel,
        out_shape=tuple(jax.ShapeDtypeStruct((48, lanes), jnp.float32) for lanes in WIRE),
        in_specs=[vmem] * 4,
        out_specs=(vmem,) * 4,
        scratch_shapes=scratch + [pltpu.SemaphoreType.DMA((SUMS * 4,)), pltpu.SemaphoreType.DMA((SUMS * 4,))],
        compiler_params=pltpu.CompilerParams(collective_id=1, has_side_effects=True, vmem_limit_bytes=60 * 2**20),
    )(*pieces)


def on_wire(gradient, rows):
    lanes = gradient.shape[1]
    return gradient.reshape(32, rows, 2, lanes // 2).swapaxes(1, 2).reshape(32, 2 * rows, lanes // 2)


def vector_rows(vectors, lead):
    padded = [jnp.pad(one.reshape(*lead, -1), [(0, 0)] * len(lead) + [(0, 128 - one.size // math.prod(lead))]) for one in vectors]
    return jnp.pad(jnp.stack(padded, axis=-2), [(0, 0)] * len(lead) + [(0, 48 - len(vectors)), (0, 0)])


def fast_weights(shards):
    vectors = vector_rows(shards[7:], ())
    qkv, out, up, embed, down, rows = gather_all(*shards[:5], shards[6], shards[5], vectors)
    widths = [one.shape[0] for one in shards[7:]]
    full = [rows[:, i, :width].reshape(-1) for i, width in enumerate(widths)]
    return (qkv[:, :768], qkv[:, 768:1536], qkv[:, 1536:], out, up, down, embed, *full)


def fast_sums(totals):
    low = lambda one: one.astype(jnp.bfloat16)
    first = on_wire(low(jnp.concatenate(totals[:3], axis=1)), 24)
    first = jnp.concatenate([first, low(vector_rows(totals[7:], (32,)))], axis=-1)
    third = on_wire(low(jnp.concatenate([totals[4], totals[6], jnp.zeros((768, 128), jnp.float32)], axis=1)), 24)
    fourth = low(totals[5]).reshape(32, 2, 48, 768).swapaxes(1, 2).reshape(32, 48, 1536)
    pieces = (first, on_wire(low(totals[3]), 24), third, fourth)
    qkv, out, up, down = scatter_all([one.reshape(4, 2, 2, 2, 48, -1) for one in pieces])
    rows = jnp.concatenate([qkv[:24, :1152], qkv[24:, :1152]], axis=1)
    ups = jnp.concatenate([up[:24], up[24:]], axis=1)
    widths = [one.size // 32 for one in totals[7:]]
    return (
        rows[:, :768],
        rows[:, 768:1536],
        rows[:, 1536:],
        jnp.concatenate([out[:24], out[24:]], axis=1),
        ups[:, :3072],
        jnp.concatenate([down[:, :768], down[:, 768:]], axis=0),
        ups[:, 3072:3200],
        *[qkv[i, 1152 : 1152 + width] for i, width in enumerate(widths)],
    )


def body(fast, tokens_short, lengths_short, tokens_long, lengths_long, *rest):
    shards, (cotangent_short, cotangent_long) = rest[:16], rest[16:]
    if fast:
        weights = fast_weights(shards)
    else:
        weights = tuple(lax.all_gather(one, BOTH, axis=0, tiled=True) for one in shards)
    embed_short, saved_short = forward(tokens_short, lengths_short, weights)
    embed_long, saved_long = forward(tokens_long, lengths_long, weights)
    input_short, grads_short = backward(saved_short, weights, cotangent_short)
    input_long, grads_long = backward(saved_long, weights, cotangent_long)
    totals = jax.tree.map(jnp.add, grads_short, grads_long)
    if fast:
        owned = fast_sums(totals)
    else:
        owned = tuple(lax.psum_scatter(one, BOTH, scatter_dimension=0, tiled=True) for one in totals)
    return (embed_short, embed_long, input_short, input_long, *owned)


def solution(mesh):
    split = lambda rank: P(BOTH, *([None] * (rank - 1)))
    weights = [split(2)] * 7 + [split(1)] * 9
    in_specs = (split(3), split(1), split(3), split(1), *weights, split(3), split(3))
    out_specs = (split(3),) * 4 + tuple(weights)
    fast = mesh.shape["wide"] == 16 and mesh.shape["narrow"] == 2
    step = functools.partial(body, fast)
    return jax.shard_map(step, mesh=mesh, in_specs=in_specs, out_specs=out_specs, check_vma=False)
```

```python
import functools
import math

import jax
import jax.numpy as jnp
from jax import lax
from jax.experimental import pallas as pl
from jax.experimental.pallas import tpu as pltpu
from jax.sharding import PartitionSpec as P

MESH = pl.DeviceIdType.MESH

HD = 64
P_SIZE = 128


norm_epsilon = 1e-12
unit_epsilon = 1e-06
masked_fill = -1000000000.0


def layer_norm(residual, norm_gain, norm_shift):
    center = residual - jnp.mean(residual, axis=-1, keepdims=True)
    variance = jnp.mean(center * center, axis=-1, keepdims=True)
    return center * lax.rsqrt(variance + norm_epsilon) * norm_gain + norm_shift


def gelu_exact(pre_act):
    return 0.5 * pre_act * (1.0 + lax.erf(pre_act * (1.0 / math.sqrt(2.0))))


def normalize(embedding, token_mask):
    squares = jnp.sum(embedding * embedding, axis=-1, keepdims=True)
    return math.sqrt(P_SIZE) * embedding * lax.rsqrt(squares + unit_epsilon) * token_mask[..., None]


def soft_weights(scaled, key_mask):
    masked = jnp.where(key_mask, scaled, masked_fill)
    row_peak = jnp.max(masked, axis=-1, keepdims=True)
    exponent = jnp.exp(masked - row_peak)
    return exponent / jnp.sum(exponent, axis=-1, keepdims=True)


def matmul(left_side, right_side, form):
    return jnp.einsum(form, left_side, right_side, preferred_element_type=jnp.float32)


def forward(tokens, lengths, full_weights):
    (
        query_weight,
        key_weight,
        value_weight,
        out_weight,
        up_weight,
        down_weight,
        embed_weight,
        query_bias,
        value_bias,
        out_bias,
        attention_gain,
        attention_shift,
        up_bias,
        down_bias,
        final_gain,
        final_shift,
    ) = full_weights
    seq_count, length, model_width = tokens.shape
    head_count = model_width // HD
    score_scale = 1.0 / math.sqrt(HD)
    positions = jnp.arange(length, dtype=jnp.int32)
    token_mask = (positions[None, :] < lengths[:, None]).astype(jnp.float32)
    key_mask = token_mask[:, None, None, :] > 0.5
    query_low = (matmul(tokens, query_weight, "bld,de->ble") + query_bias).astype(jnp.bfloat16)
    query_low = query_low.reshape(seq_count, length, head_count, HD)
    key_low = matmul(tokens, key_weight, "bld,de->ble").astype(jnp.bfloat16)
    key_low = key_low.reshape(seq_count, length, head_count, HD)
    value_low = (matmul(tokens, value_weight, "bld,de->ble") + value_bias).astype(jnp.bfloat16)
    value_low = value_low.reshape(seq_count, length, head_count, HD)
    raw_scores = matmul(query_low, key_low, "bqhe,bkhe->bhqk") * score_scale
    attn_probs = soft_weights(raw_scores, key_mask)
    probs_low = attn_probs.astype(jnp.bfloat16)
    context_low = matmul(probs_low, value_low, "bhqk,bkhe->bqhe")
    context_low = context_low.reshape(seq_count, length, model_width).astype(jnp.bfloat16)
    attn_out = matmul(context_low, out_weight, "bld,de->ble") + out_bias
    resid_one = tokens.astype(jnp.float32) + attn_out
    normed_one = layer_norm(resid_one, attention_gain, attention_shift)
    hidden_low = normed_one.astype(jnp.bfloat16)
    pre_act = matmul(hidden_low, up_weight, "bld,df->blf") + up_bias
    act_low = gelu_exact(pre_act).astype(jnp.bfloat16)
    ffn_out = matmul(act_low, down_weight, "blf,fd->bld") + down_bias
    resid_two = normed_one + ffn_out
    final_low = layer_norm(resid_two, final_gain, final_shift).astype(jnp.bfloat16)
    embedding = matmul(final_low, embed_weight, "bld,dp->blp")
    result = normalize(embedding, token_mask)
    saved = (
        tokens,
        token_mask,
        query_low,
        key_low,
        value_low,
        attn_probs,
        probs_low,
        context_low,
        resid_one,
        hidden_low,
        pre_act,
        act_low,
        resid_two,
        final_low,
        embedding,
    )
    return (result, saved)


def backward(saved, full_weights, cotangent):
    (
        tokens,
        token_mask,
        query_low,
        key_low,
        value_low,
        attn_probs,
        probs_low,
        context_low,
        resid_one,
        hidden_low,
        pre_act,
        act_low,
        resid_two,
        final_low,
        embedding,
    ) = saved
    (
        query_weight,
        key_weight,
        value_weight,
        out_weight,
        up_weight,
        down_weight,
        embed_weight,
        query_bias,
        value_bias,
        out_bias,
        attention_gain,
        attention_shift,
        up_bias,
        down_bias,
        final_gain,
        final_shift,
    ) = full_weights
    seq_count, length, model_width = tokens.shape
    score_scale = 1.0 / math.sqrt(HD)
    _, pull_norm = jax.vjp(lambda vector: normalize(vector, token_mask), embedding)
    (embed_grad,) = pull_norm(cotangent.astype(jnp.float32))
    embed_low = embed_grad.astype(jnp.bfloat16)
    grad_embed = matmul(final_low, embed_low, "bld,blp->dp")
    final_grad = matmul(embed_low, embed_weight, "blp,dp->bld")
    _, pull_two = jax.vjp(
        layer_norm, resid_two, final_gain.astype(jnp.float32), final_shift.astype(jnp.float32)
    )
    resid_two_grad, grad_final_gain, grad_final_shift = pull_two(final_grad)
    ffn_low = resid_two_grad.astype(jnp.bfloat16)
    grad_down_bias = jnp.sum(ffn_low, axis=(0, 1), dtype=jnp.float32)
    grad_down = matmul(act_low, ffn_low, "blf,bld->fd")
    act_grad = matmul(ffn_low, down_weight, "bld,fd->blf")
    _, pull_gelu = jax.vjp(gelu_exact, pre_act)
    (pre_grad,) = pull_gelu(act_grad)
    pre_low = pre_grad.astype(jnp.bfloat16)
    grad_up_bias = jnp.sum(pre_low, axis=(0, 1), dtype=jnp.float32)
    grad_up = matmul(hidden_low, pre_low, "bld,blf->df")
    normed_grad = resid_two_grad + matmul(pre_low, up_weight, "blf,df->bld")
    _, pull_one = jax.vjp(
        layer_norm,
        resid_one,
        attention_gain.astype(jnp.float32),
        attention_shift.astype(jnp.float32),
    )
    resid_one_grad, grad_attention_gain, grad_attention_shift = pull_one(normed_grad)
    attn_low = resid_one_grad.astype(jnp.bfloat16)
    grad_out_bias = jnp.sum(attn_low, axis=(0, 1), dtype=jnp.float32)
    grad_out = matmul(context_low, attn_low, "bld,ble->de")
    context_grad = matmul(attn_low, out_weight, "ble,de->bld").astype(jnp.bfloat16)
    context_grad = context_grad.reshape(seq_count, length, -1, HD)
    value_grad = matmul(probs_low, context_grad, "bhqk,bqhe->bkhe")
    probs_grad = matmul(context_grad, value_low, "bqhe,bkhe->bhqk")
    score_low = attn_probs * (probs_grad - jnp.sum(probs_grad * attn_probs, axis=-1, keepdims=True))
    score_low = score_low.astype(jnp.bfloat16)
    query_grad = (matmul(score_low, key_low, "bhqk,bkhe->bqhe") * score_scale).astype(jnp.bfloat16)
    query_grad = query_grad.reshape(seq_count, length, model_width)
    key_grad = (matmul(score_low, query_low, "bhqk,bqhe->bkhe") * score_scale).astype(jnp.bfloat16)
    key_grad = key_grad.reshape(seq_count, length, model_width)
    value_grad_low = value_grad.astype(jnp.bfloat16).reshape(seq_count, length, model_width)
    grad_query_bias = jnp.sum(query_grad, axis=(0, 1), dtype=jnp.float32)
    grad_value_bias = jnp.sum(value_grad_low, axis=(0, 1), dtype=jnp.float32)
    grad_query = matmul(tokens, query_grad, "bld,ble->de")
    grad_key = matmul(tokens, key_grad, "bld,ble->de")
    grad_value = matmul(tokens, value_grad_low, "bld,ble->de")
    input_grad = (
        resid_one_grad
        + matmul(query_grad, query_weight, "ble,de->bld")
        + matmul(key_grad, key_weight, "ble,de->bld")
        + matmul(value_grad_low, value_weight, "ble,de->bld")
    )
    gradients = (
        grad_query,
        grad_key,
        grad_value,
        grad_out,
        grad_up,
        grad_down,
        grad_embed,
        grad_query_bias,
        grad_value_bias,
        grad_out_bias,
        grad_attention_gain,
        grad_attention_shift,
        grad_up_bias,
        grad_down_bias,
        grad_final_gain,
        grad_final_shift,
    )
    return (input_grad, gradients)


BOTH = ("wide", "narrow")
WIRE = (1280, 512, 1536, 1536)
CUT = (640, 256, 768, 768)
ROWS = 1792
SHORT = 512
COPIES = 39


def place():
    wide = lax.axis_index("wide")
    return wide // 4, (wide // 2) % 2, wide % 2, lax.axis_index("narrow")


def greet(z, y, c, x):
    partners = [device((z + d) % 4, y, c, x) for d in (1, 2, 3)]
    partners += [device(z, 1 - y, c, x), device(z, y, 1 - c, x), device(z, y, c, 1 - x)]
    barrier = pltpu.get_barrier_semaphore()
    for partner in partners:
        pl.semaphore_signal(barrier, inc=1, device_id=partner, device_id_type=MESH)
    pl.semaphore_wait(barrier, len(partners))


def device(z, y, c, x):
    return (z * 4 + y * 2 + c, x)


class Lazy:
    def __init__(self, make):
        self.make = make

    def __getitem__(self, way):
        return self.make(way)


class Gather:
    def __init__(self, held, cut, send, recv, first):
        self.held, self.cut, self.send, self.recv, self.first = held, cut, send, recv, first
        self.z, self.y, self.c, self.x = place()

    def view(self, block, half):
        if half is None:
            return self.held.at[block]
        lanes = self.held.shape[-1]
        low, size = ((0, self.cut), (self.cut, lanes - self.cut))[half]
        return self.held.at[(*block, slice(None), pl.ds(low, size))]

    def plan(self, slot, out, into, half, target):
        def copy(block):
            return pltpu.make_async_remote_copy(
                src_ref=self.view(block, half),
                dst_ref=self.view(block, half),
                send_sem=self.send.at[self.first + slot],
                recv_sem=self.recv.at[self.first + slot],
                device_id=target,
                device_id_type=MESH,
            )

        return Lazy(lambda way: copy((out, into)[way]))

    def along_z(self, d):
        z, y, c, x = self.z, self.y, self.c, self.x
        return self.plan(d - 1, (z, y, c, x), ((z + 4 - d) % 4, y, c, x), None, device((z + d) % 4, y, c, x))

    def to_x(self, d):
        z, y, c, x = (self.z + 4 - d) % 4, self.y, self.c, self.x
        return self.plan(3 + d, (z, y, c, x), (z, y, c, 1 - x), None, device(self.z, y, c, 1 - x))

    def to_y(self, d):
        z, y, c, x = (self.z + 4 - d) % 4, self.y, self.c, self.x
        return self.plan(7 + d, (z, y, c, x), (z, 1 - y, c, x), None, device(self.z, 1 - y, c, x))

    def corner(self, d, half):
        z, y, c, x = (self.z + 4 - d) % 4, self.y, self.c, self.x
        if half == 0:
            return self.plan(11 + d, (z, y, c, 1 - x), (z, 1 - y, c, 1 - x), 0, device(self.z, 1 - y, c, x))
        return self.plan(15 + d, (z, 1 - y, c, x), (z, 1 - y, c, 1 - x), 1, device(self.z, y, c, 1 - x))

    def to_core(self, d, kind):
        z, c = (self.z + 4 - d) % 4, self.c
        y = 1 - self.y if kind >= 2 else self.y
        x = 1 - self.x if kind in (1, 3, 4) else self.x
        half = kind - 3 if kind >= 3 else None
        return self.plan(19 + 4 * kind + d, (z, y, c, x), (z, y, 1 - c, x), half, device(self.z, self.y, 1 - c, self.x))

    def start_z(self):
        for d in (1, 2, 3):
            self.along_z(d)[0].start()

    def spread(self, d):
        self.to_x(d)[0].start()
        self.to_y(d)[0].start()
        self.to_core(d, 0)[0].start()

    def column(self, d):
        self.along_z(d)[1].wait_recv()
        self.spread(d)

    def turn(self, d):
        self.to_x(d)[1].wait_recv()
        self.corner(d, 0)[0].start()
        self.to_core(d, 1)[0].start()
        self.to_y(d)[1].wait_recv()
        self.corner(d, 1)[0].start()
        self.to_core(d, 2)[0].start()

    def finish(self, d):
        for half in (0, 1):
            self.corner(d, half)[1].wait_recv()
            self.to_core(d, 3 + half)[0].start()

    def arrive(self):
        for d in range(4):
            for kind in range(5):
                self.to_core(d, kind)[1].wait_recv()

    def drain(self):
        for d in range(4):
            if d:
                self.along_z(d)[0].wait_send()
            self.to_x(d)[0].wait_send()
            self.to_y(d)[0].wait_send()
            for half in (0, 1):
                self.corner(d, half)[0].wait_send()
            for kind in range(5):
                self.to_core(d, kind)[0].wait_send()


def stack_halves(whole):
    half = whole.shape[1] // 2
    return jnp.concatenate([whole[:, :half], whole[:, half:]], axis=0).astype(jnp.bfloat16)


def unpack_rows(held, targets):
    def pair(p, carry):
        z, y, c = p // 4, (p // 2) % 2, p % 2
        one, two = held[z, y, c, 0].astype(jnp.float32), held[z, y, c, 1].astype(jnp.float32)
        for side, low, ref, column, lanes in targets:
            rows = slice(24 * side, 24 * side + 24)
            both = jnp.concatenate([one[rows, low : low + lanes], two[rows, low : low + lanes]], axis=0)
            ref[pl.ds(pl.multiple_of(p * 48, 48), 48), column : column + lanes] = both.astype(jnp.bfloat16)
        return carry

    lax.fori_loop(0, 16, pair, 0)


NN = (((1,), (0,)), ((), ()))
NT = (((1,), (1,)), ((), ()))
TN = (((0,), (0,)), ((), ()))


def dot(left, right, dims):
    return lax.dot_general(left, right, dims, preferred_element_type=jnp.float32)


class Steps:
    def __init__(self, steps):
        self.steps = list(steps)

    def run(self, count=1):
        for _ in range(count):
            if self.steps:
                self.steps.pop(0)()

    def rest(self):
        self.run(len(self.steps))


def attend(qkv, context, probs, row, length, valid):
    rows = pl.ds(row, length)
    fill = jnp.where(lax.broadcasted_iota(jnp.int32, (1, length), 1) < valid, 0.0, masked_fill)
    lane = lax.broadcasted_iota(jnp.int32, (length, 128), 1)

    def pair(p, carry):
        at = lambda base: pl.ds(pl.multiple_of(base + p * 128, 128), 128)
        query = qkv[rows, at(0)] * jnp.bfloat16(1.0 / math.sqrt(HD))
        key, value = qkv[rows, at(768)], qkv[rows, at(1536)]
        total = None
        for h in (0, 1):
            here = (lane < 64) if h == 0 else (lane >= 64)
            scores = dot(query, jnp.where(here, key, jnp.bfloat16(0)), NT) + fill
            peak = jnp.max(scores, axis=1, keepdims=True)
            exponent = jnp.exp(scores - peak)
            scale = 1.0 / jnp.sum(exponent, axis=1, keepdims=True)
            low = (exponent * scale).astype(jnp.bfloat16)
            probs[2 * p + h] = low
            part = dot(low, jnp.where(here, value, jnp.bfloat16(0)), NN)
            total = part if total is None else total + part
        context[rows, at(0)] = total.astype(jnp.bfloat16)
        return carry

    lax.fori_loop(0, 6, pair, 0)


def natural_vectors(held, spread, spread_up, vec_out):
    blocks = [held[p // 8, (p // 4) % 2, (p // 2) % 2, p % 2, :16, 1152:1280] for p in range(32)]
    stacked = jnp.concatenate(blocks, axis=0)
    wide = dot(stacked, spread[...], NN)
    lane = lax.broadcasted_iota(jnp.int32, (512, 768), 1)
    start = (lax.broadcasted_iota(jnp.int32, (512, 768), 0) >> 4) * 24
    wide = jnp.where((lane >= start) & (lane < start + 24), wide, 0.0)
    vec_out[:, :768] = jnp.sum(wide.reshape(32, 16, 768), axis=0)
    picked = dot(
        (lax.broadcasted_iota(jnp.int32, (32, 512), 1) == lax.broadcasted_iota(jnp.int32, (32, 512), 0) * 16 + 5).astype(jnp.bfloat16),
        stacked,
        NN,
    ).astype(jnp.bfloat16)
    wide = dot(picked, spread_up[...], NN)
    lane = lax.broadcasted_iota(jnp.int32, (32, 3072), 1)
    start = lax.broadcasted_iota(jnp.int32, (32, 3072), 0) * 96
    wide = jnp.where((lane >= start) & (lane < start + 96), wide, 0.0)
    vec_out[9:10, :] = jnp.sum(wide, axis=0, keepdims=True)


def first_kernel(
    len_short, len_long, xs, xl, q_ref, k_ref, v_ref, o_ref, u_ref, e_ref, d_ref, vec_ref, spread, spread_up,
    qkv_out, out_out, up_out, embed_out, down_out, vec_out, proj_out, context_out, ps_out, pl_out,
    h0, h1, h2, h3, w_qkv, w_out, w_up, w_embed, w_down, proj, context, ps, pls, send, recv, away,
):
    z, y, c, x = place()
    wide = lambda ref: ref[...].astype(jnp.float32)
    h0[z, y, c, x, :, :1152] = stack_halves(jnp.concatenate([wide(q_ref), wide(k_ref), wide(v_ref)], axis=1))
    h0[z, y, c, x, :, 1152:] = vec_ref[...]
    h1[z, y, c, x, :, :384] = stack_halves(wide(o_ref))
    h1[z, y, c, x, :, 384:] = jnp.concatenate([wide(e_ref), wide(e_ref)], axis=0).astype(jnp.bfloat16)
    h2[z, y, c, x] = stack_halves(wide(u_ref))
    h3[z, y, c, x, :, :768] = d_ref[:48]
    h3[z, y, c, x, :, 768:] = d_ref[48:]
    greet(z, y, c, x)
    one, two, three, four = gathers = [Gather(h, CUT[i], send, recv, COPIES * i) for i, h in enumerate((h0, h1, h2, h3))]
    for piece in gathers:
        piece.start_z()
    one.spread(0)
    for d in (1, 2, 3):
        one.column(d)
    two.spread(0)
    for d in range(4):
        one.turn(d)
    three.spread(0)
    for d in range(4):
        one.finish(d)
    one.arrive()
    kept = []

    def keep(source, target):
        copy = pltpu.make_async_copy(source, target, away.at[len(kept)])
        copy.start()
        kept.append(copy)

    unpack_rows(h0, [(0, 0, w_qkv, 0, 1152), (1, 0, w_qkv, 1152, 1152)])
    keep(w_qkv, qkv_out)
    natural_vectors(h0, spread, spread_up, vec_out)
    steps = Steps(
        [functools.partial(two.column, d) for d in (1, 2, 3)]
        + [functools.partial(three.column, d) for d in (1, 2, 3)]
        + [functools.partial(two.turn, d) for d in range(4)]
        + [functools.partial(four.spread, 0)]
        + [functools.partial(three.turn, d) for d in range(4)]
        + [functools.partial(two.finish, d) for d in range(4)]
        + [functools.partial(four.column, d) for d in (1, 2, 3)]
        + [functools.partial(three.finish, d) for d in range(4)]
        + [functools.partial(four.turn, d) for d in range(4)]
        + [functools.partial(four.finish, d) for d in range(4)]
    )
    for row, tokens in [(0, xs[...].reshape(SHORT, 768))] + [(SHORT + 320 * s, xl[s]) for s in range(4)]:
        for part in range(3):
            lanes = slice(768 * part, 768 * part + 768)
            result = dot(tokens, w_qkv[:, lanes], NN)
            if part != 1:
                result = result + vec_out[part // 2 : part // 2 + 1, :768]
            proj[row : row + tokens.shape[0], lanes] = result.astype(jnp.bfloat16)
            steps.run(1)
    keep(proj, proj_out)
    for s in range(4):
        attend(proj, context, ps.at[s], 128 * s, 128, len_short[s])
        steps.run(1)
    keep(ps, ps_out)
    slots = []
    for s in range(4):
        if s >= 2:
            slots[s - 2].wait()
        attend(proj, context, pls.at[s % 2], SHORT + 320 * s, 320, len_long[s])
        copy = pltpu.make_async_copy(pls.at[s % 2], pl_out.at[s], away.at[8 + s])
        copy.start()
        slots.append(copy)
        steps.run(3)
    keep(context, context_out)
    steps.rest()
    two.arrive()
    unpack_rows(h1, [(0, 0, w_out, 0, 384), (1, 0, w_out, 384, 384), (0, 384, w_embed, 0, 128)])
    keep(w_out, out_out)
    keep(w_embed, embed_out)
    three.arrive()
    unpack_rows(h2, [(0, 0, w_up, 0, 1536), (1, 0, w_up, 1536, 1536)])
    keep(w_up, up_out)
    four.arrive()

    def down(p, carry):
        block = h3[p // 8, (p // 4) % 2, (p // 2) % 2, p % 2]
        w_down[pl.ds(pl.multiple_of(p * 96, 96), 48)] = block[:, :768]
        w_down[pl.ds(pl.multiple_of(p * 96 + 48, 48), 48)] = block[:, 768:]
        return carry

    lax.fori_loop(0, 32, down, 0)
    keep(w_down, down_out)
    for copy in kept + slots[2:]:
        copy.wait()
    for piece in gathers:
        piece.drain()


def spread_table(group, lanes):
    return (jnp.arange(lanes)[None, :] % group == jnp.arange(128)[:, None]).astype(jnp.bfloat16)


def first(len_short, len_long, xs, xl, shards):
    query, key, value, out, up, down, embed, *vectors = shards
    vmem, smem, anywhere = (pl.BlockSpec(memory_space=m) for m in (pltpu.VMEM, pltpu.SMEM, pl.ANY))
    low = lambda *dims: jax.ShapeDtypeStruct(dims, jnp.bfloat16)
    held = lambda *dims: pltpu.VMEM(dims, jnp.bfloat16)
    weights = [(768, 2304), (768, 768), (768, 3072), (768, 128), (3072, 768)]
    return pl.pallas_call(
        first_kernel,
        out_shape=(
            *[low(*dims) for dims in weights],
            jax.ShapeDtypeStruct((16, 3072), jnp.float32),
            low(ROWS, 2304), low(ROWS, 768), low(4, 12, 128, 128), low(4, 12, 320, 320),
        ),
        in_specs=[smem] * 2 + [vmem] * 12,
        out_specs=(anywhere,) * 5 + (vmem,) + (anywhere,) * 4,
        scratch_shapes=[held(4, 2, 2, 2, 48, lanes) for lanes in WIRE]
        + [held(*dims) for dims in weights]
        + [held(ROWS, 2304), held(ROWS, 768), held(4, 12, 128, 128), held(2, 12, 320, 320)]
        + [pltpu.SemaphoreType.DMA((COPIES * 4,)), pltpu.SemaphoreType.DMA((COPIES * 4,)), pltpu.SemaphoreType.DMA((12,))],
        compiler_params=pltpu.CompilerParams(collective_id=0, has_side_effects=True, vmem_limit_bytes=62 * 2**20),
    )(len_short, len_long, xs, xl, query, key, value, out, up, embed, down, vector_rows(vectors, ()), spread_table(24, 768), spread_table(96, 3072))


TILE = 256


def center(value):
    return value - jnp.mean(value, axis=1, keepdims=True)


def normal(value):
    value = center(value)
    scale = lax.rsqrt(jnp.mean(value * value, axis=1, keepdims=True) + norm_epsilon)
    return value * scale, scale


def normal_back(grad, unit, scale):
    inner = jnp.mean(grad * unit, axis=1, keepdims=True)
    return scale * (center(grad) - unit * inner)


def token_kernel(
    len_short, len_long, xs, xl, cs, cl, ctx_ref, w_out, w_up, w_down, w_embed, vec,
    es_out, el_out, act_out, pre_out, hidden_out, ffn_out, attn_out, final_out, eg_out, resid_out, cg_out, sums,
    slope,
):
    tile = pl.program_id(0)
    is_short = tile < 2
    row = lambda k: vec[k : k + 1, :768]
    low = lambda value: value.astype(jnp.bfloat16)
    wide = lambda value: value.astype(jnp.float32)

    @pl.when(tile == 0)
    def _():
        sums[...] = jnp.zeros_like(sums)

    def add(k, value):
        sums[k : k + 1, : value.shape[1]] += jnp.sum(value, axis=0, keepdims=True)

    tokens = jnp.where(is_short, xs[...], xl[...])
    context = ctx_ref[...]
    unit_one, scale_one = normal(wide(tokens) + (dot(context, w_out[...], NN) + row(2)))
    normed_one = unit_one * row(3) + row(4)
    hidden = low(normed_one)
    hidden_out[...] = hidden
    ffn = None
    for f in range(4):
        lanes = slice(768 * f, 768 * f + 768)
        pre = dot(hidden, w_up[:, lanes], NN) + vec[9:10, lanes]
        cdf = 0.5 + 0.5 * lax.erf(pre * (1.0 / math.sqrt(2.0)))
        act = low(pre * cdf)
        act_out[:, lanes] = act
        slope[:, lanes] = cdf + pre * (jnp.exp(-0.5 * pre * pre) * (1.0 / math.sqrt(2.0 * math.pi)))
        part = dot(act, w_down[lanes, :], NN)
        ffn = part if ffn is None else ffn + part
    unit_two, scale_two = normal(normed_one + (ffn + row(6)))
    final = low(unit_two * row(7) + row(8))
    final_out[...] = final
    embedding = dot(final, w_embed[...], NN)
    inverse = lax.rsqrt(jnp.sum(embedding * embedding, axis=1, keepdims=True) + unit_epsilon)
    first = jnp.where(is_short, tile, tile - 2) * TILE
    at = lax.broadcasted_iota(jnp.int32, (TILE, 1), 0) + first
    stride = jnp.where(is_short, 128, 320)
    mask = jnp.zeros((TILE, 1), jnp.float32)
    for s in range(4):
        size = jnp.where(is_short, len_short[s], len_long[s])
        mask = mask + jnp.where((at >= s * stride) & (at < s * stride + size), 1.0, 0.0)
    result = math.sqrt(P_SIZE) * embedding * inverse * mask

    @pl.when(is_short)
    def _():
        es_out[...] = result

    @pl.when(jnp.logical_not(is_short))
    def _():
        el_out[...] = result

    grad = wide(jnp.where(is_short, cs[...], cl[...])) * mask
    inner = jnp.sum(grad * embedding, axis=1, keepdims=True)
    embed_grad = low(math.sqrt(P_SIZE) * inverse * (grad - inverse * inverse * embedding * inner))
    eg_out[...] = embed_grad
    final_grad = dot(embed_grad, w_embed[...], NT)
    add(7, final_grad * unit_two)
    add(8, final_grad)
    resid_two = normal_back(final_grad * row(7), unit_two, scale_two)
    ffn_grad = low(resid_two)
    ffn_out[...] = ffn_grad
    add(6, wide(ffn_grad))
    normed_grad = resid_two
    for f in range(4):
        lanes = slice(768 * f, 768 * f + 768)
        pre_grad = low(dot(ffn_grad, w_down[lanes, :], NT) * slope[:, lanes])
        pre_out[:, lanes] = pre_grad
        sums[9:10, lanes] += jnp.sum(wide(pre_grad), axis=0, keepdims=True)
        normed_grad = normed_grad + dot(pre_grad, w_up[:, lanes], NT)
    add(3, normed_grad * unit_one)
    add(4, normed_grad)
    resid_one = normal_back(normed_grad * row(3), unit_one, scale_one)
    resid_out[...] = resid_one
    attn_grad = low(resid_one)
    attn_out[...] = attn_grad
    add(2, wide(attn_grad))
    cg_out[...] = low(dot(attn_grad, w_out[...], NT))


def token_chain(len_short, len_long, xs, xl, cs, cl, context, w_out, w_up, w_down, w_embed, vec):
    smem = pl.BlockSpec(memory_space=pltpu.SMEM)
    short = lambda lanes: pl.BlockSpec((TILE, lanes), lambda i: (jnp.minimum(i, 1), 0))
    long = lambda lanes: pl.BlockSpec((TILE, lanes), lambda i: (jnp.maximum(i - 2, 0), 0))
    every = lambda lanes: pl.BlockSpec((TILE, lanes), lambda i: (i, 0))
    whole = lambda array: pl.BlockSpec(array.shape, lambda i: (0, 0), pipeline_mode=pl.Buffered(1))
    shape = lambda kind, *dims: jax.ShapeDtypeStruct(dims, kind)
    low = lambda lanes: shape(jnp.bfloat16, ROWS, lanes)
    return pl.pallas_call(
        token_kernel,
        grid=(ROWS // TILE,),
        out_shape=(
            shape(jnp.float32, SHORT, P_SIZE), shape(jnp.float32, ROWS - SHORT, P_SIZE),
            low(3072), low(3072), low(768), low(768), low(768), low(768), low(P_SIZE),
            shape(jnp.float32, ROWS, 768), low(768), shape(jnp.float32, 16, 3072),
        ),
        in_specs=[smem, smem, short(768), long(768), short(P_SIZE), long(P_SIZE), every(768)]
        + [whole(one) for one in (w_out, w_up, w_down, w_embed, vec)],
        out_specs=(
            short(P_SIZE), long(P_SIZE), every(3072), every(3072), every(768), every(768), every(768), every(768), every(P_SIZE),
            every(768), every(768), pl.BlockSpec((16, 3072), lambda i: (0, 0)),
        ),
        scratch_shapes=[pltpu.VMEM((TILE, 3072), jnp.float32)],
        compiler_params=pltpu.CompilerParams(vmem_limit_bytes=60 * 2**20),
    )(len_short, len_long, xs.reshape(SHORT, 768), xl.reshape(ROWS - SHORT, 768), cs.reshape(SHORT, P_SIZE), cl.reshape(ROWS - SHORT, P_SIZE), context, w_out, w_up, w_down, w_embed, vec)


def wire_rows(total, out, left, right, lanes, low):
    def one(i, carry):
        rows = pl.ds(pl.multiple_of(i * 24, 8), 24)
        both = jnp.concatenate([total[rows, left : left + lanes], total[rows, right : right + lanes]], axis=0)
        out[i, :, low : low + lanes] = both.astype(jnp.bfloat16)
        return carry

    lax.fori_loop(0, 32, one, 0)


def down_kernel(act, grad, out):
    total = dot(act[...], grad[...], TN).astype(jnp.bfloat16)
    for i in range(8):
        out[i, :, :768] = total[96 * i : 96 * i + 48]
        out[i, :, 768:] = total[96 * i + 48 : 96 * i + 96]


def up_kernel(hidden, left, right, out, total):
    lanes = left.shape[1]
    total[:, :lanes] = dot(hidden[...], left[...], TN)
    total[:, lanes:] = dot(hidden[...], right[...], TN)
    wire_rows(total, out, 0, lanes, lanes, 0)


def out_kernel(context, attn, final, embed, out, total):
    total[:, :768] = dot(context[...], attn[...], TN)
    total[:, 768:] = dot(final[...], embed[...], TN)
    wire_rows(total, out, 0, 384, 384, 0)
    wire_rows(total, out, 768, 768, 128, 384)


def weight_sums(context, act, pre, hidden, ffn, attn, final, embed):
    low = lambda *dims: jax.ShapeDtypeStruct(dims, jnp.bfloat16)
    params = pltpu.CompilerParams(vmem_limit_bytes=60 * 2**20)
    fixed = lambda lanes: pl.BlockSpec((ROWS, lanes), lambda i: (0, 0))
    down = pl.pallas_call(
        down_kernel,
        grid=(4,),
        out_shape=low(32, 48, 1536),
        in_specs=[pl.BlockSpec((ROWS, 768), lambda i: (0, i)), fixed(768)],
        out_specs=pl.BlockSpec((8, 48, 1536), lambda i: (i, 0, 0)),
        compiler_params=params,
    )(act, ffn)
    lanes = 512
    up = pl.pallas_call(
        up_kernel,
        grid=(1536 // lanes,),
        out_shape=low(32, 48, 1536),
        in_specs=[fixed(768), pl.BlockSpec((ROWS, lanes), lambda i: (0, i)), pl.BlockSpec((ROWS, lanes), lambda i: (0, i + 1536 // lanes))],
        out_specs=pl.BlockSpec((32, 48, lanes), lambda i: (0, 0, i)),
        scratch_shapes=[pltpu.VMEM((768, 2 * lanes), jnp.float32)],
        compiler_params=params,
    )(hidden, pre, pre)
    out = pl.pallas_call(
        out_kernel,
        out_shape=low(32, 48, 512),
        scratch_shapes=[pltpu.VMEM((768, 896), jnp.float32)],
        compiler_params=params,
    )(context, attn, final, embed)
    return out, up, down


class Scatter:
    def __init__(self, mine, cut, work, send, recv, local, number):
        self.mine, self.cut, self.send, self.recv, self.first = mine, cut, send, recv, SUMS * number
        self.core_in, self.total, self.corner_y, self.corner_x, self.from_x, self.from_y, self.from_z = work
        self.z, self.y, self.c, self.x = place()
        self.own = pltpu.make_async_copy(mine.at[:, :, self.c], self.total, local.at[number])

    def copy(self, slot, source, target, partner):
        return pltpu.make_async_remote_copy(
            src_ref=source,
            dst_ref=target,
            send_sem=self.send.at[self.first + slot],
            recv_sem=self.recv.at[self.first + slot],
            device_id=partner,
            device_id_type=MESH,
        )

    def spot(self, kind):
        return (1 - self.y if kind in (0, 2) else self.y), (1 - self.x if kind in (0, 1) else self.x)

    def core(self, kind):
        y, x = self.spot(kind)
        return self.copy(
            kind,
            self.mine.at[:, y, 1 - self.c, x],
            self.core_in.at[:, y, x],
            device(self.z, self.y, 1 - self.c, self.x),
        )

    def corner(self, d, half):
        z = (self.z + d) % 4
        y, x = self.spot(0)
        low, size = ((0, self.cut), (self.cut, self.total.shape[-1] - self.cut))[half]
        source = self.total.at[z, y, x, :, pl.ds(low, size)]
        if half == 0:
            return self.copy(4 + d, source, self.corner_y.at[z], device(self.z, 1 - self.y, self.c, self.x))
        return self.copy(8 + d, source, self.corner_x.at[z], device(self.z, self.y, self.c, 1 - self.x))

    def to_x(self, d):
        z = (self.z + d) % 4
        return self.copy(12 + d, self.total.at[z, self.y, 1 - self.x], self.from_x.at[z], device(self.z, self.y, self.c, 1 - self.x))

    def to_y(self, d):
        z = (self.z + d) % 4
        return self.copy(16 + d, self.total.at[z, 1 - self.y, self.x], self.from_y.at[z], device(self.z, 1 - self.y, self.c, self.x))

    def along_z(self, d):
        z = (self.z + d) % 4
        return self.copy(19 + d, self.total.at[z, self.y, self.x], self.from_z.at[d - 1], device(z, self.y, self.c, self.x))

    def start(self):
        self.own.start()
        for kind in range(4):
            self.core(kind).start()

    def merge(self, kind):
        if kind == 0:
            self.own.wait()
        self.core(kind).wait_recv()
        y, x = self.spot(kind)

        def add(z, carry):
            here = self.total[z, y, x].astype(jnp.float32)
            self.total[z, y, x] = (here + self.core_in[z, y, x].astype(jnp.float32)).astype(jnp.bfloat16)
            return carry

        lax.fori_loop(0, 4, add, 0)
        if kind == 0:
            for d in (1, 2, 3, 0):
                self.corner(d, 0).start()
                self.corner(d, 1).start()

    def bend(self, d):
        z = (self.z + d) % 4
        self.corner(d, 0).wait_recv()
        here = self.total[z, self.y, 1 - self.x, :, : self.cut].astype(jnp.float32)
        self.total[z, self.y, 1 - self.x, :, : self.cut] = (here + self.corner_y[z].astype(jnp.float32)).astype(jnp.bfloat16)
        self.to_x(d).start()
        self.corner(d, 1).wait_recv()
        here = self.total[z, 1 - self.y, self.x, :, self.cut :].astype(jnp.float32)
        self.total[z, 1 - self.y, self.x, :, self.cut :] = (here + self.corner_x[z].astype(jnp.float32)).astype(jnp.bfloat16)
        self.to_y(d).start()

    def close(self, d):
        z = (self.z + d) % 4
        self.to_x(d).wait_recv()
        self.to_y(d).wait_recv()
        here = self.total[z, self.y, self.x].astype(jnp.float32) + self.from_x[z].astype(jnp.float32)
        self.total[z, self.y, self.x] = (here + self.from_y[z].astype(jnp.float32)).astype(jnp.bfloat16)
        if d:
            self.along_z(d).start()

    def result(self, store):
        total = self.total[self.z, self.y, self.x].astype(jnp.float32)
        for d in (1, 2, 3):
            self.along_z(d).wait_recv()
            total = total + self.from_z[d - 1].astype(jnp.float32)
        store(total)

    def drain(self):
        for kind in range(4):
            self.core(kind).wait_send()
        for d in range(4):
            self.corner(d, 0).wait_send()
            self.corner(d, 1).wait_send()
            self.to_x(d).wait_send()
            self.to_y(d).wait_send()
            if d:
                self.along_z(d).wait_send()


SUMS = 23
BACK = (1536, 1536, 512, 512, 384, 384)
BACK_CUT = (768, 768, 256, 256, 128, 256)


def work_shapes(lanes, cut):
    held = lambda *dims: pltpu.VMEM((*dims, 48, lanes), jnp.bfloat16)
    part = lambda size: pltpu.VMEM((4, 48, size), jnp.bfloat16)
    return [held(4, 2, 2), held(4, 2, 2), part(cut), part(lanes - cut), held(4), held(4), held(3)]


def attend_back(proj, grads_in, probs, grads, vectors, row, length, first, last):
    rows = pl.ds(row, length)
    lane = lax.broadcasted_iota(jnp.int32, (length, 128), 1)
    score_scale = 1.0 / math.sqrt(HD)

    def pair(p, carry):
        at = lambda base: pl.ds(pl.multiple_of(base + p * 128, 128), 128)
        query, key, value = (proj[:length, at(base)] for base in (0, 768, 1536))
        context_grad = grads_in[:length, at(0)]
        query_grad, key_grads, value_grads = None, [], []
        for h in (0, 1):
            here = (lane < 64) if h == 0 else (lane >= 64)
            low = probs[2 * p + h, :length, :length]
            weight = low.astype(jnp.float32)
            weight_grad = dot(context_grad, jnp.where(here, value, jnp.bfloat16(0)), NT)
            inner = jnp.sum(weight_grad * weight, axis=1, keepdims=True)
            score_grad = (weight * (weight_grad - inner)).astype(jnp.bfloat16)
            part = dot(score_grad, jnp.where(here, key, jnp.bfloat16(0)), NN)
            query_grad = part if query_grad is None else query_grad + part
            key_grads.append(dot(score_grad, query, TN))
            value_grads.append(dot(low, context_grad, TN))
        query_low = (query_grad * score_scale).astype(jnp.bfloat16)
        key_low = (jnp.where(lane < 64, *key_grads) * score_scale).astype(jnp.bfloat16)
        value_low = jnp.where(lane < 64, *value_grads).astype(jnp.bfloat16)
        grads[rows, at(0)] = query_low
        grads[rows, at(768)] = key_low
        grads[rows, at(1536)] = value_low
        vectors[0:1, at(0)] += jnp.sum(query_low.astype(jnp.float32), axis=0, keepdims=True)
        vectors[1:2, at(0)] += jnp.sum(value_low.astype(jnp.float32), axis=0, keepdims=True)
        return carry

    lax.fori_loop(first, last, pair, 0)


def vectors_on_wire(vectors, spread, spread_up, out, low):
    lane = lax.broadcasted_iota(jnp.int32, (512, 768), 1)
    start = (lax.broadcasted_iota(jnp.int32, (512, 768), 0) >> 4) * 24
    wide = jnp.broadcast_to(vectors[:, :768][None], (32, 16, 768)).reshape(512, 768)
    wide = jnp.where((lane >= start) & (lane < start + 24), wide, 0.0).astype(jnp.bfloat16)
    rows = dot(wide, spread[...], NT).reshape(32, 16, 128)
    lane = lax.broadcasted_iota(jnp.int32, (32, 3072), 1)
    start = lax.broadcasted_iota(jnp.int32, (32, 3072), 0) * 96
    wide = jnp.where((lane >= start) & (lane < start + 96), vectors[9:10, :], 0.0).astype(jnp.bfloat16)
    up_rows = dot(wide, spread_up[...], NT)
    number = lax.broadcasted_iota(jnp.int32, (32, 16, 128), 1)
    rows = jnp.where(number == 5, up_rows[:, None, :], rows).astype(jnp.bfloat16)
    for i in range(32):
        out[i // 8, (i // 4) % 2, (i // 2) % 2, i % 2, :16, low : low + 128] = rows[i]
        out[i // 8, (i // 4) % 2, (i // 2) % 2, i % 2, 16:, low : low + 128] = jnp.zeros((32, 128), jnp.bfloat16)


def wire_blocks(total, out):
    def one(i, carry):
        rows = pl.ds(pl.multiple_of(i * 24, 8), 24)
        both = jnp.concatenate([total[rows, :384], total[rows, 384:]], axis=0)
        out[i // 8, (i // 4) % 2, (i // 2) % 2, i % 2, :, :384] = both.astype(jnp.bfloat16)
        return carry

    lax.fori_loop(0, 32, one, 0)


def last_kernel(
    p_down, p_up, p_out, proj, context_grad, ps, pls, w_qkv_in, resid, sums, xs, xl, spread, spread_up,
    gs_out, gl_out, q_out, k_out, v_out, o_out, u_out, d_out, e_out, vec_out,
    p_query, p_key, p_value, slot_proj, slot_grad, slot_pl, grads, w_qkv, total, vectors, *rest,
):
    work, (send, recv, local, load, fetch) = rest[: 7 * len(BACK)], rest[7 * len(BACK) :]
    mine = (p_down, p_up, p_out, p_query, p_key, p_value)
    greet(*place())
    down, up, out, query, key, value = pieces = [
        Scatter(one, BACK_CUT[i], work[7 * i : 7 * i + 7], send, recv, local, i) for i, one in enumerate(mine)
    ]
    order = [(SHORT + 320 * s, 320, s) for s in range(4)] + [(128 * s, 128, s) for s in range(4)]

    def loads(n):
        row, length, s = order[n]
        slot = n % 2
        source = pls if length == 320 else ps
        return [
            pltpu.make_async_copy(proj.at[pl.ds(row, length)], slot_proj.at[slot, :length], load.at[slot, 0]),
            pltpu.make_async_copy(context_grad.at[pl.ds(row, length)], slot_grad.at[slot, :length], load.at[slot, 1]),
            pltpu.make_async_copy(source.at[s], slot_pl.at[slot, :, :length, :length], load.at[slot, 2]),
        ]

    for copy in loads(0):
        copy.start()
    for piece in (down, up, out):
        piece.start()
    fetches = [
        pltpu.make_async_copy(w_qkv_in, w_qkv, fetch.at[0]),
        pltpu.make_async_copy(resid.at[:SHORT], gs_out, fetch.at[1]),
        pltpu.make_async_copy(resid.at[SHORT:], gl_out, fetch.at[2]),
    ]
    for copy in fetches:
        copy.start()
    vectors[...] = sums[...]

    def put(target):
        def store(value):
            half = target.shape[1] // 2
            target[:, :half] = value[:24, :half]
            target[:, half:] = value[24:, :half]

        return store

    def put_down(value):
        d_out[:48], d_out[48:] = value[:, :768], value[:, 768:]

    def put_out(value):
        put(o_out)(value)
        e_out[...] = value[:24, 384:]

    def put_query(value):
        put(q_out)(value)
        vec_out[...] = value[:16, 384:]

    stores = (put_down, put(u_out), put_out, put_query, put(k_out), put(v_out))
    merges, bends, closes = ([[functools.partial(getattr(one, name), d) for d in range(4)] for one in pieces] for name in ("merge", "bend", "close"))
    turned = lambda rows: [rows[d] for d in (1, 2, 3, 0)]
    ends = [functools.partial(one.result, store) for one, store in zip(pieces, stores)]
    steps = Steps(
        merges[0] + merges[1] + turned(bends[0]) + merges[2] + turned(bends[1]) + turned(closes[0])
        + turned(bends[2]) + turned(closes[1]) + turned(closes[2]) + ends[:3]
    )
    for n, (row, length, s) in enumerate(order):
        if n + 1 < len(order):
            for copy in loads(n + 1):
                copy.start()
        for copy in loads(n):
            copy.wait()
        slot = n % 2
        probs = slot_pl.at[slot]
        cuts = (0, 2, 4, 6) if length == 320 else (0, 6)
        for first, last in zip(cuts[:-1], cuts[1:]):
            attend_back(slot_proj.at[slot], slot_grad.at[slot], probs, grads, vectors, row, length, first, last)
            steps.run(3)
    tokens = [xs[...].reshape(SHORT, 768), xl[...].reshape(ROWS - SHORT, 768)]
    vectors_on_wire(vectors, spread, spread_up, p_query, 384)
    for part, (piece, held) in enumerate(((query, p_query), (key, p_key), (value, p_value))):
        lanes = slice(768 * part, 768 * part + 768)
        total[...] = dot(tokens[0], grads[:SHORT, lanes], TN) + dot(tokens[1], grads[SHORT:, lanes], TN)
        wire_blocks(total, held)
        piece.start()
        steps.run(3)
    for copy in fetches:
        copy.wait()
    steps.rest()
    steps = Steps(
        merges[3] + merges[4] + merges[5] + turned(bends[3]) + turned(bends[4]) + turned(bends[5])
        + turned(closes[3]) + turned(closes[4]) + turned(closes[5]) + ends[3:]
    )
    for target, at, row, length in [(gs_out, 0, 0, SHORT)] + [(gl_out, 320 * s, SHORT + 320 * s, 320) for s in range(4)]:
        target[at : at + length] += dot(grads[row : row + length], w_qkv[...], NT)
        steps.run(3)
    steps.rest()
    for piece in pieces:
        piece.drain()


def last(pieces, proj, context_grad, ps, pls, w_qkv, resid, sums, xs, xl):
    vmem, anywhere = (pl.BlockSpec(memory_space=m) for m in (pltpu.VMEM, pl.ANY))
    full = lambda *dims: jax.ShapeDtypeStruct(dims, jnp.float32)
    held = lambda *dims: pltpu.VMEM(dims, jnp.bfloat16)
    semaphores = lambda *dims: pltpu.SemaphoreType.DMA(dims)
    scratch = []
    for lanes, cut in zip(BACK, BACK_CUT):
        scratch += work_shapes(lanes, cut)
    out, up, down = (one.reshape(4, 2, 2, 2, 48, -1) for one in pieces)
    return pl.pallas_call(
        last_kernel,
        out_shape=(
            full(SHORT, 768), full(ROWS - SHORT, 768), full(24, 768), full(24, 768), full(24, 768), full(24, 768),
            full(24, 3072), full(96, 768), full(24, 128), full(16, 128),
        ),
        in_specs=[anywhere] * 9 + [vmem] * 5,
        out_specs=(vmem,) * 10,
        scratch_shapes=[held(4, 2, 2, 2, 48, lanes) for lanes in BACK[3:]]
        + [held(2, 320, 2304), held(2, 320, 768), held(2, 12, 320, 320), held(ROWS, 2304), held(768, 2304)]
        + [pltpu.VMEM((768, 768), jnp.float32), pltpu.VMEM((16, 3072), jnp.float32)]
        + scratch
        + [semaphores(SUMS * len(BACK)), semaphores(SUMS * len(BACK)), semaphores(len(BACK)), semaphores(2, 3), semaphores(3)],
        compiler_params=pltpu.CompilerParams(collective_id=1, has_side_effects=True, vmem_limit_bytes=63 * 2**20),
    )(down, up, out, proj, context_grad, ps, pls, w_qkv, resid, sums, xs, xl, spread_table(24, 768), spread_table(96, 3072))


def vector_rows(vectors, lead):
    padded = [jnp.pad(one.reshape(*lead, -1), [(0, 0)] * len(lead) + [(0, 128 - one.size // math.prod(lead))]) for one in vectors]
    return jnp.pad(jnp.stack(padded, axis=-2), [(0, 0)] * len(lead) + [(0, 48 - len(vectors)), (0, 0)])


def fast_body(xs, len_short, xl, len_long, shards, cs, cl):
    w_qkv, w_out, w_up, w_embed, w_down, vec, proj, context, ps, pls = first(len_short, len_long, xs, xl, shards)
    es, el, act, pre, hidden, ffn, attn, final, embed_grad, resid, context_grad, sums = token_chain(
        len_short, len_long, xs, xl, cs, cl, context, w_out, w_up, w_down, w_embed, vec
    )
    pieces = weight_sums(context, act, pre, hidden, ffn, attn, final, embed_grad)
    gs, gl, query, key, value, out, up, down, embed, rows = last(pieces, proj, context_grad, ps, pls, w_qkv, resid, sums, xs, xl)
    owned = [rows[i, : one.shape[0]] for i, one in enumerate(shards[7:])]
    shaped = lambda flat, like: flat.reshape(*like.shape[:2], -1)
    return (shaped(es, xs), shaped(el, xl), shaped(gs, xs), shaped(gl, xl), query, key, value, out, up, down, embed, *owned)


def body(tokens_short, lengths_short, tokens_long, lengths_long, *rest):
    shards, (cotangent_short, cotangent_long) = rest[:16], rest[16:]
    weights = tuple(lax.all_gather(one, BOTH, axis=0, tiled=True) for one in shards)
    embed_short, saved_short = forward(tokens_short, lengths_short, weights)
    embed_long, saved_long = forward(tokens_long, lengths_long, weights)
    input_short, grads_short = backward(saved_short, weights, cotangent_short)
    input_long, grads_long = backward(saved_long, weights, cotangent_long)
    totals = jax.tree.map(jnp.add, grads_short, grads_long)
    owned = tuple(lax.psum_scatter(one, BOTH, scatter_dimension=0, tiled=True) for one in totals)
    return (embed_short, embed_long, input_short, input_long, *owned)


def solution(mesh):
    split = lambda rank: P(BOTH, *([None] * (rank - 1)))
    weights = [split(2)] * 7 + [split(1)] * 9
    in_specs = (split(3), split(1), split(3), split(1), *weights, split(3), split(3))
    out_specs = (split(3),) * 4 + tuple(weights)
    fast = mesh.shape["wide"] == 16 and mesh.shape["narrow"] == 2

    def step(xs, len_short, xl, len_long, *rest):
        if fast:
            return fast_body(xs, len_short, xl, len_long, rest[:16], *rest[16:])
        return body(xs, len_short, xl, len_long, *rest)

    return jax.shard_map(step, mesh=mesh, in_specs=in_specs, out_specs=out_specs, check_vma=False)
```

```python
import functools
import math

import jax
import jax.numpy as jnp
from jax import lax
from jax.experimental import pallas as pl
from jax.experimental.pallas import tpu as pltpu
from jax.sharding import PartitionSpec as P

MESH = pl.DeviceIdType.MESH

HD = 64
P_SIZE = 128


norm_epsilon = 1e-12
unit_epsilon = 1e-06
masked_fill = -1000000000.0


def layer_norm(residual, norm_gain, norm_shift):
    center = residual - jnp.mean(residual, axis=-1, keepdims=True)
    variance = jnp.mean(center * center, axis=-1, keepdims=True)
    return center * lax.rsqrt(variance + norm_epsilon) * norm_gain + norm_shift


def gelu_exact(pre_act):
    return 0.5 * pre_act * (1.0 + lax.erf(pre_act * (1.0 / math.sqrt(2.0))))


def normalize(embedding, token_mask):
    squares = jnp.sum(embedding * embedding, axis=-1, keepdims=True)
    return math.sqrt(P_SIZE) * embedding * lax.rsqrt(squares + unit_epsilon) * token_mask[..., None]


def soft_weights(scaled, key_mask):
    masked = jnp.where(key_mask, scaled, masked_fill)
    row_peak = jnp.max(masked, axis=-1, keepdims=True)
    exponent = jnp.exp(masked - row_peak)
    return exponent / jnp.sum(exponent, axis=-1, keepdims=True)


def matmul(left_side, right_side, form):
    return jnp.einsum(form, left_side, right_side, preferred_element_type=jnp.float32)


def forward(tokens, lengths, full_weights):
    (
        query_weight,
        key_weight,
        value_weight,
        out_weight,
        up_weight,
        down_weight,
        embed_weight,
        query_bias,
        value_bias,
        out_bias,
        attention_gain,
        attention_shift,
        up_bias,
        down_bias,
        final_gain,
        final_shift,
    ) = full_weights
    seq_count, length, model_width = tokens.shape
    head_count = model_width // HD
    score_scale = 1.0 / math.sqrt(HD)
    positions = jnp.arange(length, dtype=jnp.int32)
    token_mask = (positions[None, :] < lengths[:, None]).astype(jnp.float32)
    key_mask = token_mask[:, None, None, :] > 0.5
    query_low = (matmul(tokens, query_weight, "bld,de->ble") + query_bias).astype(jnp.bfloat16)
    query_low = query_low.reshape(seq_count, length, head_count, HD)
    key_low = matmul(tokens, key_weight, "bld,de->ble").astype(jnp.bfloat16)
    key_low = key_low.reshape(seq_count, length, head_count, HD)
    value_low = (matmul(tokens, value_weight, "bld,de->ble") + value_bias).astype(jnp.bfloat16)
    value_low = value_low.reshape(seq_count, length, head_count, HD)
    raw_scores = matmul(query_low, key_low, "bqhe,bkhe->bhqk") * score_scale
    attn_probs = soft_weights(raw_scores, key_mask)
    probs_low = attn_probs.astype(jnp.bfloat16)
    context_low = matmul(probs_low, value_low, "bhqk,bkhe->bqhe")
    context_low = context_low.reshape(seq_count, length, model_width).astype(jnp.bfloat16)
    attn_out = matmul(context_low, out_weight, "bld,de->ble") + out_bias
    resid_one = tokens.astype(jnp.float32) + attn_out
    normed_one = layer_norm(resid_one, attention_gain, attention_shift)
    hidden_low = normed_one.astype(jnp.bfloat16)
    pre_act = matmul(hidden_low, up_weight, "bld,df->blf") + up_bias
    act_low = gelu_exact(pre_act).astype(jnp.bfloat16)
    ffn_out = matmul(act_low, down_weight, "blf,fd->bld") + down_bias
    resid_two = normed_one + ffn_out
    final_low = layer_norm(resid_two, final_gain, final_shift).astype(jnp.bfloat16)
    embedding = matmul(final_low, embed_weight, "bld,dp->blp")
    result = normalize(embedding, token_mask)
    saved = (
        tokens,
        token_mask,
        query_low,
        key_low,
        value_low,
        attn_probs,
        probs_low,
        context_low,
        resid_one,
        hidden_low,
        pre_act,
        act_low,
        resid_two,
        final_low,
        embedding,
    )
    return (result, saved)


def backward(saved, full_weights, cotangent):
    (
        tokens,
        token_mask,
        query_low,
        key_low,
        value_low,
        attn_probs,
        probs_low,
        context_low,
        resid_one,
        hidden_low,
        pre_act,
        act_low,
        resid_two,
        final_low,
        embedding,
    ) = saved
    (
        query_weight,
        key_weight,
        value_weight,
        out_weight,
        up_weight,
        down_weight,
        embed_weight,
        query_bias,
        value_bias,
        out_bias,
        attention_gain,
        attention_shift,
        up_bias,
        down_bias,
        final_gain,
        final_shift,
    ) = full_weights
    seq_count, length, model_width = tokens.shape
    score_scale = 1.0 / math.sqrt(HD)
    _, pull_norm = jax.vjp(lambda vector: normalize(vector, token_mask), embedding)
    (embed_grad,) = pull_norm(cotangent.astype(jnp.float32))
    embed_low = embed_grad.astype(jnp.bfloat16)
    grad_embed = matmul(final_low, embed_low, "bld,blp->dp")
    final_grad = matmul(embed_low, embed_weight, "blp,dp->bld")
    _, pull_two = jax.vjp(
        layer_norm, resid_two, final_gain.astype(jnp.float32), final_shift.astype(jnp.float32)
    )
    resid_two_grad, grad_final_gain, grad_final_shift = pull_two(final_grad)
    ffn_low = resid_two_grad.astype(jnp.bfloat16)
    grad_down_bias = jnp.sum(ffn_low, axis=(0, 1), dtype=jnp.float32)
    grad_down = matmul(act_low, ffn_low, "blf,bld->fd")
    act_grad = matmul(ffn_low, down_weight, "bld,fd->blf")
    _, pull_gelu = jax.vjp(gelu_exact, pre_act)
    (pre_grad,) = pull_gelu(act_grad)
    pre_low = pre_grad.astype(jnp.bfloat16)
    grad_up_bias = jnp.sum(pre_low, axis=(0, 1), dtype=jnp.float32)
    grad_up = matmul(hidden_low, pre_low, "bld,blf->df")
    normed_grad = resid_two_grad + matmul(pre_low, up_weight, "blf,df->bld")
    _, pull_one = jax.vjp(
        layer_norm,
        resid_one,
        attention_gain.astype(jnp.float32),
        attention_shift.astype(jnp.float32),
    )
    resid_one_grad, grad_attention_gain, grad_attention_shift = pull_one(normed_grad)
    attn_low = resid_one_grad.astype(jnp.bfloat16)
    grad_out_bias = jnp.sum(attn_low, axis=(0, 1), dtype=jnp.float32)
    grad_out = matmul(context_low, attn_low, "bld,ble->de")
    context_grad = matmul(attn_low, out_weight, "ble,de->bld").astype(jnp.bfloat16)
    context_grad = context_grad.reshape(seq_count, length, -1, HD)
    value_grad = matmul(probs_low, context_grad, "bhqk,bqhe->bkhe")
    probs_grad = matmul(context_grad, value_low, "bqhe,bkhe->bhqk")
    score_low = attn_probs * (probs_grad - jnp.sum(probs_grad * attn_probs, axis=-1, keepdims=True))
    score_low = score_low.astype(jnp.bfloat16)
    query_grad = (matmul(score_low, key_low, "bhqk,bkhe->bqhe") * score_scale).astype(jnp.bfloat16)
    query_grad = query_grad.reshape(seq_count, length, model_width)
    key_grad = (matmul(score_low, query_low, "bhqk,bqhe->bkhe") * score_scale).astype(jnp.bfloat16)
    key_grad = key_grad.reshape(seq_count, length, model_width)
    value_grad_low = value_grad.astype(jnp.bfloat16).reshape(seq_count, length, model_width)
    grad_query_bias = jnp.sum(query_grad, axis=(0, 1), dtype=jnp.float32)
    grad_value_bias = jnp.sum(value_grad_low, axis=(0, 1), dtype=jnp.float32)
    grad_query = matmul(tokens, query_grad, "bld,ble->de")
    grad_key = matmul(tokens, key_grad, "bld,ble->de")
    grad_value = matmul(tokens, value_grad_low, "bld,ble->de")
    input_grad = (
        resid_one_grad
        + matmul(query_grad, query_weight, "ble,de->bld")
        + matmul(key_grad, key_weight, "ble,de->bld")
        + matmul(value_grad_low, value_weight, "ble,de->bld")
    )
    gradients = (
        grad_query,
        grad_key,
        grad_value,
        grad_out,
        grad_up,
        grad_down,
        grad_embed,
        grad_query_bias,
        grad_value_bias,
        grad_out_bias,
        grad_attention_gain,
        grad_attention_shift,
        grad_up_bias,
        grad_down_bias,
        grad_final_gain,
        grad_final_shift,
    )
    return (input_grad, gradients)


BOTH = ("wide", "narrow")
WIRE = ((48, 512), (48, 768), (48, 512), (48, 1536), (96, 768))
CUT = (256, 384, 256, 768, 384)
ROWS = 1792
SHORT = 512
COPIES = 39


def place():
    wide = lax.axis_index("wide")
    return wide // 4, (wide // 2) % 2, wide % 2, lax.axis_index("narrow")


def greet(z, y, c, x):
    partners = [device((z + d) % 4, y, c, x) for d in (1, 2, 3)]
    partners += [device(z, 1 - y, c, x), device(z, y, 1 - c, x), device(z, y, c, 1 - x)]
    barrier = pltpu.get_barrier_semaphore()
    for partner in partners:
        pl.semaphore_signal(barrier, inc=1, device_id=partner, device_id_type=MESH)
    pl.semaphore_wait(barrier, len(partners))


def device(z, y, c, x):
    return (z * 4 + y * 2 + c, x)


class Lazy:
    def __init__(self, make):
        self.make = make

    def __getitem__(self, way):
        return self.make(way)


class Gather:
    def __init__(self, held, cut, send, recv, first):
        self.held, self.cut, self.send, self.recv, self.first = held, cut, send, recv, first
        self.z, self.y, self.c, self.x = place()

    def view(self, block, half):
        if half is None:
            return self.held.at[block]
        lanes = self.held.shape[-1]
        low, size = ((0, self.cut), (self.cut, lanes - self.cut))[half]
        return self.held.at[(*block, slice(None), pl.ds(low, size))]

    def plan(self, slot, out, into, half, target):
        def copy(block):
            return pltpu.make_async_remote_copy(
                src_ref=self.view(block, half),
                dst_ref=self.view(block, half),
                send_sem=self.send.at[self.first + slot],
                recv_sem=self.recv.at[self.first + slot],
                device_id=target,
                device_id_type=MESH,
            )

        return Lazy(lambda way: copy((out, into)[way]))

    def along_z(self, d):
        z, y, c, x = self.z, self.y, self.c, self.x
        return self.plan(d - 1, (z, y, c, x), ((z + 4 - d) % 4, y, c, x), None, device((z + d) % 4, y, c, x))

    def to_x(self, d):
        z, y, c, x = (self.z + 4 - d) % 4, self.y, self.c, self.x
        return self.plan(3 + d, (z, y, c, x), (z, y, c, 1 - x), None, device(self.z, y, c, 1 - x))

    def to_y(self, d):
        z, y, c, x = (self.z + 4 - d) % 4, self.y, self.c, self.x
        return self.plan(7 + d, (z, y, c, x), (z, 1 - y, c, x), None, device(self.z, 1 - y, c, x))

    def corner(self, d, half):
        z, y, c, x = (self.z + 4 - d) % 4, self.y, self.c, self.x
        if half == 0:
            return self.plan(11 + d, (z, y, c, 1 - x), (z, 1 - y, c, 1 - x), 0, device(self.z, 1 - y, c, x))
        return self.plan(15 + d, (z, 1 - y, c, x), (z, 1 - y, c, 1 - x), 1, device(self.z, y, c, 1 - x))

    def to_core(self, d, kind):
        z, c = (self.z + 4 - d) % 4, self.c
        y = 1 - self.y if kind >= 2 else self.y
        x = 1 - self.x if kind in (1, 3, 4) else self.x
        half = kind - 3 if kind >= 3 else None
        return self.plan(19 + 4 * kind + d, (z, y, c, x), (z, y, 1 - c, x), half, device(self.z, self.y, 1 - c, self.x))

    def start_z(self):
        for d in (1, 2, 3):
            self.along_z(d)[0].start()

    def spread(self, d):
        self.to_x(d)[0].start()
        self.to_y(d)[0].start()
        self.to_core(d, 0)[0].start()

    def column(self, d):
        self.along_z(d)[1].wait_recv()
        self.spread(d)

    def turn(self, d):
        self.to_x(d)[1].wait_recv()
        self.corner(d, 0)[0].start()
        self.to_core(d, 1)[0].start()
        self.to_y(d)[1].wait_recv()
        self.corner(d, 1)[0].start()
        self.to_core(d, 2)[0].start()

    def finish(self, d):
        for half in (0, 1):
            self.corner(d, half)[1].wait_recv()
            self.to_core(d, 3 + half)[0].start()

    def arrive(self):
        for d in range(4):
            for kind in range(5):
                self.to_core(d, kind)[1].wait_recv()

    def drain(self):
        for d in range(4):
            if d:
                self.along_z(d)[0].wait_send()
            self.to_x(d)[0].wait_send()
            self.to_y(d)[0].wait_send()
            for half in (0, 1):
                self.corner(d, half)[0].wait_send()
            for kind in range(5):
                self.to_core(d, kind)[0].wait_send()


def stack_halves(whole):
    half = whole.shape[1] // 2
    return jnp.concatenate([whole[:, :half], whole[:, half:]], axis=0).astype(jnp.bfloat16)


def unpack_rows(held, targets):
    def pair(p, carry):
        z, y, c = p // 4, (p // 2) % 2, p % 2
        one, two = held[z, y, c, 0].astype(jnp.float32), held[z, y, c, 1].astype(jnp.float32)
        for side, low, ref, column, lanes in targets:
            rows = slice(24 * side, 24 * side + 24)
            both = jnp.concatenate([one[rows, low : low + lanes], two[rows, low : low + lanes]], axis=0)
            ref[pl.ds(pl.multiple_of(p * 48, 48), 48), column : column + lanes] = both.astype(jnp.bfloat16)
        return carry

    lax.fori_loop(0, 16, pair, 0)


NN = (((1,), (0,)), ((), ()))
NT = (((1,), (1,)), ((), ()))
TN = (((0,), (0,)), ((), ()))


def dot(left, right, dims):
    return lax.dot_general(left, right, dims, preferred_element_type=jnp.float32)


class Steps:
    def __init__(self, steps):
        self.steps = list(steps)

    def run(self, count=1):
        for _ in range(count):
            if self.steps:
                self.steps.pop(0)()

    def rest(self):
        self.run(len(self.steps))


def attend(qkv, context, probs, row, length, valid, first, last):
    rows = pl.ds(row, length)
    fill = jnp.where(lax.broadcasted_iota(jnp.int32, (1, length), 1) < valid, 0.0, masked_fill)
    lane = lax.broadcasted_iota(jnp.int32, (length, 128), 1)

    def pair(p, carry):
        at = lambda base: pl.ds(pl.multiple_of(base + p * 128, 128), 128)
        query = qkv[rows, at(0)] * jnp.bfloat16(1.0 / math.sqrt(HD))
        key, value = qkv[rows, at(768)], qkv[rows, at(1536)]
        total = None
        for h in (0, 1):
            here = (lane < 64) if h == 0 else (lane >= 64)
            scores = dot(query, jnp.where(here, key, jnp.bfloat16(0)), NT) + fill
            peak = jnp.max(scores, axis=1, keepdims=True)
            exponent = jnp.exp(scores - peak)
            scale = 1.0 / jnp.sum(exponent, axis=1, keepdims=True)
            low = (exponent * scale).astype(jnp.bfloat16)
            probs[2 * p + h] = low
            part = dot(low, jnp.where(here, value, jnp.bfloat16(0)), NN)
            total = part if total is None else total + part
        context[rows, at(0)] = total.astype(jnp.bfloat16)
        return carry

    lax.fori_loop(first, last, pair, 0)


def spread_table(group, lanes):
    lane = lax.broadcasted_iota(jnp.int32, (128, lanes), 1).astype(jnp.float32)
    row = lax.broadcasted_iota(jnp.int32, (128, lanes), 0).astype(jnp.float32)
    return (lane - group * jnp.floor((lane + 0.5) * (1.0 / group)) == row).astype(jnp.bfloat16)


def natural_vectors(held, vec_out):
    blocks = [held[p // 8, (p // 4) % 2, (p // 2) % 2, p % 2, :16, 384:512] for p in range(32)]
    stacked = jnp.concatenate(blocks, axis=0)
    wide = dot(stacked, spread_table(24, 768), NN)
    lane = lax.broadcasted_iota(jnp.int32, (512, 768), 1)
    start = (lax.broadcasted_iota(jnp.int32, (512, 768), 0) >> 4) * 24
    wide = jnp.where((lane >= start) & (lane < start + 24), wide, 0.0)
    vec_out[:, :768] = jnp.sum(wide.reshape(32, 16, 768), axis=0)
    picked = dot(
        (lax.broadcasted_iota(jnp.int32, (32, 512), 1) == lax.broadcasted_iota(jnp.int32, (32, 512), 0) * 16 + 5).astype(jnp.bfloat16),
        stacked,
        NN,
    ).astype(jnp.bfloat16)
    wide = dot(picked, spread_table(96, 3072), NN)
    lane = lax.broadcasted_iota(jnp.int32, (32, 3072), 1)
    start = lax.broadcasted_iota(jnp.int32, (32, 3072), 0) * 96
    wide = jnp.where((lane >= start) & (lane < start + 96), wide, 0.0)
    vec_out[9:10, :] = jnp.sum(wide, axis=0, keepdims=True)


def first_kernel(
    len_short, len_long, xs, xl, cs, cl, q_ref, k_ref, v_ref, o_ref, u_ref, d_ref, e_ref, *rest
):
    vec_refs, rest = rest[:9], rest[9:]
    (qkv_out, out_out, up_out, embed_out, down_out, vec_out, proj_out, context_out, ps_out, pl_out, x_out, c_out), rest = rest[:12], rest[12:]
    h0, h1, h2, h3, h4, w_qkv, w_out, w_up, w_embed, proj, context, ps, pls, rows, send, recv, away = rest
    z, y, c, x = place()
    rows[...] = jnp.zeros_like(rows)
    for i, ref in enumerate(vec_refs):
        width = ref.shape[0]
        rows[i : i + 1, :width] = ref[...].astype(jnp.float32).reshape(1, width)
    wide = lambda ref: ref[...].astype(jnp.float32)
    h0[z, y, c, x, :, :384] = stack_halves(wide(q_ref))
    h0[z, y, c, x, :, 384:] = rows[...].astype(jnp.bfloat16)
    h1[z, y, c, x, :, :384] = stack_halves(wide(k_ref))
    h1[z, y, c, x, :, 384:] = stack_halves(wide(v_ref))
    h2[z, y, c, x, :, :384] = stack_halves(wide(o_ref))
    h2[z, y, c, x, :, 384:] = jnp.concatenate([wide(e_ref), wide(e_ref)], axis=0).astype(jnp.bfloat16)
    h3[z, y, c, x] = stack_halves(wide(u_ref))
    h4[z, y, c, x] = d_ref[...]
    greet(z, y, c, x)
    one, two, three, four, five = gathers = [Gather(h, CUT[i], send, recv, COPIES * i) for i, h in enumerate((h0, h1, h2, h3, h4))]
    for piece in gathers:
        piece.start_z()
    for piece in gathers:
        piece.spread(0)
    kept = []

    def keep(source, target):
        copy = pltpu.make_async_copy(source, target, away.at[len(kept)])
        copy.start()
        kept.append(copy)

    for source, target, low in ((xs, x_out, 0), (xl, x_out, SHORT), (cs, c_out, 0), (cl, c_out, SHORT)):
        keep(source, target.at[pl.ds(low, source.shape[0])])
    for d in (1, 2, 3):
        one.column(d)
    for d in (1, 2, 3):
        two.column(d)
    for d in range(4):
        one.turn(d)
    for d in (1, 2, 3):
        three.column(d)
    for d in range(4):
        two.turn(d)
    for d in range(4):
        one.finish(d)
    for d in (1, 2, 3):
        four.column(d)
    one.arrive()
    unpack_rows(h0, [(0, 0, w_qkv, 0, 384), (1, 0, w_qkv, 384, 384)])
    natural_vectors(h0, vec_out)
    for d in range(4):
        two.finish(d)
    steps = Steps(
        [functools.partial(three.turn, d) for d in range(4)]
        + [functools.partial(five.column, d) for d in (1, 2, 3)]
        + [functools.partial(three.finish, d) for d in range(4)]
        + [functools.partial(four.turn, d) for d in range(4)]
        + [functools.partial(four.finish, d) for d in range(4)]
        + [functools.partial(five.turn, d) for d in range(4)]
        + [functools.partial(five.finish, d) for d in range(4)]
    )
    tiles = [(0, xs[...])] + [(SHORT + 320 * s, xl[320 * s : 320 * s + 320]) for s in range(4)]
    for part in range(3):
        if part == 1:
            two.arrive()
            unpack_rows(h1, [(0, 0, w_qkv, 768, 384), (1, 0, w_qkv, 1152, 384), (0, 384, w_qkv, 1536, 384), (1, 384, w_qkv, 1920, 384)])
            keep(w_qkv, qkv_out)
        lanes = slice(768 * part, 768 * part + 768)
        for row, tokens in tiles:
            result = dot(tokens, w_qkv[:, lanes], NN)
            if part != 1:
                result = result + vec_out[part // 2 : part // 2 + 1, :768]
            proj[row : row + tokens.shape[0], lanes] = result.astype(jnp.bfloat16)
        steps.run(2 if part == 0 else 3)
    keep(proj, proj_out)
    for s in range(4):
        attend(proj, context, ps.at[s], 128 * s, 128, len_short[s], 0, 6)
        steps.run(1)
    keep(ps, ps_out)
    slots = []
    for s in range(4):
        if s >= 2:
            slots[s - 2].wait()
        for part in (0, 3):
            attend(proj, context, pls.at[s % 2], SHORT + 320 * s, 320, len_long[s], part, part + 3)
            steps.run(2)
        copy = pltpu.make_async_copy(pls.at[s % 2], pl_out.at[s], away.at[12 + s])
        copy.start()
        slots.append(copy)
        if s == 1:
            three.arrive()
            unpack_rows(h2, [(0, 0, w_out, 0, 384), (1, 0, w_out, 384, 384), (0, 384, w_embed, 0, 128)])
            keep(w_out, out_out)
            keep(w_embed, embed_out)
    keep(context, context_out)
    steps.rest()
    four.arrive()
    unpack_rows(h3, [(0, 0, w_up, 0, 1536), (1, 0, w_up, 1536, 1536)])
    keep(w_up, up_out)
    five.arrive()
    keep(h4, down_out)
    for copy in kept + slots[2:]:
        copy.wait()
    for piece in gathers:
        piece.drain()


def first(len_short, len_long, xs, xl, cs, cl, shards):
    vmem, smem, anywhere = (pl.BlockSpec(memory_space=m) for m in (pltpu.VMEM, pltpu.SMEM, pl.ANY))
    low = lambda *dims: jax.ShapeDtypeStruct(dims, jnp.bfloat16)
    held = lambda *dims: pltpu.VMEM(dims, jnp.bfloat16)
    semaphores = lambda count: pltpu.SemaphoreType.DMA((count,))
    weights = [(768, 2304), (768, 768), (768, 3072), (768, 128)]
    return pl.pallas_call(
        first_kernel,
        out_shape=(
            *[low(*dims) for dims in weights], low(4, 2, 2, 2, *WIRE[4]),
            jax.ShapeDtypeStruct((16, 3072), jnp.float32),
            low(ROWS, 2304), low(ROWS, 768), low(4, 12, 128, 128), low(4, 12, 320, 320), low(ROWS, 768), low(ROWS, P_SIZE),
        ),
        in_specs=[smem] * 2 + [vmem] * 2 + [anywhere] * 2 + [vmem] * 16,
        out_specs=(anywhere,) * 5 + (vmem,) + (anywhere,) * 6,
        scratch_shapes=[held(4, 2, 2, 2, *dims) for dims in WIRE]
        + [held(*dims) for dims in weights]
        + [held(ROWS, 2304), held(ROWS, 768), held(4, 12, 128, 128), held(2, 12, 320, 320), pltpu.VMEM((48, 128), jnp.float32)]
        + [semaphores(COPIES * 5), semaphores(COPIES * 5), semaphores(16)],
        compiler_params=pltpu.CompilerParams(collective_id=0, has_side_effects=True, vmem_limit_bytes=62 * 2**20),
    )(len_short, len_long, xs, xl, cs, cl, *shards)


TILE = 448
PART = 224


def center(value):
    return value - jnp.mean(value, axis=1, keepdims=True)


def normal(value):
    value = center(value)
    scale = lax.rsqrt(jnp.mean(value * value, axis=1, keepdims=True) + norm_epsilon)
    return value * scale, scale


def normal_back(grad, unit, scale):
    inner = jnp.mean(grad * unit, axis=1, keepdims=True)
    return scale * (center(grad) - unit * inner)


def embed_copies(step, embedded, es_out, el_out, away):
    low, high = TILE * step, TILE * step + TILE
    cut = min(max(SHORT, low), high)
    copies = []
    if low < cut:
        copies.append((embedded.at[pl.ds(0, cut - low)], es_out.at[pl.ds(low, cut - low)]))
    if cut < high:
        copies.append((embedded.at[pl.ds(cut - low, high - cut)], el_out.at[pl.ds(cut - SHORT, high - cut)]))
    return [pltpu.make_async_copy(source, target, away.at[i]) for i, (source, target) in enumerate(copies)]


def token_kernel(
    len_short, len_long, x_ref, cot_ref, ctx_ref, w_out, w_up, w_down, w_embed, vec,
    es_out, el_out, act_out, pre_out, hidden_out, ffn_out, attn_out, final_out, eg_out, resid_out, cg_out, sums,
    slope, embedded, away,
):
    tile = pl.program_id(0)
    row = lambda k: vec[k : k + 1, :768]
    low = lambda value: value.astype(jnp.bfloat16)
    wide = lambda value: value.astype(jnp.float32)

    @pl.when(tile == 0)
    def _():
        sums[...] = jnp.zeros_like(sums)

    def add(k, value):
        sums[k : k + 1, : value.shape[1]] += jnp.sum(value, axis=0, keepdims=True)

    def chain(start):
        rows = slice(start, start + PART)
        mixed = wide(x_ref[rows]) + (dot(ctx_ref[rows], w_out[...], NN) + row(2))
        yield
        unit_one, scale_one = normal(mixed)
        normed_one = unit_one * row(3) + row(4)
        hidden = low(normed_one)
        hidden_out[rows] = hidden
        ffn = None
        for f in range(4):
            lanes = slice(768 * f, 768 * f + 768)
            pre = dot(hidden, w_up[:, lanes], NN) + vec[9:10, lanes]
            cdf = 0.5 + 0.5 * lax.erf(pre * (1.0 / math.sqrt(2.0)))
            act = low(pre * cdf)
            act_out[rows, lanes] = act
            slope[rows, lanes] = cdf + pre * (jnp.exp(-0.5 * pre * pre) * (1.0 / math.sqrt(2.0 * math.pi)))
            part = dot(act, w_down[lanes, :], NN)
            ffn = part if ffn is None else ffn + part
        yield
        unit_two, scale_two = normal(normed_one + (ffn + row(6)))
        final = low(unit_two * row(7) + row(8))
        final_out[rows] = final
        embedding = dot(final, w_embed[...], NN)
        inverse = lax.rsqrt(jnp.sum(embedding * embedding, axis=1, keepdims=True) + unit_epsilon)
        at = lax.broadcasted_iota(jnp.int32, (PART, 1), 0) + (tile * TILE + start)
        mask = jnp.zeros((PART, 1), jnp.float32)
        for sizes, low_row, stride in ((len_short, 0, 128), (len_long, SHORT, 320)):
            for s in range(4):
                begin = low_row + s * stride
                mask = mask + jnp.where((at >= begin) & (at < begin + sizes[s]), 1.0, 0.0)
        embedded[rows] = math.sqrt(P_SIZE) * embedding * inverse * mask
        grad = wide(cot_ref[rows]) * mask
        inner = jnp.sum(grad * embedding, axis=1, keepdims=True)
        embed_grad = low(math.sqrt(P_SIZE) * inverse * (grad - inverse * inverse * embedding * inner))
        eg_out[rows] = embed_grad
        final_grad = dot(embed_grad, w_embed[...], NT)
        yield
        add(7, final_grad * unit_two)
        add(8, final_grad)
        resid_two = normal_back(final_grad * row(7), unit_two, scale_two)
        ffn_grad = low(resid_two)
        ffn_out[rows] = ffn_grad
        add(6, wide(ffn_grad))
        normed_grad = resid_two
        for f in range(4):
            lanes = slice(768 * f, 768 * f + 768)
            pre_grad = low(dot(ffn_grad, w_down[lanes, :], NT) * slope[rows, lanes])
            pre_out[rows, lanes] = pre_grad
            sums[9:10, lanes] += jnp.sum(wide(pre_grad), axis=0, keepdims=True)
            normed_grad = normed_grad + dot(pre_grad, w_up[:, lanes], NT)
        yield
        add(3, normed_grad * unit_one)
        add(4, normed_grad)
        resid_one = normal_back(normed_grad * row(3), unit_one, scale_one)
        resid_out[rows] = resid_one
        attn_grad = low(resid_one)
        attn_out[rows] = attn_grad
        add(2, wide(attn_grad))
        cg_out[rows] = low(dot(attn_grad, w_out[...], NT))
        yield

    chains = [chain(start) for start in range(0, TILE, PART)]
    for _ in range(5):
        for one in chains:
            next(one)

    def embeds(act):
        for step in range(ROWS // TILE):

            @pl.when(tile == step)
            def _():
                for copy in embed_copies(step, embedded, es_out, el_out, away):
                    getattr(copy, act)()

    embeds("start")
    embeds("wait")


def token_chain(len_short, len_long, x, cot, context, w_out, w_up, w_down, w_embed, vec):
    smem, anywhere = pl.BlockSpec(memory_space=pltpu.SMEM), pl.BlockSpec(memory_space=pl.ANY)
    every = lambda lanes: pl.BlockSpec((TILE, lanes), lambda i: (i, 0))
    whole = lambda array: pl.BlockSpec(array.shape, lambda i: (0, 0), pipeline_mode=pl.Buffered(1))
    shape = lambda kind, *dims: jax.ShapeDtypeStruct(dims, kind)
    low = lambda lanes: shape(jnp.bfloat16, ROWS, lanes)
    return pl.pallas_call(
        token_kernel,
        grid=(ROWS // TILE,),
        out_shape=(
            shape(jnp.float32, SHORT, P_SIZE), shape(jnp.float32, ROWS - SHORT, P_SIZE),
            low(3072), low(3072), low(768), low(768), low(768), low(768), low(P_SIZE),
            shape(jnp.float32, ROWS, 768), low(768), shape(jnp.float32, 16, 3072),
        ),
        in_specs=[smem, smem, every(768), every(P_SIZE), every(768)] + [whole(one) for one in (w_out, w_up, w_down, w_embed, vec)],
        out_specs=(
            anywhere, anywhere, every(3072), every(3072), every(768), every(768), every(768), every(768), every(P_SIZE),
            every(768), every(768), pl.BlockSpec((16, 3072), lambda i: (0, 0)),
        ),
        scratch_shapes=[pltpu.VMEM((TILE, 3072), jnp.float32), pltpu.VMEM((TILE, P_SIZE), jnp.float32), pltpu.SemaphoreType.DMA((2,))],
        compiler_params=pltpu.CompilerParams(vmem_limit_bytes=62 * 2**20),
    )(len_short, len_long, x, cot, context, w_out, w_up, w_down, w_embed, vec)


class Scatter:
    def __init__(self, mine, cut, work, send, recv, local, number):
        self.mine, self.cut, self.send, self.recv, self.first = mine, cut, send, recv, SUMS * number
        self.core_in, self.total, self.corner_y, self.corner_x, self.from_x, self.from_y, self.from_z = work
        self.z, self.y, self.c, self.x = place()
        self.own = pltpu.make_async_copy(mine.at[:, :, self.c], self.total, local.at[number])

    def copy(self, slot, source, target, partner):
        return pltpu.make_async_remote_copy(
            src_ref=source,
            dst_ref=target,
            send_sem=self.send.at[self.first + slot],
            recv_sem=self.recv.at[self.first + slot],
            device_id=partner,
            device_id_type=MESH,
        )

    def spot(self, kind):
        return (1 - self.y if kind in (0, 2) else self.y), (1 - self.x if kind in (0, 1) else self.x)

    def core(self, kind):
        y, x = self.spot(kind)
        return self.copy(
            kind,
            self.mine.at[:, y, 1 - self.c, x],
            self.core_in.at[:, y, x],
            device(self.z, self.y, 1 - self.c, self.x),
        )

    def corner(self, d, half):
        z = (self.z + d) % 4
        y, x = self.spot(0)
        low, size = ((0, self.cut), (self.cut, self.total.shape[-1] - self.cut))[half]
        source = self.total.at[z, y, x, :, pl.ds(low, size)]
        if half == 0:
            return self.copy(4 + d, source, self.corner_y.at[z], device(self.z, 1 - self.y, self.c, self.x))
        return self.copy(8 + d, source, self.corner_x.at[z], device(self.z, self.y, self.c, 1 - self.x))

    def to_x(self, d):
        z = (self.z + d) % 4
        return self.copy(12 + d, self.total.at[z, self.y, 1 - self.x], self.from_x.at[z], device(self.z, self.y, self.c, 1 - self.x))

    def to_y(self, d):
        z = (self.z + d) % 4
        return self.copy(16 + d, self.total.at[z, 1 - self.y, self.x], self.from_y.at[z], device(self.z, 1 - self.y, self.c, self.x))

    def along_z(self, d):
        z = (self.z + d) % 4
        return self.copy(19 + d, self.total.at[z, self.y, self.x], self.from_z.at[d - 1], device(z, self.y, self.c, self.x))

    def start(self):
        self.own.start()
        for kind in range(4):
            self.core(kind).start()

    def merge(self, kind):
        if kind == 0:
            self.own.wait()
        self.core(kind).wait_recv()
        y, x = self.spot(kind)

        def add(z, carry):
            here = self.total[z, y, x].astype(jnp.float32)
            self.total[z, y, x] = (here + self.core_in[z, y, x].astype(jnp.float32)).astype(jnp.bfloat16)
            return carry

        lax.fori_loop(0, 4, add, 0)
        if kind == 0:
            for d in (1, 2, 3, 0):
                self.corner(d, 0).start()
                self.corner(d, 1).start()

    def bend(self, d):
        z = (self.z + d) % 4
        self.corner(d, 0).wait_recv()
        here = self.total[z, self.y, 1 - self.x, :, : self.cut].astype(jnp.float32)
        self.total[z, self.y, 1 - self.x, :, : self.cut] = (here + self.corner_y[z].astype(jnp.float32)).astype(jnp.bfloat16)
        self.to_x(d).start()
        self.corner(d, 1).wait_recv()
        here = self.total[z, 1 - self.y, self.x, :, self.cut :].astype(jnp.float32)
        self.total[z, 1 - self.y, self.x, :, self.cut :] = (here + self.corner_x[z].astype(jnp.float32)).astype(jnp.bfloat16)
        self.to_y(d).start()

    def close(self, d):
        z = (self.z + d) % 4
        self.to_x(d).wait_recv()
        self.to_y(d).wait_recv()
        here = self.total[z, self.y, self.x].astype(jnp.float32) + self.from_x[z].astype(jnp.float32)
        self.total[z, self.y, self.x] = (here + self.from_y[z].astype(jnp.float32)).astype(jnp.bfloat16)
        if d:
            self.along_z(d).start()

    def result(self, store):
        total = self.total[self.z, self.y, self.x].astype(jnp.float32)
        for d in (1, 2, 3):
            self.along_z(d).wait_recv()
            total = total + self.from_z[d - 1].astype(jnp.float32)
        store[...] = total

    def drain(self):
        for kind in range(4):
            self.core(kind).wait_send()
        for d in range(4):
            self.corner(d, 0).wait_send()
            self.corner(d, 1).wait_send()
            self.to_x(d).wait_send()
            self.to_y(d).wait_send()
            if d:
                self.along_z(d).wait_send()


SUMS = 23
BACK = ((96, 768), (48, 1536), (48, 512), (48, 384), (48, 384), (48, 512))
BACK_CUT = (384, 768, 256, 128, 128, 256)


def work_shapes(rows, lanes, cut):
    held = lambda *dims: pltpu.VMEM((*dims, rows, lanes), jnp.bfloat16)
    part = lambda size: pltpu.VMEM((4, rows, size), jnp.bfloat16)
    return [held(4, 2, 2), held(4, 2, 2), part(cut), part(lanes - cut), held(4), held(4), held(3)]


def attend_back(proj, grads_in, probs, grads, vectors, row, length, group):
    rows = pl.ds(row, length)
    lane = lax.broadcasted_iota(jnp.int32, (length, 128), 1)
    score_scale = 1.0 / math.sqrt(HD)

    def pair(p):
        at = lambda base: pl.ds(base + p * 128, 128)
        query, key, value = (proj[:length, at(base)] for base in (0, 256, 512))
        context_grad = grads_in[:length, at(0)]
        query_grad, key_grads, value_grads = None, [], []
        for h in (0, 1):
            here = (lane < 64) if h == 0 else (lane >= 64)
            low = probs[2 * p + h, :length, :length]
            weight = low.astype(jnp.float32)
            weight_grad = dot(context_grad, jnp.where(here, value, jnp.bfloat16(0)), NT)
            inner = jnp.sum(weight_grad * weight, axis=1, keepdims=True)
            score_grad = (weight * (weight_grad - inner)).astype(jnp.bfloat16)
            part = dot(score_grad, jnp.where(here, key, jnp.bfloat16(0)), NN)
            query_grad = part if query_grad is None else query_grad + part
            key_grads.append(dot(score_grad, query, TN))
            value_grads.append(dot(low, context_grad, TN))
        query_low = (query_grad * score_scale).astype(jnp.bfloat16)
        key_low = (jnp.where(lane < 64, *key_grads) * score_scale).astype(jnp.bfloat16)
        value_low = jnp.where(lane < 64, *value_grads).astype(jnp.bfloat16)
        grads[rows, at(768 * group)] = query_low
        grads[rows, at(768 * group + 256)] = key_low
        grads[rows, at(768 * group + 512)] = value_low
        vectors[0:1, at(256 * group)] += jnp.sum(query_low.astype(jnp.float32), axis=0, keepdims=True)
        vectors[1:2, at(256 * group)] += jnp.sum(value_low.astype(jnp.float32), axis=0, keepdims=True)

    for p in range(2):
        pair(p)


def vectors_on_wire(vectors, out, low):
    lane = lax.broadcasted_iota(jnp.int32, (512, 768), 1)
    start = (lax.broadcasted_iota(jnp.int32, (512, 768), 0) >> 4) * 24
    wide = jnp.broadcast_to(vectors[:, :768][None], (32, 16, 768)).reshape(512, 768)
    wide = jnp.where((lane >= start) & (lane < start + 24), wide, 0.0).astype(jnp.bfloat16)
    rows = dot(wide, spread_table(24, 768), NT).reshape(32, 16, 128)
    lane = lax.broadcasted_iota(jnp.int32, (32, 3072), 1)
    start = lax.broadcasted_iota(jnp.int32, (32, 3072), 0) * 96
    wide = jnp.where((lane >= start) & (lane < start + 96), vectors[9:10, :], 0.0).astype(jnp.bfloat16)
    up_rows = dot(wide, spread_table(96, 3072), NT)
    number = lax.broadcasted_iota(jnp.int32, (32, 16, 128), 1)
    rows = jnp.where(number == 5, up_rows[:, None, :], rows).astype(jnp.bfloat16)
    for i in range(32):
        out[i // 8, (i // 4) % 2, (i // 2) % 2, i % 2, :16, low : low + 128] = rows[i]
        out[i // 8, (i // 4) % 2, (i // 2) % 2, i % 2, 16:, low : low + 128] = jnp.zeros((32, 128), jnp.bfloat16)


def wire_blocks(total, out, left=0, right=384, lanes=384, low=0):
    for i in range(32):
        rows = slice(24 * i, 24 * i + 24)
        both = jnp.concatenate([total[rows, left : left + lanes], total[rows, right : right + lanes]], axis=0)
        out[i // 8, (i // 4) % 2, (i // 2) % 2, i % 2, :, low : low + lanes] = both.astype(jnp.bfloat16)


def last_kernel(*refs):
    act, pre, hidden, ffn, attn, final, embed_grad, context, proj, context_grad, ps, pls, w_qkv_in = refs[:13]
    sums, x_in = refs[13:15]
    part_out, d_out, u_out, o_out, g0_out, g1_out, g2_out, p_down, p_up, p_out = refs[15:25]
    stage, p_first, p_second, p_third, slot_proj, slot_grad, slot_pl, grads, w_qkv, total, vectors, token_part, eg_held, x_ref = refs[25:39]
    work, (send, recv, local, load, fetch, away) = refs[39 : 39 + 7 * len(BACK)], refs[39 + 7 * len(BACK) :]
    greet(*place())
    groups = (p_first, p_second, p_third)
    mine = (p_down, p_up, p_out, *groups)
    down, up, out, *heads = pieces = [
        Scatter(one, BACK_CUT[i], work[7 * i : 7 * i + 7], send, recv, local, i) for i, one in enumerate(mine)
    ]
    merges, bends, closes = ([[functools.partial(getattr(one, name), d) for d in range(4)] for one in pieces] for name in ("merge", "bend", "close"))
    bends, closes = ([[rows[d] for d in (1, 2, 3, 0)] for rows in kind] for kind in (bends, closes))
    stores = (d_out, u_out, o_out, g0_out, g1_out, g2_out)
    ends = [functools.partial(one.result, store) for one, store in zip(pieces, stores)]

    s0, s1, s2, s3 = [grads.at[:, pl.ds(768 * i, 768)] for i in range(3)] + [token_part]
    halves = lambda j, slot: [
        (pre.at[:, pl.ds(384 * j, 384)], slot.at[:, pl.ds(0, 384)]),
        (pre.at[:, pl.ds(1536 + 384 * j, 384)], slot.at[:, pl.ds(384, 384)]),
    ]
    acts = lambda j, slot: [(act.at[:, pl.ds(768 * j, 768)], slot)]
    started, carried = [], []

    def bring(pairs):
        copies = []
        for source, target in pairs:
            copies.append(pltpu.make_async_copy(source, target, fetch.at[len(started)]))
            copies[-1].start()
            started.append(copies[-1])
        return copies

    def have(copies):
        for copy in copies:
            copy.wait()

    def carry(source, target):
        copy = pltpu.make_async_copy(source, target, away.at[len(carried)])
        copy.start()
        carried.append(copy)
        return copy

    ffn_here, here = bring([(ffn, s0)]), {}
    for j, slot in enumerate((s1, s2, s3)):
        here["act", j] = bring(acts(j, slot))
    eg_here = bring([(embed_grad, eg_held)])
    lanes = [(w_qkv_in.at[:, pl.ds(768 * p + 256 * g, 256)], w_qkv.at[:, pl.ds(768 * g + 256 * p, 256)]) for g in range(3) for p in range(3)]
    vectors[...] = sums[...]
    have(ffn_here)
    sent = {}
    for j, slot in enumerate((s1, s2, s3, s1)):
        have(here["act", j])
        low = dot(slot[...], s0[...], TN).astype(jnp.bfloat16)
        if j >= 2:
            sent[j - 2].wait()
        stage[j % 2] = low.reshape(2, 2, 2, 96, 768)
        sent[j] = carry(stage.at[j % 2], p_down.at[j])
        if j == 0:
            here["act", 3] = bring(acts(3, s1))
        elif j == 1:
            hidden_here = bring([(hidden, s2)])
        elif j == 2:
            here["pre", 0] = bring(halves(0, s3))
    here["pre", 1] = bring(halves(1, s0))
    here["pre", 2] = bring(halves(2, s1))
    sent[2].wait()
    sent[3].wait()
    down.start()
    have(hidden_here)
    hooks = iter([merges[0][:1], merges[0][1:], bends[0][:1], bends[0][1:2]])
    for j, slot in enumerate((s3, s0, s1, s3)):
        have(here["pre", j])
        total[...] = dot(s2[...], slot[...], TN)
        held = groups[j % 2]
        if j >= 2:
            sent[j + 2].wait()
        wire_blocks(total, held)
        sent[4 + j] = carry(held.at[:, :, :, :, :, pl.ds(0, 384)], p_up.at[:, :, :, :, :, pl.ds(384 * j, 384)])
        if j == 0:
            here["pre", 3] = bring(halves(3, s3))
        elif j == 1:
            context_here = bring([(context, s0)])
        elif j == 2:
            attn_here = bring([(attn, s1)])
        for step in next(hooks):
            step()
    final_here = bring([(final, s2)])
    x_here = bring([(x_in, x_ref)])
    weights_here = bring(lanes)
    sent[6].wait()
    sent[7].wait()
    up.start()
    order = [(SHORT + 320 * s, 320, s) for s in range(4)] + [(128 * s, 128, s) for s in range(4)]
    order = [(g, *one) for g in range(3) for one in order]

    def loads(n):
        group, row, length, s = order[n]
        slot = n % 2
        rows = pl.ds(row, length)
        copies = [
            (proj.at[rows, pl.ds(768 * p + 256 * group, 256)], slot_proj.at[slot, pl.ds(0, length), pl.ds(256 * p, 256)]) for p in range(3)
        ]
        copies.append((context_grad.at[rows, pl.ds(256 * group, 256)], slot_grad.at[slot, pl.ds(0, length)]))
        source = pls if length == 320 else ps
        copies.append((source.at[s, pl.ds(4 * group, 4)], slot_pl.at[slot, :, pl.ds(0, length), pl.ds(0, length)]))
        return [pltpu.make_async_copy(source, target, load.at[slot, i]) for i, (source, target) in enumerate(copies)]

    for copy in loads(0):
        copy.start()
    have(context_here)
    have(attn_here)
    total[...] = dot(s0[...], s1[...], TN)
    wire_blocks(total, p_third)
    for step in bends[0][2:3]:
        step()
    have(final_here)
    have(eg_here)
    total[:, :128] = dot(s2[...], eg_held[...], TN)
    wire_blocks(total, p_third, 0, 0, 128, 384)
    carry(p_third, p_out).wait()
    out.start()
    hooks = iter([
        [*bends[0][3:], merges[1][0]], merges[1][1:], [merges[2][0]], merges[2][1:], [], [], closes[0][:2], closes[0][2:],
        bends[1][:1],
        bends[1][1:2], bends[1][2:3], bends[1][3:], [ends[0]], [merges[3][0]], merges[3][1:], bends[2][:2], bends[2][2:],
        bends[3][:2],
        bends[3][2:], closes[1][:1], closes[1][1:2], [merges[4][0], *closes[1][2:3]], merges[4][1:], closes[1][3:], closes[2][:2], closes[2][2:],
        [ends[1], *bends[4]],
        [merges[5][0], *closes[3][:2]], [*merges[5][1:], *closes[3][2:]], [ends[2], *closes[4][:2]], [*closes[4][2:], *bends[5][:2]], [*bends[5][2:], ends[3]],
    ])

    def hook():
        for step in next(hooks):
            step()

    for n, (group, row, length, s) in enumerate(order):
        if n + 1 < len(order):
            for copy in loads(n + 1):
                copy.start()
        for copy in loads(n):
            copy.wait()
        slot = n % 2
        attend_back(slot_proj.at[slot], slot_grad.at[slot], slot_pl.at[slot], grads, vectors, row, length, group)
        hook()
        if n % 8 == 7:
            if group == 0:
                have(x_here)
            total[...] = dot(x_ref[...], grads[:, 768 * group : 768 * group + 768], TN)
            if group == 2:
                vectors_on_wire(vectors, p_third, 384)
            wire_blocks(total, groups[group])
            heads[group].start()
            hook()
    have(weights_here)
    for row, length in [(0, SHORT)] + [(SHORT + 320 * s, 320) for s in range(4)]:
        rows = pl.ds(row, length)
        token_part[rows] = dot(grads[rows], w_qkv[...], NT).astype(jnp.bfloat16)
        carry(token_part.at[rows], part_out.at[rows])
        hook()
    for step in [ends[4], *closes[5], ends[5]]:
        step()
    for copy in carried[9:]:
        copy.wait()
    for piece in pieces:
        piece.drain()


def last(operands, sums, x):
    vmem, anywhere = (pl.BlockSpec(memory_space=m) for m in (pltpu.VMEM, pl.ANY))
    full = lambda *dims: jax.ShapeDtypeStruct(dims, jnp.float32)
    low = lambda *dims: jax.ShapeDtypeStruct(dims, jnp.bfloat16)
    held = lambda *dims: pltpu.VMEM(dims, jnp.bfloat16)
    semaphores = lambda *dims: pltpu.SemaphoreType.DMA(dims)
    scratch = []
    for dims, cut in zip(BACK, BACK_CUT):
        scratch += work_shapes(*dims, cut)
    return pl.pallas_call(
        last_kernel,
        out_shape=(low(ROWS, 768), *[full(*dims) for dims in BACK], *[low(4, 2, 2, 2, *dims) for dims in BACK[:3]]),
        in_specs=[anywhere] * 13 + [vmem, anywhere],
        out_specs=(anywhere,) + (vmem,) * 6 + (anywhere,) * 3,
        scratch_shapes=[held(2, 2, 2, 2, 96, 768)]
        + [held(4, 2, 2, 2, *dims) for dims in BACK[3:]]
        + [held(2, 320, 768), held(2, 320, 256), held(2, 4, 320, 320), held(ROWS, 2304), held(768, 2304)]
        + [pltpu.VMEM((768, 768), jnp.float32), pltpu.VMEM((16, 3072), jnp.float32), held(ROWS, 768), held(ROWS, P_SIZE), held(ROWS, 768)]
        + scratch
        + [semaphores(SUMS * len(BACK)), semaphores(SUMS * len(BACK)), semaphores(len(BACK)), semaphores(2, 5), semaphores(32), semaphores(16)],
        compiler_params=pltpu.CompilerParams(collective_id=1, has_side_effects=True, vmem_limit_bytes=63 * 2**20),
    )(*operands, sums, x)[:7]


def finish_kernel(resid, part, d, u, o, g0, g1, g2, gs, gl, q_out, k_out, v_out, o_out, u_out, d_out, e_out, *vectors):
    tile = pl.program_id(0)
    value = resid[...] + part[...].astype(jnp.float32)

    @pl.when(tile < 2)
    def _():
        gs[...] = value

    @pl.when(tile >= 2)
    def _():
        gl[...] = value

    @pl.when(tile == 0)
    def _():
        d_out[...] = d[...]
        for wire, target, half in ((u, u_out, 1536), (o, o_out, 384)):
            target[:, :half] = wire[:24, :half]
            target[:, half:] = wire[24:, :half]
        e_out[...] = o[:24, 384:]
        for g, wire in enumerate((g0, g1, g2)):
            low = 256 * g
            q_out[:, low : low + 256] = wire[:24, :256]
            k_out[:, low : low + 128] = wire[:24, 256:384]
            k_out[:, low + 128 : low + 256] = wire[24:, :128]
            v_out[:, low : low + 256] = wire[24:, 128:384]
        for i, target in enumerate(vectors):
            width = target.shape[0]
            target[...] = g2[i : i + 1, 384 : 384 + width].reshape(width)


def finish(resid, part, wires, shards):
    tile = 256
    full = lambda *dims: jax.ShapeDtypeStruct(dims, jnp.float32)
    every = pl.BlockSpec((tile, 768), lambda i: (i, 0))
    whole = lambda one: pl.BlockSpec(one.shape, lambda i: (0,) * one.ndim)
    cut = SHORT // tile
    query, key, value, out, up, down, embed, *vectors = shards
    return pl.pallas_call(
        finish_kernel,
        grid=(ROWS // tile,),
        out_shape=(full(SHORT, 768), full(ROWS - SHORT, 768), *[full(*one.shape) for one in shards]),
        in_specs=[every, every] + [whole(one) for one in wires],
        out_specs=(
            pl.BlockSpec((tile, 768), lambda i: (jnp.minimum(i, cut - 1), 0)),
            pl.BlockSpec((tile, 768), lambda i: (jnp.maximum(i - cut, 0), 0)),
            *[whole(one) for one in shards],
        ),
        compiler_params=pltpu.CompilerParams(vmem_limit_bytes=40 * 2**20),
    )(resid, part, *wires)


def fast_body(xs, len_short, xl, len_long, shards, cs, cl):
    flat = lambda one: one.reshape(-1, one.shape[-1])
    w_qkv, w_out, w_up, w_embed, w_down, vec, proj, context, ps, pls, x, cot = first(
        len_short, len_long, flat(xs), flat(xl), flat(cs), flat(cl), shards
    )
    es, el, act, pre, hidden, ffn, attn, final, embed_grad, resid, context_grad, sums = token_chain(
        len_short, len_long, x, cot, context, w_out, w_up, w_down.reshape(3072, 768), w_embed, vec
    )
    part, *wires = last((act, pre, hidden, ffn, attn, final, embed_grad, context, proj, context_grad, ps, pls, w_qkv), sums, x)
    gs, gl, *owned = finish(resid, part, wires, shards)
    shaped = lambda value, like: value.reshape(*like.shape[:2], -1)
    return (shaped(es, xs), shaped(el, xl), shaped(gs, xs), shaped(gl, xl), *owned)


def body(tokens_short, lengths_short, tokens_long, lengths_long, *rest):
    shards, (cotangent_short, cotangent_long) = rest[:16], rest[16:]
    weights = tuple(lax.all_gather(one, BOTH, axis=0, tiled=True) for one in shards)
    embed_short, saved_short = forward(tokens_short, lengths_short, weights)
    embed_long, saved_long = forward(tokens_long, lengths_long, weights)
    input_short, grads_short = backward(saved_short, weights, cotangent_short)
    input_long, grads_long = backward(saved_long, weights, cotangent_long)
    totals = jax.tree.map(jnp.add, grads_short, grads_long)
    owned = tuple(lax.psum_scatter(one, BOTH, scatter_dimension=0, tiled=True) for one in totals)
    return (embed_short, embed_long, input_short, input_long, *owned)


def solution(mesh):
    split = lambda rank: P(BOTH, *([None] * (rank - 1)))
    weights = [split(2)] * 7 + [split(1)] * 9
    in_specs = (split(3), split(1), split(3), split(1), *weights, split(3), split(3))
    out_specs = (split(3),) * 4 + tuple(weights)
    fast = mesh.shape["wide"] == 16 and mesh.shape["narrow"] == 2

    def step(xs, len_short, xl, len_long, *rest):
        if fast:
            return fast_body(xs, len_short, xl, len_long, rest[:16], *rest[16:])
        return body(xs, len_short, xl, len_long, *rest)

    return jax.shard_map(step, mesh=mesh, in_specs=in_specs, out_specs=out_specs, check_vma=False)
```

```python
import functools
import math

import jax
import jax.numpy as jnp
from jax import lax
from jax.experimental import pallas as pl
from jax.experimental.pallas import tpu as pltpu
from jax.sharding import PartitionSpec as P

MESH = pl.DeviceIdType.MESH

HD = 64
P_SIZE = 128


norm_epsilon = 1e-12
unit_epsilon = 1e-06
masked_fill = -1000000000.0


def layer_norm(residual, norm_gain, norm_shift):
    center = residual - jnp.mean(residual, axis=-1, keepdims=True)
    variance = jnp.mean(center * center, axis=-1, keepdims=True)
    return center * lax.rsqrt(variance + norm_epsilon) * norm_gain + norm_shift


def gelu_exact(pre_act):
    return 0.5 * pre_act * (1.0 + lax.erf(pre_act * (1.0 / math.sqrt(2.0))))


def normalize(embedding, token_mask):
    squares = jnp.sum(embedding * embedding, axis=-1, keepdims=True)
    return math.sqrt(P_SIZE) * embedding * lax.rsqrt(squares + unit_epsilon) * token_mask[..., None]


def soft_weights(scaled, key_mask):
    masked = jnp.where(key_mask, scaled, masked_fill)
    row_peak = jnp.max(masked, axis=-1, keepdims=True)
    exponent = jnp.exp(masked - row_peak)
    return exponent / jnp.sum(exponent, axis=-1, keepdims=True)


def matmul(left_side, right_side, form):
    return jnp.einsum(form, left_side, right_side, preferred_element_type=jnp.float32)


def forward(tokens, lengths, full_weights):
    (
        query_weight,
        key_weight,
        value_weight,
        out_weight,
        up_weight,
        down_weight,
        embed_weight,
        query_bias,
        value_bias,
        out_bias,
        attention_gain,
        attention_shift,
        up_bias,
        down_bias,
        final_gain,
        final_shift,
    ) = full_weights
    seq_count, length, model_width = tokens.shape
    head_count = model_width // HD
    score_scale = 1.0 / math.sqrt(HD)
    positions = jnp.arange(length, dtype=jnp.int32)
    token_mask = (positions[None, :] < lengths[:, None]).astype(jnp.float32)
    key_mask = token_mask[:, None, None, :] > 0.5
    query_low = (matmul(tokens, query_weight, "bld,de->ble") + query_bias).astype(jnp.bfloat16)
    query_low = query_low.reshape(seq_count, length, head_count, HD)
    key_low = matmul(tokens, key_weight, "bld,de->ble").astype(jnp.bfloat16)
    key_low = key_low.reshape(seq_count, length, head_count, HD)
    value_low = (matmul(tokens, value_weight, "bld,de->ble") + value_bias).astype(jnp.bfloat16)
    value_low = value_low.reshape(seq_count, length, head_count, HD)
    raw_scores = matmul(query_low, key_low, "bqhe,bkhe->bhqk") * score_scale
    attn_probs = soft_weights(raw_scores, key_mask)
    probs_low = attn_probs.astype(jnp.bfloat16)
    context_low = matmul(probs_low, value_low, "bhqk,bkhe->bqhe")
    context_low = context_low.reshape(seq_count, length, model_width).astype(jnp.bfloat16)
    attn_out = matmul(context_low, out_weight, "bld,de->ble") + out_bias
    resid_one = tokens.astype(jnp.float32) + attn_out
    normed_one = layer_norm(resid_one, attention_gain, attention_shift)
    hidden_low = normed_one.astype(jnp.bfloat16)
    pre_act = matmul(hidden_low, up_weight, "bld,df->blf") + up_bias
    act_low = gelu_exact(pre_act).astype(jnp.bfloat16)
    ffn_out = matmul(act_low, down_weight, "blf,fd->bld") + down_bias
    resid_two = normed_one + ffn_out
    final_low = layer_norm(resid_two, final_gain, final_shift).astype(jnp.bfloat16)
    embedding = matmul(final_low, embed_weight, "bld,dp->blp")
    result = normalize(embedding, token_mask)
    saved = (
        tokens,
        token_mask,
        query_low,
        key_low,
        value_low,
        attn_probs,
        probs_low,
        context_low,
        resid_one,
        hidden_low,
        pre_act,
        act_low,
        resid_two,
        final_low,
        embedding,
    )
    return (result, saved)


def backward(saved, full_weights, cotangent):
    (
        tokens,
        token_mask,
        query_low,
        key_low,
        value_low,
        attn_probs,
        probs_low,
        context_low,
        resid_one,
        hidden_low,
        pre_act,
        act_low,
        resid_two,
        final_low,
        embedding,
    ) = saved
    (
        query_weight,
        key_weight,
        value_weight,
        out_weight,
        up_weight,
        down_weight,
        embed_weight,
        query_bias,
        value_bias,
        out_bias,
        attention_gain,
        attention_shift,
        up_bias,
        down_bias,
        final_gain,
        final_shift,
    ) = full_weights
    seq_count, length, model_width = tokens.shape
    score_scale = 1.0 / math.sqrt(HD)
    _, pull_norm = jax.vjp(lambda vector: normalize(vector, token_mask), embedding)
    (embed_grad,) = pull_norm(cotangent.astype(jnp.float32))
    embed_low = embed_grad.astype(jnp.bfloat16)
    grad_embed = matmul(final_low, embed_low, "bld,blp->dp")
    final_grad = matmul(embed_low, embed_weight, "blp,dp->bld")
    _, pull_two = jax.vjp(
        layer_norm, resid_two, final_gain.astype(jnp.float32), final_shift.astype(jnp.float32)
    )
    resid_two_grad, grad_final_gain, grad_final_shift = pull_two(final_grad)
    ffn_low = resid_two_grad.astype(jnp.bfloat16)
    grad_down_bias = jnp.sum(ffn_low, axis=(0, 1), dtype=jnp.float32)
    grad_down = matmul(act_low, ffn_low, "blf,bld->fd")
    act_grad = matmul(ffn_low, down_weight, "bld,fd->blf")
    _, pull_gelu = jax.vjp(gelu_exact, pre_act)
    (pre_grad,) = pull_gelu(act_grad)
    pre_low = pre_grad.astype(jnp.bfloat16)
    grad_up_bias = jnp.sum(pre_low, axis=(0, 1), dtype=jnp.float32)
    grad_up = matmul(hidden_low, pre_low, "bld,blf->df")
    normed_grad = resid_two_grad + matmul(pre_low, up_weight, "blf,df->bld")
    _, pull_one = jax.vjp(
        layer_norm,
        resid_one,
        attention_gain.astype(jnp.float32),
        attention_shift.astype(jnp.float32),
    )
    resid_one_grad, grad_attention_gain, grad_attention_shift = pull_one(normed_grad)
    attn_low = resid_one_grad.astype(jnp.bfloat16)
    grad_out_bias = jnp.sum(attn_low, axis=(0, 1), dtype=jnp.float32)
    grad_out = matmul(context_low, attn_low, "bld,ble->de")
    context_grad = matmul(attn_low, out_weight, "ble,de->bld").astype(jnp.bfloat16)
    context_grad = context_grad.reshape(seq_count, length, -1, HD)
    value_grad = matmul(probs_low, context_grad, "bhqk,bqhe->bkhe")
    probs_grad = matmul(context_grad, value_low, "bqhe,bkhe->bhqk")
    score_low = attn_probs * (probs_grad - jnp.sum(probs_grad * attn_probs, axis=-1, keepdims=True))
    score_low = score_low.astype(jnp.bfloat16)
    query_grad = (matmul(score_low, key_low, "bhqk,bkhe->bqhe") * score_scale).astype(jnp.bfloat16)
    query_grad = query_grad.reshape(seq_count, length, model_width)
    key_grad = (matmul(score_low, query_low, "bhqk,bqhe->bkhe") * score_scale).astype(jnp.bfloat16)
    key_grad = key_grad.reshape(seq_count, length, model_width)
    value_grad_low = value_grad.astype(jnp.bfloat16).reshape(seq_count, length, model_width)
    grad_query_bias = jnp.sum(query_grad, axis=(0, 1), dtype=jnp.float32)
    grad_value_bias = jnp.sum(value_grad_low, axis=(0, 1), dtype=jnp.float32)
    grad_query = matmul(tokens, query_grad, "bld,ble->de")
    grad_key = matmul(tokens, key_grad, "bld,ble->de")
    grad_value = matmul(tokens, value_grad_low, "bld,ble->de")
    input_grad = (
        resid_one_grad
        + matmul(query_grad, query_weight, "ble,de->bld")
        + matmul(key_grad, key_weight, "ble,de->bld")
        + matmul(value_grad_low, value_weight, "ble,de->bld")
    )
    gradients = (
        grad_query,
        grad_key,
        grad_value,
        grad_out,
        grad_up,
        grad_down,
        grad_embed,
        grad_query_bias,
        grad_value_bias,
        grad_out_bias,
        grad_attention_gain,
        grad_attention_shift,
        grad_up_bias,
        grad_down_bias,
        grad_final_gain,
        grad_final_shift,
    )
    return (input_grad, gradients)


BOTH = ("wide", "narrow")
WIRE = ((48, 512), (48, 768), (48, 512), (48, 1536), (96, 768))
CUT = (256, 384, 256, 768, 384)
ROWS = 1792
SHORT = 512
COPIES = 39


def place():
    wide = lax.axis_index("wide")
    return wide // 4, (wide // 2) % 2, wide % 2, lax.axis_index("narrow")


def greet(z, y, c, x):
    partners = [device((z + d) % 4, y, c, x) for d in (1, 2, 3)]
    partners += [device(z, 1 - y, c, x), device(z, y, 1 - c, x), device(z, y, c, 1 - x)]
    barrier = pltpu.get_barrier_semaphore()
    for partner in partners:
        pl.semaphore_signal(barrier, inc=1, device_id=partner, device_id_type=MESH)
    pl.semaphore_wait(barrier, len(partners))


def device(z, y, c, x):
    return (z * 4 + y * 2 + c, x)


class Lazy:
    def __init__(self, make):
        self.make = make

    def __getitem__(self, way):
        return self.make(way)


class Gather:
    def __init__(self, held, cut, send, recv, first):
        self.held, self.cut, self.send, self.recv, self.first = held, cut, send, recv, first
        self.z, self.y, self.c, self.x = place()

    def view(self, block, half):
        if half is None:
            return self.held.at[block]
        lanes = self.held.shape[-1]
        low, size = ((0, self.cut), (self.cut, lanes - self.cut))[half]
        return self.held.at[(*block, slice(None), pl.ds(low, size))]

    def plan(self, slot, out, into, half, target):
        def copy(block):
            return pltpu.make_async_remote_copy(
                src_ref=self.view(block, half),
                dst_ref=self.view(block, half),
                send_sem=self.send.at[self.first + slot],
                recv_sem=self.recv.at[self.first + slot],
                device_id=target,
                device_id_type=MESH,
            )

        return Lazy(lambda way: copy((out, into)[way]))

    def along_z(self, d):
        z, y, c, x = self.z, self.y, self.c, self.x
        return self.plan(d - 1, (z, y, c, x), ((z + 4 - d) % 4, y, c, x), None, device((z + d) % 4, y, c, x))

    def to_x(self, d):
        z, y, c, x = (self.z + 4 - d) % 4, self.y, self.c, self.x
        return self.plan(3 + d, (z, y, c, x), (z, y, c, 1 - x), None, device(self.z, y, c, 1 - x))

    def to_y(self, d):
        z, y, c, x = (self.z + 4 - d) % 4, self.y, self.c, self.x
        return self.plan(7 + d, (z, y, c, x), (z, 1 - y, c, x), None, device(self.z, 1 - y, c, x))

    def corner(self, d, half):
        z, y, c, x = (self.z + 4 - d) % 4, self.y, self.c, self.x
        if half == 0:
            return self.plan(11 + d, (z, y, c, 1 - x), (z, 1 - y, c, 1 - x), 0, device(self.z, 1 - y, c, x))
        return self.plan(15 + d, (z, 1 - y, c, x), (z, 1 - y, c, 1 - x), 1, device(self.z, y, c, 1 - x))

    def to_core(self, d, kind):
        z, c = (self.z + 4 - d) % 4, self.c
        y = 1 - self.y if kind >= 2 else self.y
        x = 1 - self.x if kind in (1, 3, 4) else self.x
        half = kind - 3 if kind >= 3 else None
        return self.plan(19 + 4 * kind + d, (z, y, c, x), (z, y, 1 - c, x), half, device(self.z, self.y, 1 - c, self.x))

    def start_z(self):
        for d in (1, 2, 3):
            self.along_z(d)[0].start()

    def spread(self, d):
        self.to_x(d)[0].start()
        self.to_y(d)[0].start()
        self.to_core(d, 0)[0].start()

    def column(self, d):
        self.along_z(d)[1].wait_recv()
        self.spread(d)

    def turn(self, d):
        self.to_x(d)[1].wait_recv()
        self.corner(d, 0)[0].start()
        self.to_core(d, 1)[0].start()
        self.to_y(d)[1].wait_recv()
        self.corner(d, 1)[0].start()
        self.to_core(d, 2)[0].start()

    def finish(self, d):
        for half in (0, 1):
            self.corner(d, half)[1].wait_recv()
            self.to_core(d, 3 + half)[0].start()

    def arrive(self):
        for d in range(4):
            for kind in range(5):
                self.to_core(d, kind)[1].wait_recv()

    def drain(self):
        for d in range(4):
            if d:
                self.along_z(d)[0].wait_send()
            self.to_x(d)[0].wait_send()
            self.to_y(d)[0].wait_send()
            for half in (0, 1):
                self.corner(d, half)[0].wait_send()
            for kind in range(5):
                self.to_core(d, kind)[0].wait_send()


def stack_halves(whole):
    half = whole.shape[1] // 2
    return jnp.concatenate([whole[:, :half], whole[:, half:]], axis=0).astype(jnp.bfloat16)


def unpack_rows(held, targets):
    def pair(p, carry):
        z, y, c = p // 4, (p // 2) % 2, p % 2
        one, two = held[z, y, c, 0].astype(jnp.float32), held[z, y, c, 1].astype(jnp.float32)
        for side, low, ref, column, lanes in targets:
            rows = slice(24 * side, 24 * side + 24)
            both = jnp.concatenate([one[rows, low : low + lanes], two[rows, low : low + lanes]], axis=0)
            ref[pl.ds(pl.multiple_of(p * 48, 48), 48), column : column + lanes] = both.astype(jnp.bfloat16)
        return carry

    lax.fori_loop(0, 16, pair, 0)


NN = (((1,), (0,)), ((), ()))
NT = (((1,), (1,)), ((), ()))
TN = (((0,), (0,)), ((), ()))


def dot(left, right, dims):
    return lax.dot_general(left, right, dims, preferred_element_type=jnp.float32)


def padded(length):
    return -(-length // 128) * 128


def two_heads(pair, width):
    length = pair.shape[0]
    lane = lax.broadcasted_iota(jnp.int32, (length, 128), 1)
    parts = []
    for here in (lane < 64, lane >= 64):
        parts.append(jnp.where(here, pair, jnp.bfloat16(0)))
        if width > length:
            parts.append(jnp.zeros((width - length, 128), jnp.bfloat16))
    return jnp.concatenate(parts, axis=0)


def attend(qkv, context, probs, row, length, valid, first, last):
    rows = pl.ds(row, length)
    width = padded(length)
    fill = jnp.where(lax.broadcasted_iota(jnp.int32, (1, width), 1) < valid, 0.0, masked_fill)

    def pair(p):
        at = lambda base: pl.ds(base + p * 128, 128)
        query = qkv[rows, at(0)] * jnp.bfloat16(1.0 / math.sqrt(HD))
        key, value = qkv[rows, at(768)], qkv[rows, at(1536)]
        scores = dot(query, two_heads(key, width), NT)
        parts = []
        for h in (0, 1):
            masked = scores[:, width * h : width * h + width] + fill
            exponent = jnp.exp(masked - jnp.max(masked, axis=1, keepdims=True))
            scale = 1.0 / jnp.sum(exponent, axis=1, keepdims=True)
            parts.append((exponent * scale).astype(jnp.bfloat16))
        low = jnp.concatenate(parts, axis=1)
        probs[p] = low
        context[rows, at(0)] = dot(low, two_heads(value, width), NN).astype(jnp.bfloat16)

    for p in range(first, last):
        pair(p)


def spread_table(group, lanes):
    lane = lax.broadcasted_iota(jnp.int32, (128, lanes), 1).astype(jnp.float32)
    row = lax.broadcasted_iota(jnp.int32, (128, lanes), 0).astype(jnp.float32)
    return (lane - group * jnp.floor((lane + 0.5) * (1.0 / group)) == row).astype(jnp.bfloat16)


def natural_vectors(held, vec_out):
    blocks = [held[p // 8, (p // 4) % 2, (p // 2) % 2, p % 2, :16, 384:512] for p in range(32)]
    stacked = jnp.concatenate(blocks, axis=0)
    wide = dot(stacked, spread_table(24, 768), NN)
    lane = lax.broadcasted_iota(jnp.int32, (512, 768), 1)
    start = (lax.broadcasted_iota(jnp.int32, (512, 768), 0) >> 4) * 24
    wide = jnp.where((lane >= start) & (lane < start + 24), wide, 0.0)
    vec_out[:, :768] = jnp.sum(wide.reshape(32, 16, 768), axis=0)
    picked = dot(
        (lax.broadcasted_iota(jnp.int32, (32, 512), 1) == lax.broadcasted_iota(jnp.int32, (32, 512), 0) * 16 + 5).astype(jnp.bfloat16),
        stacked,
        NN,
    ).astype(jnp.bfloat16)
    wide = dot(picked, spread_table(96, 3072), NN)
    lane = lax.broadcasted_iota(jnp.int32, (32, 3072), 1)
    start = lax.broadcasted_iota(jnp.int32, (32, 3072), 0) * 96
    wide = jnp.where((lane >= start) & (lane < start + 96), wide, 0.0)
    vec_out[9:10, :] = jnp.sum(wide, axis=0, keepdims=True)


def first_kernel(
    len_short, len_long, xs, xl, cs, cl, q_ref, k_ref, v_ref, o_ref, u_ref, d_ref, e_ref, *rest
):
    vec_refs, rest = rest[:9], rest[9:]
    (qkv_out, out_out, up_out, embed_out, down_out, vec_out, proj_out, context_out, ps_out, pl_out, x_out, c_out), rest = rest[:12], rest[12:]
    h0, h1, h2, h3, h4, w_qkv, w_out, w_up, w_embed, proj, context, ps, pls, rows, send, recv, away = rest
    z, y, c, x = place()
    rows[...] = jnp.zeros_like(rows)
    for i, ref in enumerate(vec_refs):
        width = ref.shape[0]
        rows[i : i + 1, :width] = ref[...].astype(jnp.float32).reshape(1, width)
    wide = lambda ref: ref[...].astype(jnp.float32)
    h0[z, y, c, x, :, :384] = stack_halves(wide(q_ref))
    h0[z, y, c, x, :, 384:] = rows[...].astype(jnp.bfloat16)
    h1[z, y, c, x, :, :384] = stack_halves(wide(k_ref))
    h1[z, y, c, x, :, 384:] = stack_halves(wide(v_ref))
    h2[z, y, c, x, :, :384] = stack_halves(wide(o_ref))
    h2[z, y, c, x, :, 384:] = jnp.concatenate([wide(e_ref), wide(e_ref)], axis=0).astype(jnp.bfloat16)
    h3[z, y, c, x] = stack_halves(wide(u_ref))
    h4[z, y, c, x] = d_ref[...]
    greet(z, y, c, x)
    one, two, three, four, five = gathers = [Gather(h, CUT[i], send, recv, COPIES * i) for i, h in enumerate((h0, h1, h2, h3, h4))]
    for piece in gathers:
        piece.start_z()
    for piece in gathers:
        piece.spread(0)
    kept = []

    def keep(source, target):
        copy = pltpu.make_async_copy(source, target, away.at[len(kept)])
        copy.start()
        kept.append(copy)

    for source, target, low in ((xs, x_out, 0), (xl, x_out, SHORT), (cs, c_out, 0), (cl, c_out, SHORT)):
        keep(source, target.at[pl.ds(low, source.shape[0])])
    for d in (1, 2, 3):
        one.column(d)
    for d in (1, 2, 3):
        two.column(d)
    for d in range(4):
        one.turn(d)
    for d in (1, 2, 3):
        three.column(d)
    for d in range(4):
        two.turn(d)
    for d in range(4):
        one.finish(d)
    for d in (1, 2, 3):
        four.column(d)
    one.arrive()
    unpack_rows(h0, [(0, 0, w_qkv, 0, 384), (1, 0, w_qkv, 384, 384)])
    natural_vectors(h0, vec_out)
    for d in range(4):
        two.finish(d)
    step = lambda name, piece, *ds: [functools.partial(getattr(piece, name), d) for d in ds]
    hooks = iter([
        step("turn", three, 0, 1) + step("turn", four, 0) + step("turn", five, 0),
        step("turn", three, 2, 3) + step("turn", four, 1), step("finish", three, 0, 1) + step("column", five, 1),
        step("column", five, 2), step("column", five, 3), step("turn", four, 2), step("turn", four, 3),
        step("finish", three, 2, 3), step("finish", four, 0, 1), step("turn", five, 1), step("turn", five, 2),
        step("turn", five, 3), step("finish", four, 2, 3), step("finish", five, 0), step("finish", five, 1),
    ])

    def hook():
        for one_step in next(hooks):
            one_step()

    tiles = [(0, xs[...])] + [(SHORT + 320 * s, xl[320 * s : 320 * s + 320]) for s in range(4)]
    for part in range(3):
        if part == 1:
            two.arrive()
            unpack_rows(h1, [(0, 0, w_qkv, 768, 384), (1, 0, w_qkv, 1152, 384), (0, 384, w_qkv, 1536, 384), (1, 384, w_qkv, 1920, 384)])
            keep(w_qkv, qkv_out)
        lanes = slice(768 * part, 768 * part + 768)
        for row, tokens in tiles:
            result = dot(tokens, w_qkv[:, lanes], NN)
            if part != 1:
                result = result + vec_out[part // 2 : part // 2 + 1, :768]
            proj[row : row + tokens.shape[0], lanes] = result.astype(jnp.bfloat16)
        hook()
    keep(proj, proj_out)
    for s in range(4):
        attend(proj, context, ps.at[s], 128 * s, 128, len_short[s], 0, 6)
        hook()
    keep(ps, ps_out)
    slots = []
    for s in range(4):
        if s >= 2:
            slots[s - 2].wait()
        for part in (0, 3):
            attend(proj, context, pls.at[s % 2], SHORT + 320 * s, 320, len_long[s], part, part + 3)
            hook()
        copy = pltpu.make_async_copy(pls.at[s % 2], pl_out.at[s], away.at[12 + s])
        copy.start()
        slots.append(copy)
        if s == 1:
            three.arrive()
            unpack_rows(h2, [(0, 0, w_out, 0, 384), (1, 0, w_out, 384, 384), (0, 384, w_embed, 0, 128)])
            keep(w_out, out_out)
            keep(w_embed, embed_out)
    keep(context, context_out)
    four.arrive()
    unpack_rows(h3, [(0, 0, w_up, 0, 1536), (1, 0, w_up, 1536, 1536)])
    keep(w_up, up_out)
    for d in (2, 3):
        five.finish(d)
    five.arrive()
    keep(h4, down_out)
    for copy in kept + slots[2:]:
        copy.wait()
    for piece in gathers:
        piece.drain()


def first(len_short, len_long, xs, xl, cs, cl, shards):
    vmem, smem, anywhere = (pl.BlockSpec(memory_space=m) for m in (pltpu.VMEM, pltpu.SMEM, pl.ANY))
    low = lambda *dims: jax.ShapeDtypeStruct(dims, jnp.bfloat16)
    held = lambda *dims: pltpu.VMEM(dims, jnp.bfloat16)
    semaphores = lambda count: pltpu.SemaphoreType.DMA((count,))
    weights = [(768, 2304), (768, 768), (768, 3072), (768, 128)]
    return pl.pallas_call(
        first_kernel,
        out_shape=(
            *[low(*dims) for dims in weights], low(4, 2, 2, 2, *WIRE[4]),
            jax.ShapeDtypeStruct((16, 3072), jnp.float32),
            low(ROWS, 2304), low(ROWS, 768), low(4, 6, 128, 256), low(4, 6, 320, 768), low(ROWS, 768), low(ROWS, P_SIZE),
        ),
        in_specs=[smem] * 2 + [vmem] * 2 + [anywhere] * 2 + [vmem] * 16,
        out_specs=(anywhere,) * 5 + (vmem,) + (anywhere,) * 6,
        scratch_shapes=[held(4, 2, 2, 2, *dims) for dims in WIRE]
        + [held(*dims) for dims in weights]
        + [held(ROWS, 2304), held(ROWS, 768), held(4, 6, 128, 256), held(2, 6, 320, 768), pltpu.VMEM((48, 128), jnp.float32)]
        + [semaphores(COPIES * 5), semaphores(COPIES * 5), semaphores(16)],
        compiler_params=pltpu.CompilerParams(collective_id=0, has_side_effects=True, vmem_limit_bytes=62 * 2**20),
    )(len_short, len_long, xs, xl, cs, cl, *shards)


TILE = 448
PART = 224


def center(value):
    return value - jnp.mean(value, axis=1, keepdims=True)


def normal(value):
    value = center(value)
    scale = lax.rsqrt(jnp.mean(value * value, axis=1, keepdims=True) + norm_epsilon)
    return value * scale, scale


def normal_back(grad, unit, scale):
    inner = jnp.mean(grad * unit, axis=1, keepdims=True)
    return scale * (center(grad) - unit * inner)


def embed_copies(step, embedded, es_out, el_out, away):
    low, high = TILE * step, TILE * step + TILE
    cut = min(max(SHORT, low), high)
    copies = []
    if low < cut:
        copies.append((embedded.at[pl.ds(0, cut - low)], es_out.at[pl.ds(low, cut - low)]))
    if cut < high:
        copies.append((embedded.at[pl.ds(cut - low, high - cut)], el_out.at[pl.ds(cut - SHORT, high - cut)]))
    return [pltpu.make_async_copy(source, target, away.at[i]) for i, (source, target) in enumerate(copies)]


def token_kernel(
    len_short, len_long, x_ref, cot_ref, ctx_ref, w_out, w_up, w_down, w_embed, vec,
    es_out, el_out, act_out, pre_out, hidden_out, ffn_out, attn_out, final_out, eg_out, resid_out, cg_out, sums,
    slope, embedded, away,
):
    tile = pl.program_id(0)
    row = lambda k: vec[k : k + 1, :768]
    low = lambda value: value.astype(jnp.bfloat16)
    wide = lambda value: value.astype(jnp.float32)

    @pl.when(tile == 0)
    def _():
        sums[...] = jnp.zeros_like(sums)

    def add(k, value):
        sums[k : k + 1, : value.shape[1]] += jnp.sum(value, axis=0, keepdims=True)

    def chain(start):
        rows = slice(start, start + PART)
        mixed = wide(x_ref[rows]) + (dot(ctx_ref[rows], w_out[...], NN) + row(2))
        yield
        unit_one, scale_one = normal(mixed)
        normed_one = unit_one * row(3) + row(4)
        hidden = low(normed_one)
        hidden_out[rows] = hidden
        ffn = None
        for f in range(4):
            lanes = slice(768 * f, 768 * f + 768)
            pre = dot(hidden, w_up[:, lanes], NN) + vec[9:10, lanes]
            cdf = 0.5 + 0.5 * lax.erf(pre * (1.0 / math.sqrt(2.0)))
            act = low(pre * cdf)
            act_out[rows, lanes] = act
            slope[rows, lanes] = cdf + pre * (jnp.exp(-0.5 * pre * pre) * (1.0 / math.sqrt(2.0 * math.pi)))
            part = dot(act, w_down[lanes, :], NN)
            ffn = part if ffn is None else ffn + part
        yield
        unit_two, scale_two = normal(normed_one + (ffn + row(6)))
        final = low(unit_two * row(7) + row(8))
        final_out[rows] = final
        embedding = dot(final, w_embed[...], NN)
        inverse = lax.rsqrt(jnp.sum(embedding * embedding, axis=1, keepdims=True) + unit_epsilon)
        at = lax.broadcasted_iota(jnp.int32, (PART, 1), 0) + (tile * TILE + start)
        mask = jnp.zeros((PART, 1), jnp.float32)
        for sizes, low_row, stride in ((len_short, 0, 128), (len_long, SHORT, 320)):
            for s in range(4):
                begin = low_row + s * stride
                mask = mask + jnp.where((at >= begin) & (at < begin + sizes[s]), 1.0, 0.0)
        embedded[rows] = math.sqrt(P_SIZE) * embedding * inverse * mask
        grad = wide(cot_ref[rows]) * mask
        inner = jnp.sum(grad * embedding, axis=1, keepdims=True)
        embed_grad = low(math.sqrt(P_SIZE) * inverse * (grad - inverse * inverse * embedding * inner))
        eg_out[rows] = embed_grad
        final_grad = dot(embed_grad, w_embed[...], NT)
        yield
        add(7, final_grad * unit_two)
        add(8, final_grad)
        resid_two = normal_back(final_grad * row(7), unit_two, scale_two)
        ffn_grad = low(resid_two)
        ffn_out[rows] = ffn_grad
        add(6, wide(ffn_grad))
        normed_grad = resid_two
        for f in range(4):
            lanes = slice(768 * f, 768 * f + 768)
            pre_grad = low(dot(ffn_grad, w_down[lanes, :], NT) * slope[rows, lanes])
            pre_out[rows, lanes] = pre_grad
            sums[9:10, lanes] += jnp.sum(wide(pre_grad), axis=0, keepdims=True)
            normed_grad = normed_grad + dot(pre_grad, w_up[:, lanes], NT)
        yield
        add(3, normed_grad * unit_one)
        add(4, normed_grad)
        resid_one = normal_back(normed_grad * row(3), unit_one, scale_one)
        resid_out[rows] = resid_one
        attn_grad = low(resid_one)
        attn_out[rows] = attn_grad
        add(2, wide(attn_grad))
        cg_out[rows] = low(dot(attn_grad, w_out[...], NT))
        yield

    chains = [chain(start) for start in range(0, TILE, PART)]
    for _ in range(5):
        for one in chains:
            next(one)

    def embeds(act):
        for step in range(ROWS // TILE):

            @pl.when(tile == step)
            def _():
                for copy in embed_copies(step, embedded, es_out, el_out, away):
                    getattr(copy, act)()

    embeds("start")
    embeds("wait")


def token_chain(len_short, len_long, x, cot, context, w_out, w_up, w_down, w_embed, vec):
    smem, anywhere = pl.BlockSpec(memory_space=pltpu.SMEM), pl.BlockSpec(memory_space=pl.ANY)
    every = lambda lanes: pl.BlockSpec((TILE, lanes), lambda i: (i, 0))
    whole = lambda array: pl.BlockSpec(array.shape, lambda i: (0, 0), pipeline_mode=pl.Buffered(1))
    shape = lambda kind, *dims: jax.ShapeDtypeStruct(dims, kind)
    low = lambda lanes: shape(jnp.bfloat16, ROWS, lanes)
    return pl.pallas_call(
        token_kernel,
        grid=(ROWS // TILE,),
        out_shape=(
            shape(jnp.float32, SHORT, P_SIZE), shape(jnp.float32, ROWS - SHORT, P_SIZE),
            low(3072), low(3072), low(768), low(768), low(768), low(768), low(P_SIZE),
            shape(jnp.float32, ROWS, 768), low(768), shape(jnp.float32, 16, 3072),
        ),
        in_specs=[smem, smem, every(768), every(P_SIZE), every(768)] + [whole(one) for one in (w_out, w_up, w_down, w_embed, vec)],
        out_specs=(
            anywhere, anywhere, every(3072), every(3072), every(768), every(768), every(768), every(768), every(P_SIZE),
            every(768), every(768), pl.BlockSpec((16, 3072), lambda i: (0, 0)),
        ),
        scratch_shapes=[pltpu.VMEM((TILE, 3072), jnp.float32), pltpu.VMEM((TILE, P_SIZE), jnp.float32), pltpu.SemaphoreType.DMA((2,))],
        compiler_params=pltpu.CompilerParams(vmem_limit_bytes=62 * 2**20),
    )(len_short, len_long, x, cot, context, w_out, w_up, w_down, w_embed, vec)


class Scatter:
    def __init__(self, mine, cut, work, send, recv, local, number):
        self.mine, self.cut, self.send, self.recv, self.first = mine, cut, send, recv, SUMS * number
        self.core_in, self.total, self.corner_y, self.corner_x, self.from_x, self.from_y, self.from_z = work
        self.z, self.y, self.c, self.x = place()
        self.own = pltpu.make_async_copy(mine.at[:, :, self.c], self.total, local.at[number])

    def copy(self, slot, source, target, partner):
        return pltpu.make_async_remote_copy(
            src_ref=source,
            dst_ref=target,
            send_sem=self.send.at[self.first + slot],
            recv_sem=self.recv.at[self.first + slot],
            device_id=partner,
            device_id_type=MESH,
        )

    def spot(self, kind):
        return (1 - self.y if kind in (0, 2) else self.y), (1 - self.x if kind in (0, 1) else self.x)

    def core(self, kind):
        y, x = self.spot(kind)
        return self.copy(
            kind,
            self.mine.at[:, y, 1 - self.c, x],
            self.core_in.at[:, y, x],
            device(self.z, self.y, 1 - self.c, self.x),
        )

    def corner(self, d, half):
        z = (self.z + d) % 4
        y, x = self.spot(0)
        low, size = ((0, self.cut), (self.cut, self.total.shape[-1] - self.cut))[half]
        source = self.total.at[z, y, x, :, pl.ds(low, size)]
        if half == 0:
            return self.copy(4 + d, source, self.corner_y.at[z], device(self.z, 1 - self.y, self.c, self.x))
        return self.copy(8 + d, source, self.corner_x.at[z], device(self.z, self.y, self.c, 1 - self.x))

    def to_x(self, d):
        z = (self.z + d) % 4
        return self.copy(12 + d, self.total.at[z, self.y, 1 - self.x], self.from_x.at[z], device(self.z, self.y, self.c, 1 - self.x))

    def to_y(self, d):
        z = (self.z + d) % 4
        return self.copy(16 + d, self.total.at[z, 1 - self.y, self.x], self.from_y.at[z], device(self.z, 1 - self.y, self.c, self.x))

    def along_z(self, d):
        z = (self.z + d) % 4
        return self.copy(19 + d, self.total.at[z, self.y, self.x], self.from_z.at[d - 1], device(z, self.y, self.c, self.x))

    def start(self):
        self.own.start()
        for kind in range(4):
            self.core(kind).start()

    def merge(self, kind):
        if kind == 0:
            self.own.wait()
        self.core(kind).wait_recv()
        y, x = self.spot(kind)

        def add(z, carry):
            self.total[z, y, x] = self.total[z, y, x] + self.core_in[z, y, x]
            return carry

        lax.fori_loop(0, 4, add, 0)
        if kind == 0:
            for d in (1, 2, 3, 0):
                self.corner(d, 0).start()
                self.corner(d, 1).start()

    def bend(self, d):
        z = (self.z + d) % 4
        self.corner(d, 0).wait_recv()
        self.total[z, self.y, 1 - self.x, :, : self.cut] = self.total[z, self.y, 1 - self.x, :, : self.cut] + self.corner_y[z]
        self.to_x(d).start()
        self.corner(d, 1).wait_recv()
        self.total[z, 1 - self.y, self.x, :, self.cut :] = self.total[z, 1 - self.y, self.x, :, self.cut :] + self.corner_x[z]
        self.to_y(d).start()

    def close(self, d):
        z = (self.z + d) % 4
        self.to_x(d).wait_recv()
        self.to_y(d).wait_recv()
        here = self.total[z, self.y, self.x].astype(jnp.float32) + self.from_x[z].astype(jnp.float32)
        self.total[z, self.y, self.x] = (here + self.from_y[z].astype(jnp.float32)).astype(jnp.bfloat16)
        if d:
            self.along_z(d).start()

    def result(self, store):
        total = self.total[self.z, self.y, self.x].astype(jnp.float32)
        for d in (1, 2, 3):
            self.along_z(d).wait_recv()
            total = total + self.from_z[d - 1].astype(jnp.float32)
        store[...] = total

    def drain(self):
        for kind in range(4):
            self.core(kind).wait_send()
        for d in range(4):
            self.corner(d, 0).wait_send()
            self.corner(d, 1).wait_send()
            self.to_x(d).wait_send()
            self.to_y(d).wait_send()
            if d:
                self.along_z(d).wait_send()


SUMS = 23
BACK = ((96, 768), (48, 1536), (48, 512), (48, 384), (48, 384), (48, 512))
BACK_CUT = (384, 768, 256, 128, 128, 256)


def work_shapes(rows, lanes, cut):
    held = lambda *dims: pltpu.VMEM((*dims, rows, lanes), jnp.bfloat16)
    part = lambda size: pltpu.VMEM((4, rows, size), jnp.bfloat16)
    return [held(4, 2, 2), held(4, 2, 2), part(cut), part(lanes - cut), held(4), held(4), held(3)]


def attend_back(proj, grads_in, probs, grads, vectors, row, length, group):
    rows = pl.ds(row, length)
    lane = lax.broadcasted_iota(jnp.int32, (length, 128), 1)
    score_scale = 1.0 / math.sqrt(HD)
    width = padded(length)

    def pair(p):
        at = lambda base: pl.ds(base + p * 128, 128)
        query, key, value = (proj[:length, at(base)] for base in (0, 256, 512))
        context_grad = grads_in[:length, at(0)]
        low = probs[p, :length, : 2 * width]
        weight = low.astype(jnp.float32)
        weight_grad = dot(context_grad, two_heads(value, width), NT)
        parts = []
        for h in (0, 1):
            lanes = slice(width * h, width * h + width)
            inner = jnp.sum(weight_grad[:, lanes] * weight[:, lanes], axis=1, keepdims=True)
            parts.append((weight[:, lanes] * (weight_grad[:, lanes] - inner)).astype(jnp.bfloat16))
        score_grad = jnp.concatenate(parts, axis=1)
        query_grad = dot(score_grad, two_heads(key, width), NN)
        key_grads = dot(score_grad, query, TN)
        value_grads = dot(low, context_grad, TN)
        both = lambda grad: jnp.where(lane < 64, grad[:length], grad[width : width + length])
        query_low = (query_grad * score_scale).astype(jnp.bfloat16)
        key_low = (both(key_grads) * score_scale).astype(jnp.bfloat16)
        value_low = both(value_grads).astype(jnp.bfloat16)
        grads[rows, at(768 * group)] = query_low
        grads[rows, at(768 * group + 256)] = key_low
        grads[rows, at(768 * group + 512)] = value_low
        vectors[0:1, at(256 * group)] += jnp.sum(query_low.astype(jnp.float32), axis=0, keepdims=True)
        vectors[1:2, at(256 * group)] += jnp.sum(value_low.astype(jnp.float32), axis=0, keepdims=True)

    for p in range(2):
        pair(p)


def vectors_on_wire(vectors, out, low):
    lane = lax.broadcasted_iota(jnp.int32, (512, 768), 1)
    start = (lax.broadcasted_iota(jnp.int32, (512, 768), 0) >> 4) * 24
    wide = jnp.broadcast_to(vectors[:, :768][None], (32, 16, 768)).reshape(512, 768)
    wide = jnp.where((lane >= start) & (lane < start + 24), wide, 0.0).astype(jnp.bfloat16)
    rows = dot(wide, spread_table(24, 768), NT).reshape(32, 16, 128)
    lane = lax.broadcasted_iota(jnp.int32, (32, 3072), 1)
    start = lax.broadcasted_iota(jnp.int32, (32, 3072), 0) * 96
    wide = jnp.where((lane >= start) & (lane < start + 96), vectors[9:10, :], 0.0).astype(jnp.bfloat16)
    up_rows = dot(wide, spread_table(96, 3072), NT)
    number = lax.broadcasted_iota(jnp.int32, (32, 16, 128), 1)
    rows = jnp.where(number == 5, up_rows[:, None, :], rows).astype(jnp.bfloat16)
    for i in range(32):
        out[i // 8, (i // 4) % 2, (i // 2) % 2, i % 2, :16, low : low + 128] = rows[i]
        out[i // 8, (i // 4) % 2, (i // 2) % 2, i % 2, 16:, low : low + 128] = jnp.zeros((32, 128), jnp.bfloat16)


def wire_blocks(total, out, left=0, right=384, lanes=384, low=0):
    for i in range(32):
        rows = slice(24 * i, 24 * i + 24)
        both = jnp.concatenate([total[rows, left : left + lanes], total[rows, right : right + lanes]], axis=0)
        out[i // 8, (i // 4) % 2, (i // 2) % 2, i % 2, :, low : low + lanes] = both.astype(jnp.bfloat16)


def last_kernel(*refs):
    act, pre, hidden, ffn, attn, final, embed_grad, context, proj, context_grad, ps, pls, w_qkv_in = refs[:13]
    sums, x_in = refs[13:15]
    part_out, d_out, u_out, o_out, g0_out, g1_out, g2_out, p_down, p_up = refs[15:24]
    stage, p_out, p_first, p_second, p_third, slot_proj, slot_grad, slot_pl, grads, w_qkv, total, vectors, token_part, eg_held, x_ref = refs[24:39]
    work, (send, recv, local, load, fetch, away) = refs[39 : 39 + 7 * len(BACK)], refs[39 + 7 * len(BACK) :]
    groups = (p_first, p_second, p_third)
    mine = (p_down, p_up, p_out, *groups)
    down, up, out, *heads = pieces = [
        Scatter(one, BACK_CUT[i], work[7 * i : 7 * i + 7], send, recv, local, i) for i, one in enumerate(mine)
    ]
    merges, bends, closes = ([[functools.partial(getattr(one, name), d) for d in range(4)] for one in pieces] for name in ("merge", "bend", "close"))
    bends, closes = ([[rows[d] for d in (1, 2, 3, 0)] for rows in kind] for kind in (bends, closes))
    stores = (d_out, u_out, o_out, g0_out, g1_out, g2_out)
    ends = [functools.partial(one.result, store) for one, store in zip(pieces, stores)]

    s0, s1, s2, s3 = [grads.at[:, pl.ds(768 * i, 768)] for i in range(3)] + [token_part]
    halves = lambda j, slot: [
        (pre.at[:, pl.ds(384 * j, 384)], slot.at[:, pl.ds(0, 384)]),
        (pre.at[:, pl.ds(1536 + 384 * j, 384)], slot.at[:, pl.ds(384, 384)]),
    ]
    acts = lambda j, slot: [(act.at[:, pl.ds(768 * j, 768)], slot)]
    started, carried = [], []

    def bring(pairs):
        copies = []
        for source, target in pairs:
            copies.append(pltpu.make_async_copy(source, target, fetch.at[len(started)]))
            copies[-1].start()
            started.append(copies[-1])
        return copies

    def have(copies):
        for copy in copies:
            copy.wait()

    def carry(source, target):
        copy = pltpu.make_async_copy(source, target, away.at[len(carried)])
        copy.start()
        carried.append(copy)
        return copy

    ffn_here, here = bring([(ffn, s0)]), {}
    for j, slot in enumerate((s1, s2, s3)):
        here["act", j] = bring(acts(j, slot))
    eg_here = bring([(embed_grad, eg_held)])
    lanes = [(w_qkv_in.at[:, pl.ds(768 * p + 256 * g, 256)], w_qkv.at[:, pl.ds(768 * g + 256 * p, 256)]) for g in range(3) for p in range(3)]
    vectors[...] = sums[...]
    greet(*place())
    have(ffn_here)
    sent = {}
    for j, slot in enumerate((s1, s2, s3, s1)):
        have(here["act", j])
        low = dot(slot[...], s0[...], TN).astype(jnp.bfloat16)
        if j >= 2:
            sent[j - 2].wait()
        stage[j % 2] = low.reshape(2, 2, 2, 96, 768)
        sent[j] = carry(stage.at[j % 2], p_down.at[j])
        if j == 0:
            here["act", 3] = bring(acts(3, s1))
        elif j == 1:
            hidden_here = bring([(hidden, s2)])
        elif j == 2:
            here["pre", 0] = bring(halves(0, s3))
    here["pre", 1] = bring(halves(1, s0))
    here["pre", 2] = bring(halves(2, s1))
    have(hidden_here)
    hooks = iter([[], merges[0][:1], merges[0][1:], bends[0][:1]])
    for j, slot in enumerate((s3, s0, s1, s3)):
        have(here["pre", j])
        total[...] = dot(s2[...], slot[...], TN)
        if j == 0:
            sent[2].wait()
            sent[3].wait()
            down.start()
        held = groups[j % 2]
        if j >= 2:
            sent[j + 2].wait()
        wire_blocks(total, held)
        sent[4 + j] = carry(held.at[:, :, :, :, :, pl.ds(0, 384)], p_up.at[:, :, :, :, :, pl.ds(384 * j, 384)])
        if j == 0:
            here["pre", 3] = bring(halves(3, s3))
        elif j == 1:
            context_here = bring([(context, s0)])
        elif j == 2:
            attn_here = bring([(attn, s1)])
        for step in next(hooks):
            step()
    final_here = bring([(final, s2)])
    x_here = bring([(x_in, x_ref)])
    weights_here = bring(lanes)
    order = [(SHORT + 320 * s, 320, s) for s in range(4)] + [(128 * s, 128, s) for s in range(4)]
    order = [(g, *one) for g in range(3) for one in order]

    def loads(n):
        group, row, length, s = order[n]
        slot = n % 2
        rows = pl.ds(row, length)
        copies = [
            (proj.at[rows, pl.ds(768 * p + 256 * group, 256)], slot_proj.at[slot, pl.ds(0, length), pl.ds(256 * p, 256)]) for p in range(3)
        ]
        copies.append((context_grad.at[rows, pl.ds(256 * group, 256)], slot_grad.at[slot, pl.ds(0, length)]))
        source = pls if length == 320 else ps
        copies.append((source.at[s, pl.ds(2 * group, 2)], slot_pl.at[slot, :, pl.ds(0, length), pl.ds(0, 2 * padded(length))]))
        return [pltpu.make_async_copy(source, target, load.at[slot, i]) for i, (source, target) in enumerate(copies)]

    for copy in loads(0):
        copy.start()
    have(context_here)
    have(attn_here)
    total[...] = dot(s0[...], s1[...], TN)
    sent[6].wait()
    sent[7].wait()
    up.start()
    wire_blocks(total, p_out)
    for step in bends[0][1:3]:
        step()
    have(final_here)
    have(eg_here)
    total[:, :128] = dot(s2[...], eg_held[...], TN)
    wire_blocks(total, p_out, 0, 0, 128, 384)
    out.start()
    hooks = iter([
        [*bends[0][3:], merges[1][0]], merges[1][1:], [merges[2][0]], merges[2][1:], [], [], closes[0][:2], closes[0][2:], [],
        [merges[3][0], *bends[1][:1]], [*merges[3][1:], *bends[1][1:2]], bends[1][2:3], bends[1][3:], bends[2][:2], bends[2][2:], bends[3][:2], bends[3][2:], [],
        [merges[4][0], *closes[1][:1]], [*merges[4][1:], *closes[1][1:2]], closes[1][2:3], closes[1][3:], closes[2][:2], closes[2][2:], bends[4][:2], bends[4][2:], [ends[0]],
        [merges[5][0], *closes[3][:2]], [*merges[5][1:], *closes[3][2:]], closes[4][:2], [*closes[4][2:], *bends[5][:2]], bends[5][2:],
    ])

    def hook():
        for step in next(hooks):
            step()

    for n, (group, row, length, s) in enumerate(order):
        if n + 1 < len(order):
            for copy in loads(n + 1):
                copy.start()
        for copy in loads(n):
            copy.wait()
        slot = n % 2
        attend_back(slot_proj.at[slot], slot_grad.at[slot], slot_pl.at[slot], grads, vectors, row, length, group)
        hook()
        if n % 8 == 7:
            if group == 0:
                have(x_here)
            total[...] = dot(x_ref[...], grads[:, 768 * group : 768 * group + 768], TN)
            if group == 2:
                vectors_on_wire(vectors, p_third, 384)
            wire_blocks(total, groups[group])
            heads[group].start()
            hook()
    have(weights_here)
    for row, length in [(0, SHORT)] + [(SHORT + 320 * s, 320) for s in range(4)]:
        rows = pl.ds(row, length)
        token_part[rows] = dot(grads[rows], w_qkv[...], NT).astype(jnp.bfloat16)
        carry(token_part.at[rows], part_out.at[rows])
        hook()
    for step in [ends[1], *closes[5], ends[2], ends[3], ends[4], ends[5]]:
        step()
    for copy in carried[8:]:
        copy.wait()
    for piece in pieces:
        piece.drain()


def last(operands, sums, x):
    vmem, anywhere = (pl.BlockSpec(memory_space=m) for m in (pltpu.VMEM, pl.ANY))
    full = lambda *dims: jax.ShapeDtypeStruct(dims, jnp.float32)
    low = lambda *dims: jax.ShapeDtypeStruct(dims, jnp.bfloat16)
    held = lambda *dims: pltpu.VMEM(dims, jnp.bfloat16)
    semaphores = lambda *dims: pltpu.SemaphoreType.DMA(dims)
    scratch = []
    for dims, cut in zip(BACK, BACK_CUT):
        scratch += work_shapes(*dims, cut)
    return pl.pallas_call(
        last_kernel,
        out_shape=(low(ROWS, 768), *[full(*dims) for dims in BACK], *[low(4, 2, 2, 2, *dims) for dims in BACK[:2]]),
        in_specs=[anywhere] * 13 + [vmem, anywhere],
        out_specs=(anywhere,) + (vmem,) * 6 + (anywhere,) * 2,
        scratch_shapes=[held(2, 2, 2, 2, 96, 768)]
        + [held(4, 2, 2, 2, *dims) for dims in BACK[2:]]
        + [held(2, 320, 768), held(2, 320, 256), held(2, 2, 320, 768), held(ROWS, 2304), held(768, 2304)]
        + [pltpu.VMEM((768, 768), jnp.float32), pltpu.VMEM((16, 3072), jnp.float32), held(ROWS, 768), held(ROWS, P_SIZE), held(ROWS, 768)]
        + scratch
        + [semaphores(SUMS * len(BACK)), semaphores(SUMS * len(BACK)), semaphores(len(BACK)), semaphores(2, 5), semaphores(32), semaphores(16)],
        compiler_params=pltpu.CompilerParams(collective_id=1, has_side_effects=True, vmem_limit_bytes=63 * 2**20),
    )(*operands, sums, x)[:7]


def finish_kernel(resid, part, d, u, o, g0, g1, g2, gs, gl, q_out, k_out, v_out, o_out, u_out, d_out, e_out, *vectors):
    tile = pl.program_id(0)
    value = resid[...] + part[...].astype(jnp.float32)

    @pl.when(tile < 2)
    def _():
        gs[...] = value

    @pl.when(tile >= 2)
    def _():
        gl[...] = value

    @pl.when(tile == 0)
    def _():
        d_out[...] = d[...]
        for wire, target, half in ((u, u_out, 1536), (o, o_out, 384)):
            target[:, :half] = wire[:24, :half]
            target[:, half:] = wire[24:, :half]
        e_out[...] = o[:24, 384:]
        for g, wire in enumerate((g0, g1, g2)):
            low = 256 * g
            q_out[:, low : low + 256] = wire[:24, :256]
            k_out[:, low : low + 128] = wire[:24, 256:384]
            k_out[:, low + 128 : low + 256] = wire[24:, :128]
            v_out[:, low : low + 256] = wire[24:, 128:384]
        for i, target in enumerate(vectors):
            width = target.shape[0]
            target[...] = g2[i : i + 1, 384 : 384 + width].reshape(width)


def finish(resid, part, wires, shards):
    tile = 256
    full = lambda *dims: jax.ShapeDtypeStruct(dims, jnp.float32)
    every = pl.BlockSpec((tile, 768), lambda i: (i, 0))
    whole = lambda one: pl.BlockSpec(one.shape, lambda i: (0,) * one.ndim)
    cut = SHORT // tile
    query, key, value, out, up, down, embed, *vectors = shards
    return pl.pallas_call(
        finish_kernel,
        grid=(ROWS // tile,),
        out_shape=(full(SHORT, 768), full(ROWS - SHORT, 768), *[full(*one.shape) for one in shards]),
        in_specs=[every, every] + [whole(one) for one in wires],
        out_specs=(
            pl.BlockSpec((tile, 768), lambda i: (jnp.minimum(i, cut - 1), 0)),
            pl.BlockSpec((tile, 768), lambda i: (jnp.maximum(i - cut, 0), 0)),
            *[whole(one) for one in shards],
        ),
        compiler_params=pltpu.CompilerParams(vmem_limit_bytes=62 * 2**20),
    )(resid, part, *wires)


def fast_body(xs, len_short, xl, len_long, shards, cs, cl):
    flat = lambda one: one.reshape(-1, one.shape[-1])
    w_qkv, w_out, w_up, w_embed, w_down, vec, proj, context, ps, pls, x, cot = first(
        len_short, len_long, flat(xs), flat(xl), flat(cs), flat(cl), shards
    )
    es, el, act, pre, hidden, ffn, attn, final, embed_grad, resid, context_grad, sums = token_chain(
        len_short, len_long, x, cot, context, w_out, w_up, w_down.reshape(3072, 768), w_embed, vec
    )
    part, *wires = last((act, pre, hidden, ffn, attn, final, embed_grad, context, proj, context_grad, ps, pls, w_qkv), sums, x)
    gs, gl, *owned = finish(resid, part, wires, shards)
    shaped = lambda value, like: value.reshape(*like.shape[:2], -1)
    return (shaped(es, xs), shaped(el, xl), shaped(gs, xs), shaped(gl, xl), *owned)


def body(tokens_short, lengths_short, tokens_long, lengths_long, *rest):
    shards, (cotangent_short, cotangent_long) = rest[:16], rest[16:]
    weights = tuple(lax.all_gather(one, BOTH, axis=0, tiled=True) for one in shards)
    embed_short, saved_short = forward(tokens_short, lengths_short, weights)
    embed_long, saved_long = forward(tokens_long, lengths_long, weights)
    input_short, grads_short = backward(saved_short, weights, cotangent_short)
    input_long, grads_long = backward(saved_long, weights, cotangent_long)
    totals = jax.tree.map(jnp.add, grads_short, grads_long)
    owned = tuple(lax.psum_scatter(one, BOTH, scatter_dimension=0, tiled=True) for one in totals)
    return (embed_short, embed_long, input_short, input_long, *owned)


def solution(mesh):
    split = lambda rank: P(BOTH, *([None] * (rank - 1)))
    weights = [split(2)] * 7 + [split(1)] * 9
    in_specs = (split(3), split(1), split(3), split(1), *weights, split(3), split(3))
    out_specs = (split(3),) * 4 + tuple(weights)
    fast = mesh.shape["wide"] == 16 and mesh.shape["narrow"] == 2

    def step(xs, len_short, xl, len_long, *rest):
        if fast:
            return fast_body(xs, len_short, xl, len_long, rest[:16], *rest[16:])
        return body(xs, len_short, xl, len_long, *rest)

    return jax.shard_map(step, mesh=mesh, in_specs=in_specs, out_specs=out_specs, check_vma=False)
```

```python
import functools
import math

import jax
import jax.numpy as jnp
from jax import lax
from jax.experimental import pallas as pl
from jax.experimental.pallas import tpu as pltpu
from jax.sharding import PartitionSpec as P

MESH = pl.DeviceIdType.MESH

HD = 64
P_SIZE = 128


norm_epsilon = 1e-12
unit_epsilon = 1e-06
masked_fill = -1000000000.0


def layer_norm(residual, norm_gain, norm_shift):
    center = residual - jnp.mean(residual, axis=-1, keepdims=True)
    variance = jnp.mean(center * center, axis=-1, keepdims=True)
    return center * lax.rsqrt(variance + norm_epsilon) * norm_gain + norm_shift


def gelu_exact(pre_act):
    return 0.5 * pre_act * (1.0 + lax.erf(pre_act * (1.0 / math.sqrt(2.0))))


def normalize(embedding, token_mask):
    squares = jnp.sum(embedding * embedding, axis=-1, keepdims=True)
    return math.sqrt(P_SIZE) * embedding * lax.rsqrt(squares + unit_epsilon) * token_mask[..., None]


def soft_weights(scaled, key_mask):
    masked = jnp.where(key_mask, scaled, masked_fill)
    row_peak = jnp.max(masked, axis=-1, keepdims=True)
    exponent = jnp.exp(masked - row_peak)
    return exponent / jnp.sum(exponent, axis=-1, keepdims=True)


def matmul(left_side, right_side, form):
    return jnp.einsum(form, left_side, right_side, preferred_element_type=jnp.float32)


def forward(tokens, lengths, full_weights):
    (
        query_weight,
        key_weight,
        value_weight,
        out_weight,
        up_weight,
        down_weight,
        embed_weight,
        query_bias,
        value_bias,
        out_bias,
        attention_gain,
        attention_shift,
        up_bias,
        down_bias,
        final_gain,
        final_shift,
    ) = full_weights
    seq_count, length, model_width = tokens.shape
    head_count = model_width // HD
    score_scale = 1.0 / math.sqrt(HD)
    positions = jnp.arange(length, dtype=jnp.int32)
    token_mask = (positions[None, :] < lengths[:, None]).astype(jnp.float32)
    key_mask = token_mask[:, None, None, :] > 0.5
    query_low = (matmul(tokens, query_weight, "bld,de->ble") + query_bias).astype(jnp.bfloat16)
    query_low = query_low.reshape(seq_count, length, head_count, HD)
    key_low = matmul(tokens, key_weight, "bld,de->ble").astype(jnp.bfloat16)
    key_low = key_low.reshape(seq_count, length, head_count, HD)
    value_low = (matmul(tokens, value_weight, "bld,de->ble") + value_bias).astype(jnp.bfloat16)
    value_low = value_low.reshape(seq_count, length, head_count, HD)
    raw_scores = matmul(query_low, key_low, "bqhe,bkhe->bhqk") * score_scale
    attn_probs = soft_weights(raw_scores, key_mask)
    probs_low = attn_probs.astype(jnp.bfloat16)
    context_low = matmul(probs_low, value_low, "bhqk,bkhe->bqhe")
    context_low = context_low.reshape(seq_count, length, model_width).astype(jnp.bfloat16)
    attn_out = matmul(context_low, out_weight, "bld,de->ble") + out_bias
    resid_one = tokens.astype(jnp.float32) + attn_out
    normed_one = layer_norm(resid_one, attention_gain, attention_shift)
    hidden_low = normed_one.astype(jnp.bfloat16)
    pre_act = matmul(hidden_low, up_weight, "bld,df->blf") + up_bias
    act_low = gelu_exact(pre_act).astype(jnp.bfloat16)
    ffn_out = matmul(act_low, down_weight, "blf,fd->bld") + down_bias
    resid_two = normed_one + ffn_out
    final_low = layer_norm(resid_two, final_gain, final_shift).astype(jnp.bfloat16)
    embedding = matmul(final_low, embed_weight, "bld,dp->blp")
    result = normalize(embedding, token_mask)
    saved = (
        tokens,
        token_mask,
        query_low,
        key_low,
        value_low,
        attn_probs,
        probs_low,
        context_low,
        resid_one,
        hidden_low,
        pre_act,
        act_low,
        resid_two,
        final_low,
        embedding,
    )
    return (result, saved)


def backward(saved, full_weights, cotangent):
    (
        tokens,
        token_mask,
        query_low,
        key_low,
        value_low,
        attn_probs,
        probs_low,
        context_low,
        resid_one,
        hidden_low,
        pre_act,
        act_low,
        resid_two,
        final_low,
        embedding,
    ) = saved
    (
        query_weight,
        key_weight,
        value_weight,
        out_weight,
        up_weight,
        down_weight,
        embed_weight,
        query_bias,
        value_bias,
        out_bias,
        attention_gain,
        attention_shift,
        up_bias,
        down_bias,
        final_gain,
        final_shift,
    ) = full_weights
    seq_count, length, model_width = tokens.shape
    score_scale = 1.0 / math.sqrt(HD)
    _, pull_norm = jax.vjp(lambda vector: normalize(vector, token_mask), embedding)
    (embed_grad,) = pull_norm(cotangent.astype(jnp.float32))
    embed_low = embed_grad.astype(jnp.bfloat16)
    grad_embed = matmul(final_low, embed_low, "bld,blp->dp")
    final_grad = matmul(embed_low, embed_weight, "blp,dp->bld")
    _, pull_two = jax.vjp(
        layer_norm, resid_two, final_gain.astype(jnp.float32), final_shift.astype(jnp.float32)
    )
    resid_two_grad, grad_final_gain, grad_final_shift = pull_two(final_grad)
    ffn_low = resid_two_grad.astype(jnp.bfloat16)
    grad_down_bias = jnp.sum(ffn_low, axis=(0, 1), dtype=jnp.float32)
    grad_down = matmul(act_low, ffn_low, "blf,bld->fd")
    act_grad = matmul(ffn_low, down_weight, "bld,fd->blf")
    _, pull_gelu = jax.vjp(gelu_exact, pre_act)
    (pre_grad,) = pull_gelu(act_grad)
    pre_low = pre_grad.astype(jnp.bfloat16)
    grad_up_bias = jnp.sum(pre_low, axis=(0, 1), dtype=jnp.float32)
    grad_up = matmul(hidden_low, pre_low, "bld,blf->df")
    normed_grad = resid_two_grad + matmul(pre_low, up_weight, "blf,df->bld")
    _, pull_one = jax.vjp(
        layer_norm,
        resid_one,
        attention_gain.astype(jnp.float32),
        attention_shift.astype(jnp.float32),
    )
    resid_one_grad, grad_attention_gain, grad_attention_shift = pull_one(normed_grad)
    attn_low = resid_one_grad.astype(jnp.bfloat16)
    grad_out_bias = jnp.sum(attn_low, axis=(0, 1), dtype=jnp.float32)
    grad_out = matmul(context_low, attn_low, "bld,ble->de")
    context_grad = matmul(attn_low, out_weight, "ble,de->bld").astype(jnp.bfloat16)
    context_grad = context_grad.reshape(seq_count, length, -1, HD)
    value_grad = matmul(probs_low, context_grad, "bhqk,bqhe->bkhe")
    probs_grad = matmul(context_grad, value_low, "bqhe,bkhe->bhqk")
    score_low = attn_probs * (probs_grad - jnp.sum(probs_grad * attn_probs, axis=-1, keepdims=True))
    score_low = score_low.astype(jnp.bfloat16)
    query_grad = (matmul(score_low, key_low, "bhqk,bkhe->bqhe") * score_scale).astype(jnp.bfloat16)
    query_grad = query_grad.reshape(seq_count, length, model_width)
    key_grad = (matmul(score_low, query_low, "bhqk,bqhe->bkhe") * score_scale).astype(jnp.bfloat16)
    key_grad = key_grad.reshape(seq_count, length, model_width)
    value_grad_low = value_grad.astype(jnp.bfloat16).reshape(seq_count, length, model_width)
    grad_query_bias = jnp.sum(query_grad, axis=(0, 1), dtype=jnp.float32)
    grad_value_bias = jnp.sum(value_grad_low, axis=(0, 1), dtype=jnp.float32)
    grad_query = matmul(tokens, query_grad, "bld,ble->de")
    grad_key = matmul(tokens, key_grad, "bld,ble->de")
    grad_value = matmul(tokens, value_grad_low, "bld,ble->de")
    input_grad = (
        resid_one_grad
        + matmul(query_grad, query_weight, "ble,de->bld")
        + matmul(key_grad, key_weight, "ble,de->bld")
        + matmul(value_grad_low, value_weight, "ble,de->bld")
    )
    gradients = (
        grad_query,
        grad_key,
        grad_value,
        grad_out,
        grad_up,
        grad_down,
        grad_embed,
        grad_query_bias,
        grad_value_bias,
        grad_out_bias,
        grad_attention_gain,
        grad_attention_shift,
        grad_up_bias,
        grad_down_bias,
        grad_final_gain,
        grad_final_shift,
    )
    return (input_grad, gradients)


BOTH = ("wide", "narrow")
WIRE = ((48, 512), (48, 768), (48, 512), (48, 1536), (96, 768))
CUT = (256, 384, 256, 768, 384)
ROWS = 1792
SHORT = 512
COPIES = 39


def place():
    wide = lax.axis_index("wide")
    return wide // 4, (wide // 2) % 2, wide % 2, lax.axis_index("narrow")


def greet(z, y, c, x):
    partners = [device((z + d) % 4, y, c, x) for d in (1, 2, 3)]
    partners += [device(z, 1 - y, c, x), device(z, y, 1 - c, x), device(z, y, c, 1 - x)]
    barrier = pltpu.get_barrier_semaphore()
    for partner in partners:
        pl.semaphore_signal(barrier, inc=1, device_id=partner, device_id_type=MESH)
    pl.semaphore_wait(barrier, len(partners))


def device(z, y, c, x):
    return (z * 4 + y * 2 + c, x)


class Lazy:
    def __init__(self, make):
        self.make = make

    def __getitem__(self, way):
        return self.make(way)


class Gather:
    def __init__(self, held, cut, send, recv, first):
        self.held, self.cut, self.send, self.recv, self.first = held, cut, send, recv, first
        self.z, self.y, self.c, self.x = place()

    def view(self, block, half):
        if half is None:
            return self.held.at[block]
        lanes = self.held.shape[-1]
        low, size = ((0, self.cut), (self.cut, lanes - self.cut))[half]
        return self.held.at[(*block, slice(None), pl.ds(low, size))]

    def plan(self, slot, out, into, half, target):
        def copy(block):
            return pltpu.make_async_remote_copy(
                src_ref=self.view(block, half),
                dst_ref=self.view(block, half),
                send_sem=self.send.at[self.first + slot],
                recv_sem=self.recv.at[self.first + slot],
                device_id=target,
                device_id_type=MESH,
            )

        return Lazy(lambda way: copy((out, into)[way]))

    def along_z(self, d):
        z, y, c, x = self.z, self.y, self.c, self.x
        return self.plan(d - 1, (z, y, c, x), ((z + 4 - d) % 4, y, c, x), None, device((z + d) % 4, y, c, x))

    def to_x(self, d):
        z, y, c, x = (self.z + 4 - d) % 4, self.y, self.c, self.x
        return self.plan(3 + d, (z, y, c, x), (z, y, c, 1 - x), None, device(self.z, y, c, 1 - x))

    def to_y(self, d):
        z, y, c, x = (self.z + 4 - d) % 4, self.y, self.c, self.x
        return self.plan(7 + d, (z, y, c, x), (z, 1 - y, c, x), None, device(self.z, 1 - y, c, x))

    def corner(self, d, half):
        z, y, c, x = (self.z + 4 - d) % 4, self.y, self.c, self.x
        if half == 0:
            return self.plan(11 + d, (z, y, c, 1 - x), (z, 1 - y, c, 1 - x), 0, device(self.z, 1 - y, c, x))
        return self.plan(15 + d, (z, 1 - y, c, x), (z, 1 - y, c, 1 - x), 1, device(self.z, y, c, 1 - x))

    def to_core(self, d, kind):
        z, c = (self.z + 4 - d) % 4, self.c
        y = 1 - self.y if kind >= 2 else self.y
        x = 1 - self.x if kind in (1, 3, 4) else self.x
        half = kind - 3 if kind >= 3 else None
        return self.plan(19 + 4 * kind + d, (z, y, c, x), (z, y, 1 - c, x), half, device(self.z, self.y, 1 - c, self.x))

    def start_z(self):
        for d in (1, 2, 3):
            self.along_z(d)[0].start()

    def spread(self, d):
        self.to_x(d)[0].start()
        self.to_y(d)[0].start()
        self.to_core(d, 0)[0].start()

    def column(self, d):
        self.along_z(d)[1].wait_recv()
        self.spread(d)

    def turn(self, d):
        self.to_x(d)[1].wait_recv()
        self.corner(d, 0)[0].start()
        self.to_core(d, 1)[0].start()
        self.to_y(d)[1].wait_recv()
        self.corner(d, 1)[0].start()
        self.to_core(d, 2)[0].start()

    def finish(self, d):
        for half in (0, 1):
            self.corner(d, half)[1].wait_recv()
            self.to_core(d, 3 + half)[0].start()

    def arrive(self):
        for d in range(4):
            for kind in range(5):
                self.to_core(d, kind)[1].wait_recv()

    def drain(self):
        for d in range(4):
            if d:
                self.along_z(d)[0].wait_send()
            self.to_x(d)[0].wait_send()
            self.to_y(d)[0].wait_send()
            for half in (0, 1):
                self.corner(d, half)[0].wait_send()
            for kind in range(5):
                self.to_core(d, kind)[0].wait_send()


def stack_halves(whole):
    half = whole.shape[1] // 2
    return jnp.concatenate([whole[:, :half], whole[:, half:]], axis=0).astype(jnp.bfloat16)


def unpack_rows(held, targets):
    def pair(p, carry):
        z, y, c = p // 4, (p // 2) % 2, p % 2
        one, two = held[z, y, c, 0].astype(jnp.float32), held[z, y, c, 1].astype(jnp.float32)
        for side, low, ref, column, lanes in targets:
            rows = slice(24 * side, 24 * side + 24)
            both = jnp.concatenate([one[rows, low : low + lanes], two[rows, low : low + lanes]], axis=0)
            ref[pl.ds(pl.multiple_of(p * 48, 48), 48), column : column + lanes] = both.astype(jnp.bfloat16)
        return carry

    lax.fori_loop(0, 16, pair, 0)


NN = (((1,), (0,)), ((), ()))
NT = (((1,), (1,)), ((), ()))
TN = (((0,), (0,)), ((), ()))


def dot(left, right, dims):
    return lax.dot_general(left, right, dims, preferred_element_type=jnp.float32)


def padded(length):
    return -(-length // 128) * 128


def two_heads(pair, width):
    length = pair.shape[0]
    lane = lax.broadcasted_iota(jnp.int32, (length, 128), 1)
    parts = []
    for here in (lane < 64, lane >= 64):
        parts.append(jnp.where(here, pair, jnp.bfloat16(0)))
        if width > length:
            parts.append(jnp.zeros((width - length, 128), jnp.bfloat16))
    return jnp.concatenate(parts, axis=0)


def attend(qkv, context, probs, row, length, valid, first, last):
    rows = pl.ds(row, length)
    width = padded(length)
    fill = jnp.where(lax.broadcasted_iota(jnp.int32, (1, width), 1) < valid, 0.0, masked_fill)

    def pair(p):
        at = lambda base: pl.ds(base + p * 128, 128)
        query = qkv[rows, at(0)] * jnp.bfloat16(1.0 / math.sqrt(HD))
        key, value = qkv[rows, at(768)], qkv[rows, at(1536)]
        scores = dot(query, two_heads(key, width), NT)
        parts = []
        for h in (0, 1):
            masked = scores[:, width * h : width * h + width] + fill
            exponent = jnp.exp(masked - jnp.max(masked, axis=1, keepdims=True))
            scale = 1.0 / jnp.sum(exponent, axis=1, keepdims=True)
            parts.append((exponent * scale).astype(jnp.bfloat16))
        low = jnp.concatenate(parts, axis=1)
        probs[p] = low
        context[rows, at(0)] = dot(low, two_heads(value, width), NN).astype(jnp.bfloat16)

    for p in range(first, last):
        pair(p)


def spread_table(group, lanes):
    lane = lax.broadcasted_iota(jnp.int32, (128, lanes), 1).astype(jnp.float32)
    row = lax.broadcasted_iota(jnp.int32, (128, lanes), 0).astype(jnp.float32)
    return (lane - group * jnp.floor((lane + 0.5) * (1.0 / group)) == row).astype(jnp.bfloat16)


def natural_vectors(held, vec_out):
    blocks = [held[p // 8, (p // 4) % 2, (p // 2) % 2, p % 2, :16, 384:512] for p in range(32)]
    stacked = jnp.concatenate(blocks, axis=0)
    wide = dot(stacked, spread_table(24, 768), NN)
    lane = lax.broadcasted_iota(jnp.int32, (512, 768), 1)
    start = (lax.broadcasted_iota(jnp.int32, (512, 768), 0) >> 4) * 24
    wide = jnp.where((lane >= start) & (lane < start + 24), wide, 0.0)
    vec_out[:, :768] = jnp.sum(wide.reshape(32, 16, 768), axis=0)
    picked = dot(
        (lax.broadcasted_iota(jnp.int32, (32, 512), 1) == lax.broadcasted_iota(jnp.int32, (32, 512), 0) * 16 + 5).astype(jnp.bfloat16),
        stacked,
        NN,
    ).astype(jnp.bfloat16)
    wide = dot(picked, spread_table(96, 3072), NN)
    lane = lax.broadcasted_iota(jnp.int32, (32, 3072), 1)
    start = lax.broadcasted_iota(jnp.int32, (32, 3072), 0) * 96
    wide = jnp.where((lane >= start) & (lane < start + 96), wide, 0.0)
    vec_out[9:10, :] = jnp.sum(wide, axis=0, keepdims=True)


def first_kernel(
    len_short, len_long, xs, xl, cs, cl, q_ref, k_ref, v_ref, o_ref, u_ref, d_ref, e_ref, *rest
):
    vec_refs, rest = rest[:9], rest[9:]
    (qkv_out, out_out, up_out, embed_out, down_out, vec_out, proj_out, context_out, ps_out, pl_out, x_out, c_out), rest = rest[:12], rest[12:]
    h0, h1, h2, h3, h4, w_qkv, w_out, w_up, w_embed, proj, context, ps, pls, rows, send, recv, away = rest
    z, y, c, x = place()
    rows[...] = jnp.zeros_like(rows)
    for i, ref in enumerate(vec_refs):
        width = ref.shape[0]
        rows[i : i + 1, :width] = ref[...].astype(jnp.float32).reshape(1, width)
    wide = lambda ref: ref[...].astype(jnp.float32)
    h0[z, y, c, x, :, :384] = stack_halves(wide(q_ref))
    h0[z, y, c, x, :, 384:] = rows[...].astype(jnp.bfloat16)
    h1[z, y, c, x, :, :384] = stack_halves(wide(k_ref))
    h1[z, y, c, x, :, 384:] = stack_halves(wide(v_ref))
    h2[z, y, c, x, :, :384] = stack_halves(wide(o_ref))
    h2[z, y, c, x, :, 384:] = jnp.concatenate([wide(e_ref), wide(e_ref)], axis=0).astype(jnp.bfloat16)
    h3[z, y, c, x] = stack_halves(wide(u_ref))
    h4[z, y, c, x] = d_ref[...]
    greet(z, y, c, x)
    one, two, three, four, five = gathers = [Gather(h, CUT[i], send, recv, COPIES * i) for i, h in enumerate((h0, h1, h2, h3, h4))]
    for piece in gathers:
        piece.start_z()
    for piece in gathers:
        piece.spread(0)
    kept = []

    def keep(source, target):
        copy = pltpu.make_async_copy(source, target, away.at[len(kept)])
        copy.start()
        kept.append(copy)

    for source, target, low in ((xs, x_out, 0), (xl, x_out, SHORT), (cs, c_out, 0), (cl, c_out, SHORT)):
        keep(source, target.at[pl.ds(low, source.shape[0])])
    for d in (1, 2, 3):
        one.column(d)
    for d in (1, 2, 3):
        two.column(d)
    for d in range(4):
        one.turn(d)
    for d in (1, 2, 3):
        three.column(d)
    for d in range(4):
        two.turn(d)
    for d in range(4):
        one.finish(d)
    for d in (1, 2, 3):
        four.column(d)
    one.arrive()
    unpack_rows(h0, [(0, 0, w_qkv, 0, 384), (1, 0, w_qkv, 384, 384)])
    natural_vectors(h0, vec_out)
    for d in range(4):
        two.finish(d)
    step = lambda name, piece, *ds: [functools.partial(getattr(piece, name), d) for d in ds]
    hooks = iter([
        step("turn", three, 0, 1) + step("turn", four, 0) + step("turn", five, 0),
        step("turn", three, 2, 3) + step("turn", four, 1), step("finish", three, 0, 1) + step("column", five, 1),
        step("column", five, 2), step("column", five, 3), step("turn", four, 2), step("turn", four, 3),
        step("finish", three, 2, 3), step("finish", four, 0, 1), step("turn", five, 1), step("turn", five, 2),
        step("turn", five, 3), step("finish", four, 2, 3), step("finish", five, 0), step("finish", five, 1),
    ])

    def hook():
        for one_step in next(hooks):
            one_step()

    tiles = [(0, xs[...])] + [(SHORT + 320 * s, xl[320 * s : 320 * s + 320]) for s in range(4)]
    for part in range(3):
        if part == 1:
            two.arrive()
            unpack_rows(h1, [(0, 0, w_qkv, 768, 384), (1, 0, w_qkv, 1152, 384), (0, 384, w_qkv, 1536, 384), (1, 384, w_qkv, 1920, 384)])
            keep(w_qkv, qkv_out)
        lanes = slice(768 * part, 768 * part + 768)
        for row, tokens in tiles:
            result = dot(tokens, w_qkv[:, lanes], NN)
            if part != 1:
                result = result + vec_out[part // 2 : part // 2 + 1, :768]
            proj[row : row + tokens.shape[0], lanes] = result.astype(jnp.bfloat16)
        hook()
    keep(proj, proj_out)
    for s in range(4):
        attend(proj, context, ps.at[s], 128 * s, 128, len_short[s], 0, 6)
        hook()
    keep(ps, ps_out)
    slots = []
    for s in range(4):
        if s >= 2:
            slots[s - 2].wait()
        for part in (0, 3):
            attend(proj, context, pls.at[s % 2], SHORT + 320 * s, 320, len_long[s], part, part + 3)
            hook()
        copy = pltpu.make_async_copy(pls.at[s % 2], pl_out.at[s], away.at[12 + s])
        copy.start()
        slots.append(copy)
        if s == 1:
            three.arrive()
            unpack_rows(h2, [(0, 0, w_out, 0, 384), (1, 0, w_out, 384, 384), (0, 384, w_embed, 0, 128)])
            keep(w_out, out_out)
            keep(w_embed, embed_out)
    keep(context, context_out)
    four.arrive()
    unpack_rows(h3, [(0, 0, w_up, 0, 1536), (1, 0, w_up, 1536, 1536)])
    keep(w_up, up_out)
    for d in (2, 3):
        five.finish(d)
    five.arrive()
    keep(h4, down_out)
    for copy in kept + slots[2:]:
        copy.wait()
    for piece in gathers:
        piece.drain()


def first(len_short, len_long, xs, xl, cs, cl, shards):
    vmem, smem, anywhere = (pl.BlockSpec(memory_space=m) for m in (pltpu.VMEM, pltpu.SMEM, pl.ANY))
    low = lambda *dims: jax.ShapeDtypeStruct(dims, jnp.bfloat16)
    held = lambda *dims: pltpu.VMEM(dims, jnp.bfloat16)
    semaphores = lambda count: pltpu.SemaphoreType.DMA((count,))
    weights = [(768, 2304), (768, 768), (768, 3072), (768, 128)]
    return pl.pallas_call(
        first_kernel,
        out_shape=(
            *[low(*dims) for dims in weights], low(4, 2, 2, 2, *WIRE[4]),
            jax.ShapeDtypeStruct((16, 3072), jnp.float32),
            low(ROWS, 2304), low(ROWS, 768), low(4, 6, 128, 256), low(4, 6, 320, 768), low(ROWS, 768), low(ROWS, P_SIZE),
        ),
        in_specs=[smem] * 2 + [vmem] * 2 + [anywhere] * 2 + [vmem] * 16,
        out_specs=(anywhere,) * 5 + (vmem,) + (anywhere,) * 6,
        scratch_shapes=[held(4, 2, 2, 2, *dims) for dims in WIRE]
        + [held(*dims) for dims in weights]
        + [held(ROWS, 2304), held(ROWS, 768), held(4, 6, 128, 256), held(2, 6, 320, 768), pltpu.VMEM((48, 128), jnp.float32)]
        + [semaphores(COPIES * 5), semaphores(COPIES * 5), semaphores(16)],
        compiler_params=pltpu.CompilerParams(collective_id=0, has_side_effects=True, vmem_limit_bytes=62 * 2**20),
    )(len_short, len_long, xs, xl, cs, cl, *shards)


TILE = 448
PART = 224


def center(value):
    return value - jnp.mean(value, axis=1, keepdims=True)


def normal(value):
    value = center(value)
    scale = lax.rsqrt(jnp.mean(value * value, axis=1, keepdims=True) + norm_epsilon)
    return value * scale, scale


def normal_back(grad, unit, scale):
    inner = jnp.mean(grad * unit, axis=1, keepdims=True)
    return scale * (center(grad) - unit * inner)


def embed_copies(step, embedded, es_out, el_out, away):
    low, high = TILE * step, TILE * step + TILE
    cut = min(max(SHORT, low), high)
    copies = []
    if low < cut:
        copies.append((embedded.at[pl.ds(0, cut - low)], es_out.at[pl.ds(low, cut - low)]))
    if cut < high:
        copies.append((embedded.at[pl.ds(cut - low, high - cut)], el_out.at[pl.ds(cut - SHORT, high - cut)]))
    return [pltpu.make_async_copy(source, target, away.at[i]) for i, (source, target) in enumerate(copies)]


def token_kernel(
    len_short, len_long, x_ref, cot_ref, ctx_ref, w_out, w_up, w_down, w_embed, vec,
    es_out, el_out, act_out, pre_out, hidden_out, ffn_out, attn_out, final_out, eg_out, resid_out, cg_out, sums,
    slope, embedded, away,
):
    tile = pl.program_id(0)
    row = lambda k: vec[k : k + 1, :768]
    low = lambda value: value.astype(jnp.bfloat16)
    wide = lambda value: value.astype(jnp.float32)

    @pl.when(tile == 0)
    def _():
        sums[...] = jnp.zeros_like(sums)

    def add(k, value):
        sums[k : k + 1, : value.shape[1]] += jnp.sum(value, axis=0, keepdims=True)

    def chain(start):
        rows = slice(start, start + PART)
        mixed = wide(x_ref[rows]) + (dot(ctx_ref[rows], w_out[...], NN) + row(2))
        yield
        unit_one, scale_one = normal(mixed)
        normed_one = unit_one * row(3) + row(4)
        hidden = low(normed_one)
        hidden_out[rows] = hidden
        ffn = None
        for f in range(4):
            lanes = slice(768 * f, 768 * f + 768)
            pre = dot(hidden, w_up[:, lanes], NN) + vec[9:10, lanes]
            cdf = 0.5 + 0.5 * lax.erf(pre * (1.0 / math.sqrt(2.0)))
            act = low(pre * cdf)
            act_out[rows, lanes] = act
            slope[rows, lanes] = cdf + pre * (jnp.exp(-0.5 * pre * pre) * (1.0 / math.sqrt(2.0 * math.pi)))
            part = dot(act, w_down[lanes, :], NN)
            ffn = part if ffn is None else ffn + part
        yield
        unit_two, scale_two = normal(normed_one + (ffn + row(6)))
        final = low(unit_two * row(7) + row(8))
        final_out[rows] = final
        embedding = dot(final, w_embed[...], NN)
        inverse = lax.rsqrt(jnp.sum(embedding * embedding, axis=1, keepdims=True) + unit_epsilon)
        at = lax.broadcasted_iota(jnp.int32, (PART, 1), 0) + (tile * TILE + start)
        mask = jnp.zeros((PART, 1), jnp.float32)
        for sizes, low_row, stride in ((len_short, 0, 128), (len_long, SHORT, 320)):
            for s in range(4):
                begin = low_row + s * stride
                mask = mask + jnp.where((at >= begin) & (at < begin + sizes[s]), 1.0, 0.0)
        embedded[rows] = math.sqrt(P_SIZE) * embedding * inverse * mask
        grad = wide(cot_ref[rows]) * mask
        inner = jnp.sum(grad * embedding, axis=1, keepdims=True)
        embed_grad = low(math.sqrt(P_SIZE) * inverse * (grad - inverse * inverse * embedding * inner))
        eg_out[rows] = embed_grad
        final_grad = dot(embed_grad, w_embed[...], NT)
        yield
        add(7, final_grad * unit_two)
        add(8, final_grad)
        resid_two = normal_back(final_grad * row(7), unit_two, scale_two)
        ffn_grad = low(resid_two)
        ffn_out[rows] = ffn_grad
        add(6, wide(ffn_grad))
        normed_grad = resid_two
        for f in range(4):
            lanes = slice(768 * f, 768 * f + 768)
            pre_grad = low(dot(ffn_grad, w_down[lanes, :], NT) * slope[rows, lanes])
            pre_out[rows, lanes] = pre_grad
            sums[9:10, lanes] += jnp.sum(wide(pre_grad), axis=0, keepdims=True)
            normed_grad = normed_grad + dot(pre_grad, w_up[:, lanes], NT)
        yield
        add(3, normed_grad * unit_one)
        add(4, normed_grad)
        resid_one = normal_back(normed_grad * row(3), unit_one, scale_one)
        resid_out[rows] = resid_one
        attn_grad = low(resid_one)
        attn_out[rows] = attn_grad
        add(2, wide(attn_grad))
        cg_out[rows] = low(dot(attn_grad, w_out[...], NT))
        yield

    chains = [chain(start) for start in range(0, TILE, PART)]
    for _ in range(5):
        for one in chains:
            next(one)

    def embeds(act):
        for step in range(ROWS // TILE):

            @pl.when(tile == step)
            def _():
                for copy in embed_copies(step, embedded, es_out, el_out, away):
                    getattr(copy, act)()

    embeds("start")
    embeds("wait")


def token_chain(len_short, len_long, x, cot, context, w_out, w_up, w_down, w_embed, vec):
    smem, anywhere = pl.BlockSpec(memory_space=pltpu.SMEM), pl.BlockSpec(memory_space=pl.ANY)
    every = lambda lanes: pl.BlockSpec((TILE, lanes), lambda i: (i, 0))
    whole = lambda array: pl.BlockSpec(array.shape, lambda i: (0, 0), pipeline_mode=pl.Buffered(1))
    shape = lambda kind, *dims: jax.ShapeDtypeStruct(dims, kind)
    low = lambda lanes: shape(jnp.bfloat16, ROWS, lanes)
    return pl.pallas_call(
        token_kernel,
        grid=(ROWS // TILE,),
        out_shape=(
            shape(jnp.float32, SHORT, P_SIZE), shape(jnp.float32, ROWS - SHORT, P_SIZE),
            low(3072), low(3072), low(768), low(768), low(768), low(768), low(P_SIZE),
            shape(jnp.float32, ROWS, 768), low(768), shape(jnp.float32, 16, 3072),
        ),
        in_specs=[smem, smem, every(768), every(P_SIZE), every(768)] + [whole(one) for one in (w_out, w_up, w_down, w_embed, vec)],
        out_specs=(
            anywhere, anywhere, every(3072), every(3072), every(768), every(768), every(768), every(768), every(P_SIZE),
            every(768), every(768), pl.BlockSpec((16, 3072), lambda i: (0, 0)),
        ),
        scratch_shapes=[pltpu.VMEM((TILE, 3072), jnp.float32), pltpu.VMEM((TILE, P_SIZE), jnp.float32), pltpu.SemaphoreType.DMA((2,))],
        compiler_params=pltpu.CompilerParams(vmem_limit_bytes=62 * 2**20),
    )(len_short, len_long, x, cot, context, w_out, w_up, w_down, w_embed, vec)


class Scatter:
    def __init__(self, mine, cut, work, send, recv, local, number):
        self.mine, self.cut, self.send, self.recv, self.first = mine, cut, send, recv, SUMS * number
        self.core_in, self.total, self.corner_y, self.corner_x, self.from_x, self.from_y, self.from_z = work
        self.z, self.y, self.c, self.x = place()
        self.own = pltpu.make_async_copy(mine.at[:, :, self.c], self.total, local.at[number])

    def copy(self, slot, source, target, partner):
        return pltpu.make_async_remote_copy(
            src_ref=source,
            dst_ref=target,
            send_sem=self.send.at[self.first + slot],
            recv_sem=self.recv.at[self.first + slot],
            device_id=partner,
            device_id_type=MESH,
        )

    def spot(self, kind):
        return (1 - self.y if kind in (0, 2) else self.y), (1 - self.x if kind in (0, 1) else self.x)

    def core(self, kind):
        y, x = self.spot(kind)
        return self.copy(
            kind,
            self.mine.at[:, y, 1 - self.c, x],
            self.core_in.at[:, y, x],
            device(self.z, self.y, 1 - self.c, self.x),
        )

    def corner(self, d, half):
        z = (self.z + d) % 4
        y, x = self.spot(0)
        low, size = ((0, self.cut), (self.cut, self.total.shape[-1] - self.cut))[half]
        source = self.total.at[z, y, x, :, pl.ds(low, size)]
        if half == 0:
            return self.copy(4 + d, source, self.corner_y.at[z], device(self.z, 1 - self.y, self.c, self.x))
        return self.copy(8 + d, source, self.corner_x.at[z], device(self.z, self.y, self.c, 1 - self.x))

    def to_x(self, d):
        z = (self.z + d) % 4
        return self.copy(12 + d, self.total.at[z, self.y, 1 - self.x], self.from_x.at[z], device(self.z, self.y, self.c, 1 - self.x))

    def to_y(self, d):
        z = (self.z + d) % 4
        return self.copy(16 + d, self.total.at[z, 1 - self.y, self.x], self.from_y.at[z], device(self.z, 1 - self.y, self.c, self.x))

    def along_z(self, d):
        z = (self.z + d) % 4
        return self.copy(19 + d, self.total.at[z, self.y, self.x], self.from_z.at[d - 1], device(z, self.y, self.c, self.x))

    def start(self):
        self.own.start()
        for kind in range(4):
            self.core(kind).start()

    def merge(self, kind):
        if kind == 0:
            self.own.wait()
        self.core(kind).wait_recv()
        y, x = self.spot(kind)

        def add(z, carry):
            self.total[z, y, x] = self.total[z, y, x] + self.core_in[z, y, x]
            return carry

        lax.fori_loop(0, 4, add, 0)
        if kind == 0:
            for d in (1, 2, 3, 0):
                self.corner(d, 0).start()
                self.corner(d, 1).start()

    def bend(self, d):
        z = (self.z + d) % 4
        self.corner(d, 0).wait_recv()
        self.total[z, self.y, 1 - self.x, :, : self.cut] = self.total[z, self.y, 1 - self.x, :, : self.cut] + self.corner_y[z]
        self.to_x(d).start()
        self.corner(d, 1).wait_recv()
        self.total[z, 1 - self.y, self.x, :, self.cut :] = self.total[z, 1 - self.y, self.x, :, self.cut :] + self.corner_x[z]
        self.to_y(d).start()

    def close(self, d):
        z = (self.z + d) % 4
        self.to_x(d).wait_recv()
        self.to_y(d).wait_recv()
        here = self.total[z, self.y, self.x].astype(jnp.float32) + self.from_x[z].astype(jnp.float32)
        self.total[z, self.y, self.x] = (here + self.from_y[z].astype(jnp.float32)).astype(jnp.bfloat16)
        if d:
            self.along_z(d).start()

    def result(self, store):
        total = self.total[self.z, self.y, self.x].astype(jnp.float32)
        for d in (1, 2, 3):
            self.along_z(d).wait_recv()
            total = total + self.from_z[d - 1].astype(jnp.float32)
        store[...] = total

    def drain(self):
        for kind in range(4):
            self.core(kind).wait_send()
        for d in range(4):
            self.corner(d, 0).wait_send()
            self.corner(d, 1).wait_send()
            self.to_x(d).wait_send()
            self.to_y(d).wait_send()
            if d:
                self.along_z(d).wait_send()


SUMS = 23
BACK = ((96, 768), (48, 1536), (48, 512), (48, 384), (48, 384), (48, 512))
BACK_CUT = (384, 768, 256, 128, 128, 256)


def work_shapes(rows, lanes, cut):
    held = lambda *dims: pltpu.VMEM((*dims, rows, lanes), jnp.bfloat16)
    part = lambda size: pltpu.VMEM((4, rows, size), jnp.bfloat16)
    return [held(4, 2, 2), held(4, 2, 2), part(cut), part(lanes - cut), held(4), held(4), held(3)]


def attend_back(proj, grads_in, probs, grads, vectors, row, length, group):
    rows = pl.ds(row, length)
    lane = lax.broadcasted_iota(jnp.int32, (length, 128), 1)
    score_scale = 1.0 / math.sqrt(HD)
    width = padded(length)

    def pair(p):
        at = lambda base: pl.ds(base + p * 128, 128)
        query, key, value = (proj[:length, at(base)] for base in (0, 256, 512))
        context_grad = grads_in[:length, at(0)]
        low = probs[p, :length, : 2 * width]
        weight = low.astype(jnp.float32)
        weight_grad = dot(context_grad, two_heads(value, width), NT)
        parts = []
        for h in (0, 1):
            lanes = slice(width * h, width * h + width)
            inner = jnp.sum(weight_grad[:, lanes] * weight[:, lanes], axis=1, keepdims=True)
            parts.append((weight[:, lanes] * (weight_grad[:, lanes] - inner)).astype(jnp.bfloat16))
        score_grad = jnp.concatenate(parts, axis=1)
        query_grad = dot(score_grad, two_heads(key, width), NN)
        key_grads = dot(score_grad, query, TN)
        value_grads = dot(low, context_grad, TN)
        both = lambda grad: jnp.where(lane < 64, grad[:length], grad[width : width + length])
        query_low = (query_grad * score_scale).astype(jnp.bfloat16)
        key_low = (both(key_grads) * score_scale).astype(jnp.bfloat16)
        value_low = both(value_grads).astype(jnp.bfloat16)
        grads[rows, at(768 * group)] = query_low
        grads[rows, at(768 * group + 256)] = key_low
        grads[rows, at(768 * group + 512)] = value_low
        vectors[0:1, at(256 * group)] += jnp.sum(query_low.astype(jnp.float32), axis=0, keepdims=True)
        vectors[1:2, at(256 * group)] += jnp.sum(value_low.astype(jnp.float32), axis=0, keepdims=True)

    for p in range(2):
        pair(p)


def vectors_on_wire(vectors, out, low):
    lane = lax.broadcasted_iota(jnp.int32, (512, 768), 1)
    start = (lax.broadcasted_iota(jnp.int32, (512, 768), 0) >> 4) * 24
    wide = jnp.broadcast_to(vectors[:, :768][None], (32, 16, 768)).reshape(512, 768)
    wide = jnp.where((lane >= start) & (lane < start + 24), wide, 0.0).astype(jnp.bfloat16)
    rows = dot(wide, spread_table(24, 768), NT).reshape(32, 16, 128)
    lane = lax.broadcasted_iota(jnp.int32, (32, 3072), 1)
    start = lax.broadcasted_iota(jnp.int32, (32, 3072), 0) * 96
    wide = jnp.where((lane >= start) & (lane < start + 96), vectors[9:10, :], 0.0).astype(jnp.bfloat16)
    up_rows = dot(wide, spread_table(96, 3072), NT)
    number = lax.broadcasted_iota(jnp.int32, (32, 16, 128), 1)
    rows = jnp.where(number == 5, up_rows[:, None, :], rows).astype(jnp.bfloat16)
    for i in range(32):
        out[i // 8, (i // 4) % 2, (i // 2) % 2, i % 2, :16, low : low + 128] = rows[i]
        out[i // 8, (i // 4) % 2, (i // 2) % 2, i % 2, 16:, low : low + 128] = jnp.zeros((32, 128), jnp.bfloat16)


def wire_blocks(total, out, left=0, right=384, lanes=384, low=0):
    for i in range(32):
        rows = slice(24 * i, 24 * i + 24)
        both = jnp.concatenate([total[rows, left : left + lanes], total[rows, right : right + lanes]], axis=0)
        out[i // 8, (i // 4) % 2, (i // 2) % 2, i % 2, :, low : low + lanes] = both.astype(jnp.bfloat16)


def last_kernel(*refs):
    act, pre, hidden, ffn, attn, final, embed_grad, context, proj, context_grad, ps, pls, w_qkv_in = refs[:13]
    sums, x_in = refs[13:15]
    part_out, d_out, u_out, o_out, g0_out, g1_out, g2_out, p_down, p_up = refs[15:24]
    stage, p_out, p_first, p_second, p_third, slot_proj, slot_grad, slot_pl, grads, w_qkv, total, vectors, token_part, eg_held, x_ref = refs[24:39]
    work, (send, recv, local, load, fetch, away) = refs[39 : 39 + 7 * len(BACK)], refs[39 + 7 * len(BACK) :]
    groups = (p_first, p_second, p_third)
    mine = (p_down, p_up, p_out, *groups)
    down, up, out, *heads = pieces = [
        Scatter(one, BACK_CUT[i], work[7 * i : 7 * i + 7], send, recv, local, i) for i, one in enumerate(mine)
    ]
    merges, bends, closes = ([[functools.partial(getattr(one, name), d) for d in range(4)] for one in pieces] for name in ("merge", "bend", "close"))
    bends, closes = ([[rows[d] for d in (1, 2, 3, 0)] for rows in kind] for kind in (bends, closes))
    stores = (d_out, u_out, o_out, g0_out, g1_out, g2_out)
    ends = [functools.partial(one.result, store) for one, store in zip(pieces, stores)]

    s0, s1, s2, s3 = [grads.at[:, pl.ds(768 * i, 768)] for i in range(3)] + [token_part]
    halves = lambda j, slot: [
        (pre.at[:, pl.ds(384 * j, 384)], slot.at[:, pl.ds(0, 384)]),
        (pre.at[:, pl.ds(1536 + 384 * j, 384)], slot.at[:, pl.ds(384, 384)]),
    ]
    acts = lambda j, slot: [(act.at[:, pl.ds(768 * j, 768)], slot)]
    started, carried = [], []

    def bring(pairs):
        copies = []
        for source, target in pairs:
            copies.append(pltpu.make_async_copy(source, target, fetch.at[len(started)]))
            copies[-1].start()
            started.append(copies[-1])
        return copies

    def have(copies):
        for copy in copies:
            copy.wait()

    def carry(source, target):
        copy = pltpu.make_async_copy(source, target, away.at[len(carried)])
        copy.start()
        carried.append(copy)
        return copy

    ffn_here, here = bring([(ffn, s0)]), {}
    for j, slot in enumerate((s1, s2, s3)):
        here["act", j] = bring(acts(j, slot))
    eg_here = bring([(embed_grad, eg_held)])
    lanes = [(w_qkv_in.at[:, pl.ds(768 * p + 256 * g, 256)], w_qkv.at[:, pl.ds(768 * g + 256 * p, 256)]) for g in range(3) for p in range(3)]
    vectors[...] = sums[...]
    greet(*place())
    have(ffn_here)
    sent = {}
    for j, slot in enumerate((s1, s2, s3, s1)):
        have(here["act", j])
        low = dot(slot[...], s0[...], TN).astype(jnp.bfloat16)
        if j >= 2:
            sent[j - 2].wait()
        stage[j % 2] = low.reshape(2, 2, 2, 96, 768)
        sent[j] = carry(stage.at[j % 2], p_down.at[j])
        if j == 0:
            here["act", 3] = bring(acts(3, s1))
        elif j == 1:
            hidden_here = bring([(hidden, s2)])
        elif j == 2:
            here["pre", 0] = bring(halves(0, s3))
    here["pre", 1] = bring(halves(1, s0))
    here["pre", 2] = bring(halves(2, s1))
    have(hidden_here)
    hooks = iter([[], merges[0][:1], merges[0][1:], bends[0][:1]])
    for j, slot in enumerate((s3, s0, s1, s3)):
        have(here["pre", j])
        total[...] = dot(s2[...], slot[...], TN)
        if j == 0:
            sent[2].wait()
            sent[3].wait()
            down.start()
        held = groups[j % 2]
        if j >= 2:
            sent[j + 2].wait()
        wire_blocks(total, held)
        sent[4 + j] = carry(held.at[:, :, :, :, :, pl.ds(0, 384)], p_up.at[:, :, :, :, :, pl.ds(384 * j, 384)])
        if j == 0:
            here["pre", 3] = bring(halves(3, s3))
        elif j == 1:
            context_here = bring([(context, s0)])
        elif j == 2:
            attn_here = bring([(attn, s1)])
        for step in next(hooks):
            step()
    final_here = bring([(final, s2)])
    x_here = bring([(x_in, x_ref)])
    weights_here = bring(lanes)
    order = [(SHORT + 320 * s, 320, s) for s in range(4)] + [(128 * s, 128, s) for s in range(4)]
    order = [(g, *one) for g in range(3) for one in order]

    def loads(n):
        group, row, length, s = order[n]
        slot = n % 2
        rows = pl.ds(row, length)
        copies = [
            (proj.at[rows, pl.ds(768 * p + 256 * group, 256)], slot_proj.at[slot, pl.ds(0, length), pl.ds(256 * p, 256)]) for p in range(3)
        ]
        copies.append((context_grad.at[rows, pl.ds(256 * group, 256)], slot_grad.at[slot, pl.ds(0, length)]))
        source = pls if length == 320 else ps
        copies.append((source.at[s, pl.ds(2 * group, 2)], slot_pl.at[slot, :, pl.ds(0, length), pl.ds(0, 2 * padded(length))]))
        return [pltpu.make_async_copy(source, target, load.at[slot, i]) for i, (source, target) in enumerate(copies)]

    for copy in loads(0):
        copy.start()
    have(context_here)
    have(attn_here)
    total[...] = dot(s0[...], s1[...], TN)
    sent[6].wait()
    sent[7].wait()
    up.start()
    wire_blocks(total, p_out)
    for step in bends[0][1:3]:
        step()
    have(final_here)
    have(eg_here)
    total[:, :128] = dot(s2[...], eg_held[...], TN)
    wire_blocks(total, p_out, 0, 0, 128, 384)
    out.start()
    hooks = iter([
        [*bends[0][3:], merges[1][0]], merges[1][1:], [merges[2][0]], merges[2][1:], [], [], closes[0][:2], closes[0][2:], [],
        bends[1][:1], [merges[3][0], *bends[1][1:2]], [*merges[3][1:], *bends[1][2:3]], bends[1][3:], bends[2][:2], bends[2][2:], [], bends[3][:2], bends[3][2:],
        closes[1][:1], [merges[4][0], *closes[1][1:2]], [*merges[4][1:], *closes[1][2:3]], closes[1][3:], closes[2][:2], closes[2][2:], bends[4][:2], bends[4][2:], [ends[0]],
        [*closes[3][:2], merges[5][0]], [*merges[5][1:], *closes[3][2:]], closes[4][:2], [*closes[4][2:], *bends[5][:2]], bends[5][2:],
    ])

    def hook():
        for step in next(hooks):
            step()

    for n, (group, row, length, s) in enumerate(order):
        if n + 1 < len(order):
            for copy in loads(n + 1):
                copy.start()
        for copy in loads(n):
            copy.wait()
        slot = n % 2
        attend_back(slot_proj.at[slot], slot_grad.at[slot], slot_pl.at[slot], grads, vectors, row, length, group)
        hook()
        if n % 8 == 7:
            if group == 0:
                have(x_here)
            total[...] = dot(x_ref[...], grads[:, 768 * group : 768 * group + 768], TN)
            if group == 2:
                vectors_on_wire(vectors, p_third, 384)
            wire_blocks(total, groups[group])
            heads[group].start()
            hook()
    have(weights_here)
    for row, length in [(0, SHORT)] + [(SHORT + 320 * s, 320) for s in range(4)]:
        rows = pl.ds(row, length)
        token_part[rows] = dot(grads[rows], w_qkv[...], NT).astype(jnp.bfloat16)
        carry(token_part.at[rows], part_out.at[rows])
        hook()
    for step in [ends[1], *closes[5], ends[2], ends[3], ends[4], ends[5]]:
        step()
    for copy in carried[8:]:
        copy.wait()
    for piece in pieces:
        piece.drain()


def last(operands, sums, x):
    vmem, anywhere = (pl.BlockSpec(memory_space=m) for m in (pltpu.VMEM, pl.ANY))
    full = lambda *dims: jax.ShapeDtypeStruct(dims, jnp.float32)
    low = lambda *dims: jax.ShapeDtypeStruct(dims, jnp.bfloat16)
    held = lambda *dims: pltpu.VMEM(dims, jnp.bfloat16)
    semaphores = lambda *dims: pltpu.SemaphoreType.DMA(dims)
    scratch = []
    for dims, cut in zip(BACK, BACK_CUT):
        scratch += work_shapes(*dims, cut)
    return pl.pallas_call(
        last_kernel,
        out_shape=(low(ROWS, 768), *[full(*dims) for dims in BACK], *[low(4, 2, 2, 2, *dims) for dims in BACK[:2]]),
        in_specs=[anywhere] * 13 + [vmem, anywhere],
        out_specs=(anywhere,) + (vmem,) * 6 + (anywhere,) * 2,
        scratch_shapes=[held(2, 2, 2, 2, 96, 768)]
        + [held(4, 2, 2, 2, *dims) for dims in BACK[2:]]
        + [held(2, 320, 768), held(2, 320, 256), held(2, 2, 320, 768), held(ROWS, 2304), held(768, 2304)]
        + [pltpu.VMEM((768, 768), jnp.float32), pltpu.VMEM((16, 3072), jnp.float32), held(ROWS, 768), held(ROWS, P_SIZE), held(ROWS, 768)]
        + scratch
        + [semaphores(SUMS * len(BACK)), semaphores(SUMS * len(BACK)), semaphores(len(BACK)), semaphores(2, 5), semaphores(32), semaphores(16)],
        compiler_params=pltpu.CompilerParams(collective_id=1, has_side_effects=True, vmem_limit_bytes=63 * 2**20),
    )(*operands, sums, x)[:7]


def finish_kernel(resid, part, d, u, o, g0, g1, g2, gs, gl, q_out, k_out, v_out, o_out, u_out, d_out, e_out, *vectors):
    tile = pl.program_id(0)
    value = resid[...] + part[...].astype(jnp.float32)

    @pl.when(tile < 2)
    def _():
        gs[...] = value

    @pl.when(tile >= 2)
    def _():
        gl[...] = value

    @pl.when(tile == 0)
    def _():
        d_out[...] = d[...]
        for wire, target, half in ((u, u_out, 1536), (o, o_out, 384)):
            target[:, :half] = wire[:24, :half]
            target[:, half:] = wire[24:, :half]
        e_out[...] = o[:24, 384:]
        for g, wire in enumerate((g0, g1, g2)):
            low = 256 * g
            q_out[:, low : low + 256] = wire[:24, :256]
            k_out[:, low : low + 128] = wire[:24, 256:384]
            k_out[:, low + 128 : low + 256] = wire[24:, :128]
            v_out[:, low : low + 256] = wire[24:, 128:384]
        for i, target in enumerate(vectors):
            width = target.shape[0]
            target[...] = g2[i : i + 1, 384 : 384 + width].reshape(width)


def finish(resid, part, wires, shards):
    tile = 256
    full = lambda *dims: jax.ShapeDtypeStruct(dims, jnp.float32)
    every = pl.BlockSpec((tile, 768), lambda i: (i, 0))
    whole = lambda one: pl.BlockSpec(one.shape, lambda i: (0,) * one.ndim)
    cut = SHORT // tile
    query, key, value, out, up, down, embed, *vectors = shards
    return pl.pallas_call(
        finish_kernel,
        grid=(ROWS // tile,),
        out_shape=(full(SHORT, 768), full(ROWS - SHORT, 768), *[full(*one.shape) for one in shards]),
        in_specs=[every, every] + [whole(one) for one in wires],
        out_specs=(
            pl.BlockSpec((tile, 768), lambda i: (jnp.minimum(i, cut - 1), 0)),
            pl.BlockSpec((tile, 768), lambda i: (jnp.maximum(i - cut, 0), 0)),
            *[whole(one) for one in shards],
        ),
        compiler_params=pltpu.CompilerParams(vmem_limit_bytes=62 * 2**20),
    )(resid, part, *wires)


def fast_body(xs, len_short, xl, len_long, shards, cs, cl):
    flat = lambda one: one.reshape(-1, one.shape[-1])
    w_qkv, w_out, w_up, w_embed, w_down, vec, proj, context, ps, pls, x, cot = first(
        len_short, len_long, flat(xs), flat(xl), flat(cs), flat(cl), shards
    )
    es, el, act, pre, hidden, ffn, attn, final, embed_grad, resid, context_grad, sums = token_chain(
        len_short, len_long, x, cot, context, w_out, w_up, w_down.reshape(3072, 768), w_embed, vec
    )
    part, *wires = last((act, pre, hidden, ffn, attn, final, embed_grad, context, proj, context_grad, ps, pls, w_qkv), sums, x)
    gs, gl, *owned = finish(resid, part, wires, shards)
    shaped = lambda value, like: value.reshape(*like.shape[:2], -1)
    return (shaped(es, xs), shaped(el, xl), shaped(gs, xs), shaped(gl, xl), *owned)


def body(tokens_short, lengths_short, tokens_long, lengths_long, *rest):
    shards, (cotangent_short, cotangent_long) = rest[:16], rest[16:]
    weights = tuple(lax.all_gather(one, BOTH, axis=0, tiled=True) for one in shards)
    embed_short, saved_short = forward(tokens_short, lengths_short, weights)
    embed_long, saved_long = forward(tokens_long, lengths_long, weights)
    input_short, grads_short = backward(saved_short, weights, cotangent_short)
    input_long, grads_long = backward(saved_long, weights, cotangent_long)
    totals = jax.tree.map(jnp.add, grads_short, grads_long)
    owned = tuple(lax.psum_scatter(one, BOTH, scatter_dimension=0, tiled=True) for one in totals)
    return (embed_short, embed_long, input_short, input_long, *owned)


def solution(mesh):
    split = lambda rank: P(BOTH, *([None] * (rank - 1)))
    weights = [split(2)] * 7 + [split(1)] * 9
    in_specs = (split(3), split(1), split(3), split(1), *weights, split(3), split(3))
    out_specs = (split(3),) * 4 + tuple(weights)
    fast = mesh.shape["wide"] == 16 and mesh.shape["narrow"] == 2

    def step(xs, len_short, xl, len_long, *rest):
        if fast:
            return fast_body(xs, len_short, xl, len_long, rest[:16], *rest[16:])
        return body(xs, len_short, xl, len_long, *rest)

    return jax.shard_map(step, mesh=mesh, in_specs=in_specs, out_specs=out_specs, check_vma=False)
```
